32 devices in a mesh: dp: 8 (over y, x, core), seq: 4 (over z).
Axes of the slice: x: 2, y: 2, z: 4, core: 2. Of those that a mesh axis runs over, the one named last changes fastest.
Arguments:
- tokens: bfloat16 [24576, 768], P(('dp', 'seq')), may hold values from -6 to 6
- first_values: bfloat16 [24576, 384], P(('dp', 'seq')), may hold values from -6 to 6
- cotangent: bfloat16 [24576, 768], P(('dp', 'seq')), may hold values from -6 to 6
- ln1_gain: bfloat16 [768], P('dp'), may hold values from 0.5 to 1.5
- ln1_bias: bfloat16 [768], P('dp'), may hold values from -3 to 3
- w_query: bfloat16 [768, 768], P(None, 'dp'), may hold values from -0.21875 to 0.21875
- w_key: bfloat16 [768, 768], P(None, 'dp'), may hold values from -0.21875 to 0.21875
- w_value: bfloat16 [768, 384], P(None, 'dp'), may hold values from -0.21875 to 0.21875
- w_out: bfloat16 [768, 768], P(None, 'dp'), may hold values from -1.75 to 1.75
- ln2_gain: bfloat16 [768], P('dp'), may hold values from 0.5 to 1.5
- ln2_bias: bfloat16 [768], P('dp'), may hold values from -3 to 3
- w_fc: bfloat16 [768, 3072], P(None, 'dp'), may hold values from -0.21875 to 0.21875
- w_proj: bfloat16 [3072, 768], P(None, 'dp'), may hold values from -0.109375 to 0.109375
Outputs:
- output: bfloat16 [24576, 768], P(('dp', 'seq'))
- grad_tokens: bfloat16 [24576, 768], P(('dp', 'seq'))
- grad_first_values: bfloat16 [24576, 384], P(('dp', 'seq'))
- grad_ln1_gain: float32 [768], P('dp')
- grad_ln1_bias: float32 [768], P('dp')
- grad_w_query: float32 [768, 768], P(None, 'dp')
- grad_w_key: float32 [768, 768], P(None, 'dp')
- grad_w_value: float32 [768, 384], P(None, 'dp')
- grad_w_out: float32 [768, 768], P(None, 'dp')
- grad_ln2_gain: float32 [768], P('dp')
- grad_ln2_bias: float32 [768], P('dp')
- grad_w_fc: float32 [768, 3072], P(None, 'dp')
- grad_w_proj: float32 [3072, 768], P(None, 'dp')
The draws below stay inside these ranges and needn't reach their ends.
All inputs are finite; a program needn't handle non-finite values.
Results may differ from the reference program's by a relative error of at most 0.015.
Values may be sent and summed in bfloat16 or wider, within the bound.
No kernel may reach another device: no remote copies, remote signals or barrier semaphores. Data moves between devices by JAX's collectives and lax.ppermute only.
A program may use at most 192 MiB of HBM per device.

```python
import jax
import jax.numpy as jnp
from jax import lax

D = 768
HEADS = 12
HEAD = 64
FF = 3072
SEQ_LEN = 3072
TOKENS = 24576
QBLOCK = 512
FRESH_WIDTH = 384
REUSED_WIDTH = 384
N_DP = 8


def spiked(values, own_key, source, target, blocks, factor):
    owner, partner = [(jnp.arange(values.shape[dim]) // (values.shape[dim] // blocks)).reshape([-1 if axis == dim else 1 for axis in range(values.ndim)]) for dim in (source, target)]
    chosen = jax.random.permutation(own_key, blocks)[partner]
    strong = (owner == chosen) | (owner == (partner + blocks // 2) % blocks)
    return jnp.where(strong, factor * values, values)


def levels(key, extent, shards, low, top_value):
    level, own = 1.0, jax.random.fold_in(key, 6)
    for axis_at, parts in shards:
        steps = jnp.exp(jax.random.uniform(jax.random.fold_in(own, axis_at), (parts,), jnp.float32, low / len(shards), top_value / len(shards)))
        level = level * jnp.repeat(steps, extent[axis_at] // parts).reshape([-1 if axis == axis_at else 1 for axis in range(len(extent))])
    return level


def noise(own_key, dims, width, bound, cuts=(), kind=jnp.bfloat16):
    level = levels(own_key, dims, cuts, -0.22, 0.18) if cuts else 1.0
    array = jax.random.normal(own_key, dims, jnp.float32) * width * level
    return jnp.minimum(jnp.maximum(array, -bound), bound).astype(kind)


def gaussian_with(own_key, shape, scale, bound, shards, heavy, held_as=jnp.bfloat16):
    drawn = scale * jax.random.normal(own_key, shape, jnp.float32)
    if shards:
        drawn = drawn * levels(own_key, shape, shards, -0.22, 0.18)
    return jnp.clip(spiked(drawn, jax.random.fold_in(own_key, 3), *heavy), -bound, bound).astype(held_as)


def setup_inputs(seed: int = 0) -> dict:
    key_list = jax.random.split(jax.random.key(seed), 14)
    tokens = noise(key_list[0], (TOKENS, D), 1.0, 6.0, ((0, 32),))
    first_values = noise(key_list[1], (TOKENS, REUSED_WIDTH), 1.0, 6.0, ((0, 32),))
    cotangent = gaussian_with(key_list[2], (TOKENS, D), 1.0, 6.0, ((0, 32),), (0, 1, 32, 2.75))
    ln1_gain = jnp.clip(1.0 + 0.1 * jax.random.normal(key_list[3], (D,), jnp.float32), 0.5, 1.5).astype(jnp.bfloat16)
    ln1_bias = noise(key_list[4], (D,), 0.5, 3.0, ((0, 8),))
    w_query = noise(key_list[5], (D, D), D ** -0.5, 0.21875, ((1, 8),))
    w_key = noise(key_list[6], (D, D), D ** -0.5, 0.21875, ((1, 8),))
    w_value = noise(key_list[7], (D, FRESH_WIDTH), D ** -0.5, 0.21875, ((1, 8),))
    w_out = noise(key_list[8], (D, D), (D // 64) ** -0.5, 1.75, ((1, 8),))
    ln2_gain = jnp.clip(1.0 + 0.1 * jax.random.normal(key_list[9], (D,), jnp.float32), 0.5, 1.5).astype(jnp.bfloat16)
    ln2_bias = noise(key_list[10], (D,), 0.5, 3.0, ((0, 8),))
    w_fc = noise(key_list[11], (D, FF), D ** -0.5, 0.21875, ((1, 8),))
    w_proj = noise(key_list[12], (FF, D), FF ** -0.5, 0.109375, ((1, 8),))
    return {"tokens": tokens, "first_values": first_values, "cotangent": cotangent, "ln1_gain": ln1_gain, "ln1_bias": ln1_bias, "w_query": w_query, "w_key": w_key, "w_value": w_value, "w_out": w_out, "ln2_gain": ln2_gain, "ln2_bias": ln2_bias, "w_fc": w_fc, "w_proj": w_proj}


@jax.custom_vjp
def low(v):
    return lax.optimization_barrier(v.astype(jnp.bfloat16)).astype(jnp.float32)

@jax.custom_vjp
def low_back(v):
    return v

def low_keep(v):
    return (low(v), None)

def low_pass(kept, grad):
    return (grad,)

def back_keep(v):
    return (v, None)

def back_low(kept, grad):
    return (low(grad),)
low.defvjp(low_keep, low_pass)
low_back.defvjp(back_keep, back_low)
EPSILON = 1e-05
PRECISE = lax.Precision.HIGHEST

def layer_norm(features_in, gain_vec, shift_vec):
    row_mean = lax.optimization_barrier(jnp.mean(features_in, axis=-1, keepdims=True))
    centred = features_in - row_mean
    variance = lax.optimization_barrier(jnp.mean(centred * centred, axis=-1, keepdims=True))
    return centred * lax.rsqrt(variance + EPSILON) * gain_vec + shift_vec

def matmul(left_side, right_side):
    return jnp.dot(left_side, right_side, precision=PRECISE, preferred_element_type=jnp.float32)

def attend_block(query_block, first_row, keys_all, values_all):
    scores = jnp.einsum('qhd,khd->hqk', query_block, keys_all, precision=PRECISE) * HEAD ** (-0.5)
    scores = low_back(scores)
    query_pos = first_row + jnp.arange(query_block.shape[0], dtype=jnp.int32)
    key_pos = jnp.arange(keys_all.shape[0], dtype=jnp.int32)
    scores = jnp.where(key_pos[None, None, :] <= query_pos[None, :, None], scores, -1e+30)
    row_max = lax.optimization_barrier(jnp.max(scores, axis=-1, keepdims=True))
    raised = jnp.exp(scores - row_max)
    weights = raised / lax.optimization_barrier(jnp.sum(raised, axis=-1, keepdims=True))
    weights = low(weights)
    return jnp.einsum('hqk,khd->qhd', weights, values_all, precision=PRECISE)

def forward(tokens_seq, reused_seq, ln1_gain, ln1_bias, w_query, w_key, w_value, w_out, ln2_gain, ln2_bias, w_fc, w_proj):
    normed_one = low(layer_norm(tokens_seq, ln1_gain, ln1_bias))
    queries = low(low_back(matmul(normed_one, w_query))).reshape(SEQ_LEN, HEADS, HEAD)
    keys_all = low(low_back(matmul(normed_one, w_key))).reshape(SEQ_LEN, HEADS, HEAD)
    joined = jnp.concatenate([matmul(normed_one, w_value), reused_seq], axis=1)
    values_all = low(low_back(joined)).reshape(SEQ_LEN, HEADS, HEAD)
    blocks = queries.reshape(SEQ_LEN // QBLOCK, QBLOCK, HEADS, HEAD)
    starts = jnp.arange(SEQ_LEN // QBLOCK, dtype=jnp.int32) * QBLOCK

    def attend_item(block_item):
        return attend_block(block_item[0], block_item[1], keys_all, values_all)
    attended = lax.map(jax.checkpoint(attend_item), (blocks, starts))
    attended = low(low_back(attended.reshape(SEQ_LEN, D)))
    residual_one = tokens_seq + low_back(matmul(attended, w_out))
    normed_two = low(layer_norm(residual_one, ln2_gain, ln2_bias))
    hidden = low_back(matmul(normed_two, w_fc))
    active = low(jax.nn.gelu(hidden, approximate=True))
    return residual_one + matmul(active, w_proj)

def reference(tokens, first_values, cotangent, ln1_gain, ln1_bias, w_query, w_key, w_value, w_out, ln2_gain, ln2_bias, w_fc, w_proj):
    params = tuple((weight.astype(jnp.float32) for weight in (ln1_gain, ln1_bias, w_query, w_key, w_value, w_out, ln2_gain, ln2_bias, w_fc, w_proj)))

    def per_sequence(carried, sequence_item):
        tokens_seq, reused_seq, grad_seq = sequence_item
        result, pullback = jax.vjp(forward, tokens_seq, reused_seq, *params)
        gradients = pullback(grad_seq)
        carried = tuple((running + fresh_grad for running, fresh_grad in zip(carried, gradients[2:])))
        return (carried, (result.astype(jnp.bfloat16), gradients[0].astype(jnp.bfloat16), gradients[1].astype(jnp.bfloat16)))
    sequences = (tokens.astype(jnp.float32).reshape(N_DP, SEQ_LEN, D), first_values.astype(jnp.float32).reshape(N_DP, SEQ_LEN, REUSED_WIDTH), cotangent.astype(jnp.float32).reshape(N_DP, SEQ_LEN, D))
    zero_grads = tuple((jnp.zeros(weight.shape, jnp.float32) for weight in params))
    totals, (outputs, grad_rows, grad_reused) = lax.scan(per_sequence, zero_grads, sequences)
    return (outputs.reshape(TOKENS, D), grad_rows.reshape(TOKENS, D), grad_reused.reshape(TOKENS, REUSED_WIDTH), totals[0], totals[1], totals[2], totals[3], totals[4], totals[5], totals[6], totals[7], totals[8], totals[9])
```

```python
import functools

import jax
import jax.numpy as jnp
from jax import lax
from jax.experimental import pallas as pl
from jax.experimental.pallas import tpu as pltpu
from jax.sharding import PartitionSpec as P

HEADS = 12
HEAD = 64
EPSILON = 1e-05
LOW = jnp.bfloat16
WIDE = jnp.float32


def dot(left, right, left_dim, right_dim):
    return lax.dot_general(
        left, right, (((left_dim,), (right_dim,)), ((), ())), preferred_element_type=WIDE
    )


def causal(scores):
    key_pos = lax.broadcasted_iota(jnp.int32, scores.shape, 0)
    query_pos = lax.broadcasted_iota(jnp.int32, scores.shape, 1)
    return jnp.where(key_pos <= query_pos, scores, -1e30)


def turned(block):
    return jnp.transpose(block.astype(WIDE)).astype(LOW)


def sub_width(rows):
    for parts in (2, 3, 4, 6):
        if rows % (parts * 128) == 0:
            return rows // parts
    return rows


def forward_kernel(q_ref, k_ref, v_ref, o_ref, log_ref, key_rows):
    step = pl.program_id(0)
    parts, rows = k_ref.shape[0], k_ref.shape[3]
    sub = sub_width(rows)

    @pl.when(step == 0)
    def _():
        for part in range(parts):
            key_rows[part] = turned(k_ref[part, 0])

    for first in range(0, rows, sub):
        cols = pl.ds(first, sub)
        q = q_ref[0, 0, :, cols]
        blocks = []
        if first:
            blocks.append((0, dot(key_rows[step, pl.ds(0, first)], q, 1, 0)))
        blocks.append((first, causal(dot(key_rows[step, cols], q, 1, 0))))
        top = functools.reduce(
            jnp.maximum, [jnp.max(scores, axis=0, keepdims=True) for _, scores in blocks]
        )
        total = jnp.zeros((1, sub), WIDE)
        mixed = jnp.zeros((HEAD, sub), WIDE)
        for offset, scores in blocks:
            raised = jnp.exp(scores - top)
            total = total + jnp.sum(raised, axis=0, keepdims=True)
            mixed = mixed + dot(
                v_ref[step, 0, :, pl.ds(offset, scores.shape[0])], raised.astype(LOW), 1, 0
            )

        def earlier(part, carried):
            top, total, mixed = carried
            scores = dot(key_rows[part], q, 1, 0)
            new_top = jnp.maximum(top, jnp.max(scores, axis=0, keepdims=True))
            shrink = jnp.exp(top - new_top)
            raised = jnp.exp(scores - new_top)
            return (
                new_top,
                shrink * total + jnp.sum(raised, axis=0, keepdims=True),
                shrink * mixed + dot(v_ref[part, 0], raised.astype(LOW), 1, 0),
            )

        top, total, mixed = lax.fori_loop(0, step, earlier, (top, total, mixed))
        o_ref[0, :, cols] = (mixed / total).astype(LOW)
        log_ref[0, :, cols] = top + jnp.log(total)


def pair_cost(parts, rows, matmuls):
    pairs = parts * parts * rows * rows // 2
    return pl.CostEstimate(
        flops=2 * matmuls * pairs * HEAD * 4,
        bytes_accessed=parts * rows * HEAD * 16,
        transcendentals=pairs,
    )


def attend(packed):
    parts, _, _, rows = packed.shape
    return pl.pallas_call(
        forward_kernel,
        grid=(parts,),
        in_specs=[
            pl.BlockSpec((1, 1, HEAD, rows), lambda i: (i, 0, 0, 0)),
            pl.BlockSpec((parts, 1, HEAD, rows), lambda i: (0, 1, 0, 0)),
            pl.BlockSpec((parts, 1, HEAD, rows), lambda i: (0, 2, 0, 0)),
        ],
        out_specs=[
            pl.BlockSpec((1, HEAD, rows), lambda i: (i, 0, 0)),
            pl.BlockSpec((1, 1, rows), lambda i: (i, 0, 0)),
        ],
        out_shape=[
            jax.ShapeDtypeStruct((parts, HEAD, rows), LOW),
            jax.ShapeDtypeStruct((parts, 1, rows), WIDE),
        ],
        scratch_shapes=[pltpu.VMEM((parts, rows, HEAD), LOW)],
        compiler_params=pltpu.CompilerParams(vmem_limit_bytes=40 << 20),
        cost_estimate=pair_cost(parts, rows, 2),
        name="attend",
    )(packed, packed, packed)


def backward_kernel(
    q_ref, k_ref, v_ref, do_ref, o_ref, log_ref, out_ref,
    key_rows, value_rows, query_rows, grad_rows, inner_ref, key_sum, value_sum,
):
    step = pl.program_id(0)
    parts, rows = k_ref.shape[0], k_ref.shape[3]
    sub = sub_width(rows)

    @pl.when(step == 0)
    def _():
        for part in range(parts):
            key_rows[part] = turned(k_ref[part, 0])
            value_rows[part] = turned(v_ref[part, 0])
        key_sum[...] = jnp.zeros_like(key_sum)
        value_sum[...] = jnp.zeros_like(value_sum)

    query_rows[...] = turned(q_ref[0, 0])
    grads = do_ref[0].astype(WIDE)
    grad_rows[...] = jnp.transpose(grads).astype(LOW)
    inner_ref[...] = jnp.sum(grads * o_ref[0].astype(WIDE), axis=0, keepdims=True)
    for first in range(0, rows, sub):
        cols = pl.ds(first, sub)
        q, do = q_ref[0, 0, :, cols], do_ref[0, :, cols]
        log_total, inner = log_ref[0, :, cols], inner_ref[:, cols]
        q_rows, do_rows = query_rows[cols], grad_rows[cols]

        def pair(part, offset, size, masked):
            span = pl.ds(offset, size)
            scores = dot(key_rows[part, span], q, 1, 0)
            if masked:
                scores = causal(scores)
            probs = jnp.exp(scores - log_total)
            grad_probs = dot(value_rows[part, span], do, 1, 0)
            grad_scores = (probs * (grad_probs - inner)).astype(LOW)
            value_sum[part, span] += dot(probs.astype(LOW), do_rows, 1, 0)
            key_sum[part, span] += dot(grad_scores, q_rows, 1, 0)
            return dot(k_ref[part, 0, :, span], grad_scores, 1, 0)

        grad_q = pair(step, first, sub, True)
        if first:
            grad_q = grad_q + pair(step, 0, first, False)
        grad_q = lax.fori_loop(
            0, step, lambda part, carried: carried + pair(part, 0, rows, False), grad_q
        )
        out_ref[step, 0, :, cols] = (grad_q * HEAD ** (-0.5)).astype(LOW)

    @pl.when(step == parts - 1)
    def _():
        for part in range(parts):
            out_ref[part, 1] = jnp.transpose(key_sum[part]).astype(LOW)
            out_ref[part, 2] = jnp.transpose(value_sum[part]).astype(LOW)


def attend_backward(packed, grads, attended, log_totals):
    parts, _, _, rows = packed.shape
    block = pl.BlockSpec((1, HEAD, rows), lambda i: (i, 0, 0))
    return pl.pallas_call(
        backward_kernel,
        grid=(parts,),
        in_specs=[
            pl.BlockSpec((1, 1, HEAD, rows), lambda i: (i, 0, 0, 0)),
            pl.BlockSpec((parts, 1, HEAD, rows), lambda i: (0, 1, 0, 0)),
            pl.BlockSpec((parts, 1, HEAD, rows), lambda i: (0, 2, 0, 0)),
            block,
            block,
            pl.BlockSpec((1, 1, rows), lambda i: (i, 0, 0)),
        ],
        out_specs=pl.BlockSpec((parts, 3, HEAD, rows), lambda i: (0, 0, 0, 0)),
        out_shape=jax.ShapeDtypeStruct(packed.shape, LOW),
        scratch_shapes=[
            pltpu.VMEM((parts, rows, HEAD), LOW),
            pltpu.VMEM((parts, rows, HEAD), LOW),
            pltpu.VMEM((rows, HEAD), LOW),
            pltpu.VMEM((rows, HEAD), LOW),
            pltpu.VMEM((1, rows), WIDE),
            pltpu.VMEM((parts, rows, HEAD), WIDE),
            pltpu.VMEM((parts, rows, HEAD), WIDE),
        ],
        compiler_params=pltpu.CompilerParams(vmem_limit_bytes=40 << 20),
        cost_estimate=pair_cost(parts, rows, 5),
        name="attend_backward",
    )(packed, packed, packed, grads, attended, log_totals)


def swap(message):
    return lax.all_to_all(message, "seq", split_axis=0, concat_axis=0, tiled=True)


def normalize(values, axis):
    centred = values - jnp.mean(values, axis=axis, keepdims=True)
    scale = lax.rsqrt(jnp.mean(centred * centred, axis=axis, keepdims=True) + EPSILON)
    return centred * scale, scale


def norm_back(grad, normed, scale):
    return scale * (
        grad
        - jnp.mean(grad, axis=0, keepdims=True)
        - normed * jnp.mean(grad * normed, axis=0, keepdims=True)
    )


def gather(shard):
    return lax.all_gather(shard, "dp", axis=0, tiled=True)


def scatter(whole):
    summed = lax.psum_scatter(whole.astype(LOW), "dp", scatter_dimension=0, tiled=True)
    return lax.psum(summed, "seq").astype(WIDE)


def shards(
    tokens, first_values, cotangent, ln1_gain, ln1_bias, w_query, w_key, w_value, w_out,
    ln2_gain, ln2_bias, w_fc, w_proj,
):
    owners = lax.axis_size("dp")
    groups = lax.axis_size("seq")
    rows, width = tokens.shape
    local = HEADS // groups
    part, fresh_part = w_query.shape[1], w_value.shape[1]
    fresh_width = fresh_part * owners

    vectors = jnp.concatenate([ln1_gain, ln1_bias, ln2_gain, ln2_bias])
    vectors = jnp.pad(vectors[None], ((0, 15), (0, width - vectors.shape[0])))
    first_pack = jnp.concatenate([w_query.T, w_key.T, w_value.T, vectors], axis=0)
    first_pack = gather(first_pack).reshape(owners, -1, width)
    query_t = first_pack[:, :part].reshape(width, width)
    key_t = first_pack[:, part : 2 * part].reshape(width, width)
    value_t = first_pack[:, 2 * part : 2 * part + fresh_part].reshape(fresh_width, width)
    vectors = first_pack[:, 2 * part + fresh_part, : 4 * part].reshape(owners, 4, part)
    vectors = vectors.transpose(1, 0, 2).reshape(4, width).astype(WIDE)
    out_t = gather(w_out.T)
    fc_t = gather(w_fc.T)
    proj_t = gather(w_proj.T)

    inputs = tokens.astype(WIDE)
    normed_one, scale_one = normalize(inputs, 1)
    low_one = (normed_one * vectors[0] + vectors[1]).astype(LOW)
    queries = dot(query_t, low_one, 1, 1).astype(LOW) * jnp.asarray(HEAD ** (-0.5), LOW)
    keys = dot(key_t, low_one, 1, 1).astype(LOW)
    fresh = dot(value_t, low_one, 1, 1).astype(LOW)
    values = jnp.concatenate([fresh, first_values.T], axis=0)
    by_head = jnp.stack([queries, keys, values]).reshape(3, groups, local, HEAD, rows)

    packed, attended, log_totals, returned = [], [], [], []
    for head in range(local):
        packed.append(swap(by_head[:, :, head].transpose(1, 0, 2, 3)))
    for head in range(local):
        mixed, log_total = attend(packed[head])
        attended.append(mixed)
        log_totals.append(log_total)
        returned.append(swap(mixed))
    attn = jnp.stack(returned, axis=1).reshape(width, rows)

    inputs_t = tokens.T.astype(WIDE)
    cot_t = cotangent.T
    residual = inputs_t + dot(out_t, attn, 1, 0)
    normed_two, scale_two = normalize(residual, 0)
    low_two = (normed_two * vectors[2][:, None] + vectors[3][:, None]).astype(LOW)
    hidden = dot(fc_t, low_two, 1, 0)
    active, gelu_pull = jax.vjp(functools.partial(jax.nn.gelu, approximate=True), hidden)
    low_active = active.astype(LOW)
    output = (residual + dot(proj_t, low_active, 1, 0)).astype(LOW).T

    (grad_hidden,) = gelu_pull(dot(proj_t, cot_t, 0, 0))
    grad_hidden = grad_hidden.astype(LOW)
    grad_proj = dot(cot_t, low_active, 1, 1)
    grad_fc = dot(grad_hidden, low_two, 1, 1)
    grad_two = dot(fc_t, grad_hidden, 0, 0)
    grad_gain_two = jnp.sum(grad_two * normed_two, axis=1)
    grad_bias_two = jnp.sum(grad_two, axis=1)
    grad_residual = cot_t.astype(WIDE) + norm_back(
        grad_two * vectors[2][:, None], normed_two, scale_two
    )
    grad_mixed = grad_residual.astype(LOW)
    grad_out = dot(grad_mixed, attn, 1, 1)
    grad_attended = dot(out_t, grad_mixed, 0, 0).astype(LOW)
    grad_attended = grad_attended.reshape(groups, local, HEAD, rows)

    grad_heads = []
    incoming = [swap(grad_attended[:, head]) for head in range(local)]
    for head in range(local):
        grads = attend_backward(packed[head], incoming[head], attended[head], log_totals[head])
        grad_heads.append(swap(grads))
    grad_heads = jnp.stack(grad_heads, axis=1)
    back_q, back_k, back_v = (
        grad_heads[:, :, which].reshape(width, rows) for which in range(3)
    )
    grad_fresh, grad_first = back_v[:fresh_width], back_v[fresh_width:].T
    grad_query = dot(back_q, low_one, 1, 0)
    grad_key = dot(back_k, low_one, 1, 0)
    grad_value = dot(grad_fresh, low_one, 1, 0)
    grad_one = dot(query_t, back_q, 0, 0) + dot(key_t, back_k, 0, 0) + dot(value_t, grad_fresh, 0, 0)
    normed_one_t, scale_one_t = normalize(inputs_t, 0)
    grad_gain_one = jnp.sum(grad_one * normed_one_t, axis=1)
    grad_bias_one = jnp.sum(grad_one, axis=1)
    grad_tokens = grad_residual + norm_back(
        grad_one * vectors[0][:, None], normed_one_t, scale_one_t
    )
    grad_tokens = grad_tokens.astype(LOW).T

    grad_vectors = jnp.stack([grad_gain_one, grad_bias_one, grad_gain_two, grad_bias_two])
    grad_vectors = grad_vectors.reshape(4, owners, part).transpose(1, 0, 2).reshape(owners, 1, -1)
    grad_vectors = jnp.pad(grad_vectors, ((0, 0), (0, 15), (0, width - 4 * part)))
    last_pack = jnp.concatenate(
        [
            grad_query.reshape(owners, part, width).astype(LOW),
            grad_key.reshape(owners, part, width).astype(LOW),
            grad_value.reshape(owners, fresh_part, width).astype(LOW),
            grad_vectors.astype(LOW),
        ],
        axis=1,
    )
    last_pack = scatter(last_pack.reshape(-1, width))
    vectors = last_pack[2 * part + fresh_part, : 4 * part].reshape(4, part)
    return (
        output,
        grad_tokens,
        grad_first,
        vectors[0],
        vectors[1],
        last_pack[:part].T,
        last_pack[part : 2 * part].T,
        last_pack[2 * part : 2 * part + fresh_part].T,
        scatter(grad_out).T,
        vectors[2],
        vectors[3],
        scatter(grad_fc).T,
        scatter(grad_proj).T,
    )


def solution(mesh):
    row = P(("dp", "seq"), None)
    vector, matrix = P("dp"), P(None, "dp")
    weights = (vector, vector, matrix, matrix, matrix, matrix, vector, vector, matrix, matrix)
    return jax.shard_map(
        shards,
        mesh=mesh,
        in_specs=(row, row, row) + weights,
        out_specs=(row, row, row) + weights,
        check_vma=False,
    )
```

```python
import functools

import jax
import jax.numpy as jnp
from jax import lax
from jax.experimental import pallas as pl
from jax.experimental.pallas import tpu as pltpu
from jax.sharding import PartitionSpec as P

HEADS = 12
HEAD = 64
EPSILON = 1e-05
LOW = jnp.bfloat16
WIDE = jnp.float32


def dot(left, right, left_dim, right_dim):
    return lax.dot_general(
        left, right, (((left_dim,), (right_dim,)), ((), ())), preferred_element_type=WIDE
    )


def causal(scores):
    key_pos = lax.broadcasted_iota(jnp.int32, scores.shape, 0)
    query_pos = lax.broadcasted_iota(jnp.int32, scores.shape, 1)
    return jnp.where(key_pos <= query_pos, scores, -1e30)


def turned(block):
    return jnp.transpose(block.astype(WIDE)).astype(LOW)


def sub_width(rows):
    for parts in (2, 3, 4, 6):
        if rows % (parts * 128) == 0:
            return rows // parts
    return rows


def forward_kernel(q_ref, k_ref, v_ref, o_ref, log_ref, key_rows):
    step = pl.program_id(0)
    parts, rows = k_ref.shape[0], k_ref.shape[3]
    sub = sub_width(rows)

    @pl.when(step == 0)
    def _():
        for part in range(parts):
            key_rows[part] = turned(k_ref[part, 0])

    for first in range(0, rows, sub):
        cols = pl.ds(first, sub)
        q = q_ref[0, 0, :, cols]
        blocks = []
        if first:
            blocks.append((0, dot(key_rows[step, pl.ds(0, first)], q, 1, 0)))
        blocks.append((first, causal(dot(key_rows[step, cols], q, 1, 0))))
        top = functools.reduce(
            jnp.maximum, [jnp.max(scores, axis=0, keepdims=True) for _, scores in blocks]
        )
        total = jnp.zeros((1, sub), WIDE)
        mixed = jnp.zeros((HEAD, sub), WIDE)
        for offset, scores in blocks:
            raised = jnp.exp(scores - top)
            total = total + jnp.sum(raised, axis=0, keepdims=True)
            mixed = mixed + dot(
                v_ref[step, 0, :, pl.ds(offset, scores.shape[0])], raised.astype(LOW), 1, 0
            )

        def earlier(part, carried):
            top, total, mixed = carried
            scores = dot(key_rows[part], q, 1, 0)
            new_top = jnp.maximum(top, jnp.max(scores, axis=0, keepdims=True))
            shrink = jnp.exp(top - new_top)
            raised = jnp.exp(scores - new_top)
            return (
                new_top,
                shrink * total + jnp.sum(raised, axis=0, keepdims=True),
                shrink * mixed + dot(v_ref[part, 0], raised.astype(LOW), 1, 0),
            )

        top, total, mixed = lax.fori_loop(0, step, earlier, (top, total, mixed))
        o_ref[0, :, cols] = (mixed / total).astype(LOW)
        log_ref[0, :, cols] = top + jnp.log(total)


def pair_cost(parts, rows, matmuls):
    pairs = parts * parts * rows * rows // 2
    return pl.CostEstimate(
        flops=2 * matmuls * pairs * HEAD * 4,
        bytes_accessed=parts * rows * HEAD * 16,
        transcendentals=pairs,
    )


def attend(packed):
    parts, _, _, rows = packed.shape
    return pl.pallas_call(
        forward_kernel,
        grid=(parts,),
        in_specs=[
            pl.BlockSpec((1, 1, HEAD, rows), lambda i: (i, 0, 0, 0)),
            pl.BlockSpec((parts, 1, HEAD, rows), lambda i: (0, 1, 0, 0)),
            pl.BlockSpec((parts, 1, HEAD, rows), lambda i: (0, 2, 0, 0)),
        ],
        out_specs=[
            pl.BlockSpec((1, HEAD, rows), lambda i: (i, 0, 0)),
            pl.BlockSpec((1, 1, rows), lambda i: (i, 0, 0)),
        ],
        out_shape=[
            jax.ShapeDtypeStruct((parts, HEAD, rows), LOW),
            jax.ShapeDtypeStruct((parts, 1, rows), WIDE),
        ],
        scratch_shapes=[pltpu.VMEM((parts, rows, HEAD), LOW)],
        compiler_params=pltpu.CompilerParams(vmem_limit_bytes=40 << 20),
        cost_estimate=pair_cost(parts, rows, 2),
        name="attend",
    )(packed, packed, packed)


def backward_kernel(
    q_ref, k_ref, v_ref, do_ref, o_ref, log_ref, out_ref,
    key_rows, value_rows, query_rows, grad_rows, inner_ref, key_sum, value_sum,
):
    step = pl.program_id(0)
    parts, rows = k_ref.shape[0], k_ref.shape[3]
    sub = sub_width(rows)

    @pl.when(step == 0)
    def _():
        for part in range(parts):
            key_rows[part] = turned(k_ref[part, 0])
            value_rows[part] = turned(v_ref[part, 0])
        key_sum[...] = jnp.zeros_like(key_sum)
        value_sum[...] = jnp.zeros_like(value_sum)

    query_rows[...] = turned(q_ref[0, 0])
    grads = do_ref[0].astype(WIDE)
    grad_rows[...] = jnp.transpose(grads).astype(LOW)
    inner_ref[...] = jnp.sum(grads * o_ref[0].astype(WIDE), axis=0, keepdims=True)
    for first in range(0, rows, sub):
        cols = pl.ds(first, sub)
        q, do = q_ref[0, 0, :, cols], do_ref[0, :, cols]
        log_total, inner = log_ref[0, :, cols], inner_ref[:, cols]
        q_rows, do_rows = query_rows[cols], grad_rows[cols]

        def pair(part, offset, size, masked):
            span = pl.ds(offset, size)
            scores = dot(key_rows[part, span], q, 1, 0)
            if masked:
                scores = causal(scores)
            probs = jnp.exp(scores - log_total)
            grad_probs = dot(value_rows[part, span], do, 1, 0)
            grad_scores = (probs * (grad_probs - inner)).astype(LOW)
            value_sum[part, span] += dot(probs.astype(LOW), do_rows, 1, 0)
            key_sum[part, span] += dot(grad_scores, q_rows, 1, 0)
            return dot(k_ref[part, 0, :, span], grad_scores, 1, 0)

        grad_q = pair(step, first, sub, True)
        if first:
            grad_q = grad_q + pair(step, 0, first, False)
        grad_q = lax.fori_loop(
            0, step, lambda part, carried: carried + pair(part, 0, rows, False), grad_q
        )
        out_ref[step, 0, :, cols] = (grad_q * HEAD ** (-0.5)).astype(LOW)

    @pl.when(step == parts - 1)
    def _():
        for part in range(parts):
            out_ref[part, 1] = jnp.transpose(key_sum[part]).astype(LOW)
            out_ref[part, 2] = jnp.transpose(value_sum[part]).astype(LOW)


def attend_backward(packed, grads, attended, log_totals):
    parts, _, _, rows = packed.shape
    block = pl.BlockSpec((1, HEAD, rows), lambda i: (i, 0, 0))
    return pl.pallas_call(
        backward_kernel,
        grid=(parts,),
        in_specs=[
            pl.BlockSpec((1, 1, HEAD, rows), lambda i: (i, 0, 0, 0)),
            pl.BlockSpec((parts, 1, HEAD, rows), lambda i: (0, 1, 0, 0)),
            pl.BlockSpec((parts, 1, HEAD, rows), lambda i: (0, 2, 0, 0)),
            block,
            block,
            pl.BlockSpec((1, 1, rows), lambda i: (i, 0, 0)),
        ],
        out_specs=pl.BlockSpec((parts, 3, HEAD, rows), lambda i: (0, 0, 0, 0)),
        out_shape=jax.ShapeDtypeStruct(packed.shape, LOW),
        scratch_shapes=[
            pltpu.VMEM((parts, rows, HEAD), LOW),
            pltpu.VMEM((parts, rows, HEAD), LOW),
            pltpu.VMEM((rows, HEAD), LOW),
            pltpu.VMEM((rows, HEAD), LOW),
            pltpu.VMEM((1, rows), WIDE),
            pltpu.VMEM((parts, rows, HEAD), WIDE),
            pltpu.VMEM((parts, rows, HEAD), WIDE),
        ],
        compiler_params=pltpu.CompilerParams(vmem_limit_bytes=40 << 20),
        cost_estimate=pair_cost(parts, rows, 5),
        name="attend_backward",
    )(packed, packed, packed, grads, attended, log_totals)


def normalize(values, axis):
    centred = values - jnp.mean(values, axis=axis, keepdims=True)
    scale = lax.rsqrt(jnp.mean(centred * centred, axis=axis, keepdims=True) + EPSILON)
    return centred * scale, scale


def norm_back(grad, normed, scale):
    return scale * (
        grad
        - jnp.mean(grad, axis=0, keepdims=True)
        - normed * jnp.mean(grad * normed, axis=0, keepdims=True)
    )


SLOPE = 0.7978845608028654


def qkv_kernel(
    order_ref, tokens_ref, gain_ref, bias_ref, near_ref, far_ref,
    q_ref, k_ref, v_ref, low_ref, low_one,
):
    step = pl.program_id(0)
    part, fresh_part = q_ref.shape[0], v_ref.shape[0]

    @pl.when(step == 0)
    def _():
        inputs = tokens_ref[...].astype(WIDE)
        centred = inputs - jnp.mean(inputs, axis=1, keepdims=True)
        scale = lax.rsqrt(jnp.mean(centred * centred, axis=1, keepdims=True) + EPSILON)
        low_one[...] = (centred * scale * gain_ref[...] + bias_ref[...]).astype(LOW)
        low_ref[...] = low_one[...]

    weights = jnp.where(order_ref[1, step] == 0, near_ref[0], far_ref[0])
    products = dot(weights, low_one[...], 1, 1)
    q_ref[...] = products[:part].astype(LOW) * jnp.asarray(HEAD ** (-0.5), LOW)
    k_ref[...] = products[part : 2 * part].astype(LOW)
    v_ref[...] = products[2 * part : 2 * part + fresh_part].astype(LOW)


def project(tokens, gain, bias, near, far, order, part, fresh_part):
    rows, width = tokens.shape
    owners = order.shape[1]
    shape = jax.ShapeDtypeStruct
    return pl.pallas_call(
        qkv_kernel,
        grid_spec=pltpu.PrefetchScalarGridSpec(
            num_scalar_prefetch=1,
            grid=(owners,),
            in_specs=[
                pl.BlockSpec((rows, width), lambda i, order: (0, 0)),
                pl.BlockSpec((1, width), lambda i, order: (0, 0)),
                pl.BlockSpec((1, width), lambda i, order: (0, 0)),
                pl.BlockSpec((1,) + near.shape[1:], lambda i, order: (order[0, i], 0, 0)),
                pl.BlockSpec((1,) + near.shape[1:], lambda i, order: (order[0, i], 0, 0)),
            ],
            out_specs=[
                pl.BlockSpec((part, rows), lambda i, order: (i, 0)),
                pl.BlockSpec((part, rows), lambda i, order: (i, 0)),
                pl.BlockSpec((fresh_part, rows), lambda i, order: (i, 0)),
                pl.BlockSpec((rows, width), lambda i, order: (0, 0)),
            ],
            scratch_shapes=[pltpu.VMEM((rows, width), LOW)],
        ),
        out_shape=[
            shape((width, rows), LOW),
            shape((width, rows), LOW),
            shape((fresh_part * owners, rows), LOW),
            shape((rows, width), LOW),
        ],
        compiler_params=pltpu.CompilerParams(vmem_limit_bytes=40 << 20),
        name="project",
    )(order, tokens, gain, bias, near, far)


def middle_kernel(
    attn_ref, tokens_ref, cot_ref, gain_ref, bias_ref, out_ref, fc_ref, proj_ref,
    output_ref, grad_out_ref, grad_fc_ref, grad_proj_ref, grad_attn_ref, grad_res_ref,
    grad_gain_ref, grad_bias_ref, low_ref, normed_ref, scale_ref, sum_ref, back_ref,
):
    step = pl.program_id(0)

    @pl.when(step == 0)
    def _():
        residual = tokens_ref[...].astype(WIDE) + dot(out_ref[...], attn_ref[...], 1, 0)
        normed, scale = normalize(residual, 0)
        low_ref[...] = (normed * gain_ref[...] + bias_ref[...]).astype(LOW)
        normed_ref[...] = normed
        scale_ref[...] = scale
        sum_ref[...] = residual
        back_ref[...] = jnp.zeros_like(back_ref)

    low = low_ref[...]
    hidden = dot(fc_ref[...], low, 1, 0)
    bent = jnp.tanh(SLOPE * (hidden + 0.044715 * hidden * hidden * hidden))
    half = 0.5 * (1.0 + bent)
    active = (hidden * half).astype(LOW)
    slope = half + hidden * (0.5 * (1.0 - bent * bent)) * (
        SLOPE * (1.0 + (3 * 0.044715) * hidden * hidden)
    )
    sum_ref[...] += dot(proj_ref[...], active, 1, 0)
    cot = cot_ref[...]
    grad_hidden = (dot(proj_ref[...], cot, 0, 0) * slope).astype(LOW)
    grad_proj_ref[...] = dot(cot, active, 1, 1).astype(LOW)
    grad_fc_ref[...] = dot(grad_hidden, low, 1, 1).astype(LOW)
    back_ref[...] += dot(fc_ref[...], grad_hidden, 0, 0)

    @pl.when(step == pl.num_programs(0) - 1)
    def _():
        output_ref[...] = jnp.transpose(sum_ref[...]).astype(LOW)
        grad, normed = back_ref[...], normed_ref[...]
        grad_gain_ref[...] = jnp.sum(grad * normed, axis=1, keepdims=True)
        grad_bias_ref[...] = jnp.sum(grad, axis=1, keepdims=True)
        grad_res = cot_ref[...].astype(WIDE) + norm_back(
            grad * gain_ref[...], normed, scale_ref[...]
        )
        grad_res_ref[...] = grad_res
        mixed = grad_res.astype(LOW)
        grad_attn_ref[...] = dot(out_ref[...], mixed, 0, 0).astype(LOW)
        grad_out_ref[...] = dot(mixed, attn_ref[...], 1, 1).astype(LOW)


def middle(attn, tokens_t, cot_t, gain, bias, out_t, fc_t, proj_t):
    width, rows = attn.shape
    hidden = fc_t.shape[0]
    block = 768 if hidden % 768 == 0 else 512
    shape = jax.ShapeDtypeStruct

    def whole(*dims):
        return pl.BlockSpec(dims, lambda j: (0, 0), pipeline_mode=pl.Buffered(1))

    down = pl.BlockSpec((block, width), lambda j: (j, 0))
    along = pl.BlockSpec((width, block), lambda j: (0, j))
    held = (width, rows)
    return pl.pallas_call(
        middle_kernel,
        grid=(hidden // block,),
        in_specs=[
            whole(*held), whole(*held), whole(*held), whole(width, 1), whole(width, 1),
            whole(width, width), down, along,
        ],
        out_specs=[
            whole(rows, width), whole(width, width), down, along, whole(*held), whole(*held),
            whole(width, 1), whole(width, 1),
        ],
        out_shape=[
            shape((rows, width), LOW), shape((width, width), LOW), shape((hidden, width), LOW),
            shape((width, hidden), LOW), shape(held, LOW), shape(held, WIDE),
            shape((width, 1), WIDE), shape((width, 1), WIDE),
        ],
        scratch_shapes=[
            pltpu.VMEM(held, LOW), pltpu.VMEM(held, WIDE), pltpu.VMEM((1, rows), WIDE),
            pltpu.VMEM(held, WIDE), pltpu.VMEM(held, WIDE),
        ],
        compiler_params=pltpu.CompilerParams(vmem_limit_bytes=56 << 20),
        name="middle",
    )(attn, tokens_t, cot_t, gain, bias, out_t, fc_t, proj_t)


def weights_kernel(
    q_ref, k_ref, v_ref, low_ref, query_ref, key_ref, value_ref, tokens_ref, gain_ref, bias_ref,
    pack_ref, grad_ref,
):
    owners = pack_ref.shape[0]
    low = low_ref[...]
    first = 0
    for back in (q_ref, k_ref, v_ref):
        grads = dot(back[...], low, 1, 0).astype(LOW)
        rows = grads.shape[0] // owners
        for owner in range(owners):
            pack_ref[owner, first : first + rows] = grads[owner * rows : (owner + 1) * rows]
        first += rows
    grad = (
        dot(query_ref[...], q_ref[...], 0, 0)
        + dot(key_ref[...], k_ref[...], 0, 0)
        + dot(value_ref[...], v_ref[...], 0, 0)
    )
    grad_ref[...] = grad
    normed, _ = normalize(tokens_ref[...].astype(WIDE), 0)
    lane = lax.broadcasted_iota(jnp.int32, (grad.shape[0], 128), 1)
    columns = (
        jnp.sum(grad * normed, axis=1, keepdims=True), jnp.sum(grad, axis=1, keepdims=True),
        gain_ref[...], bias_ref[...],
    )
    table = jnp.zeros(lane.shape, WIDE)
    for at, column in enumerate(columns):
        table = jnp.where(lane == at, column, table)
    table = jnp.transpose(table)[:16].astype(LOW)
    for owner in range(owners):
        pack_ref[owner, first : first + 16] = table


def weights_back(back_q, back_k, back_v, low_one, query_t, key_t, value_t, tokens_t, gain, bias, owners):
    width, rows = back_q.shape
    pack_rows = (2 * width + back_v.shape[0]) // owners + 16
    return pl.pallas_call(
        weights_kernel,
        out_shape=[
            jax.ShapeDtypeStruct((owners, pack_rows, width), LOW),
            jax.ShapeDtypeStruct((width, rows), WIDE),
        ],
        compiler_params=pltpu.CompilerParams(vmem_limit_bytes=56 << 20),
        name="weights_back",
    )(back_q, back_k, back_v, low_one, query_t, key_t, value_t, tokens_t, gain, bias)


def tokens_kernel(grad_ref, tokens_ref, res_ref, gain_ref, out_ref):
    normed, scale = normalize(tokens_ref[...].astype(WIDE), 0)
    grad = res_ref[...] + norm_back(grad_ref[...] * gain_ref[...], normed, scale)
    out_ref[...] = jnp.transpose(grad).astype(LOW)


def tokens_back(grad_one, tokens_t, grad_residual, gain):
    width, rows = grad_one.shape
    return pl.pallas_call(
        tokens_kernel,
        out_shape=jax.ShapeDtypeStruct((rows, width), LOW),
        compiler_params=pltpu.CompilerParams(vmem_limit_bytes=40 << 20),
        name="tokens_back",
    )(grad_one, tokens_t, grad_residual, gain)


def pick(stacked, index, axis=0):
    return lax.dynamic_index_in_dim(stacked, index, axis, keepdims=False)


def exchange(block, axis, bit):
    count = lax.axis_size(axis)
    return lax.ppermute(block, axis, [(i, i ^ (1 << bit)) for i in range(count)])


def after(*arrived):
    zero = 0
    for array in arrived:
        first = array[(0,) * array.ndim]
        zero = zero + (first != first).astype(jnp.int32)
    return zero


def swap(message, behind=None):
    count, here = lax.axis_size("seq"), lax.axis_index("seq")
    got = [pick(message, here)]
    for turn in range(1, count):
        at = (here + turn) % count
        if behind is not None:
            at = at + after(behind[turn])
        block = pick(message, at)
        got.append(
            lax.ppermute(block, "seq", [(i, (i + turn) % count) for i in range(count)])
        )
    whole = jnp.stack(got)
    return jnp.stack([pick(whole, (here - source) % count) for source in range(count)]), got


def gather_blocks(shard):
    count = lax.axis_size("dp")
    bits = count.bit_length() - 1
    half = shard.shape[0] // 2
    halves = []
    for block, order in (
        (shard[:half], range(1, bits)),
        (shard[half:], range(bits - 1, 0, -1)),
    ):
        held, offsets = block[None], [0]
        for bit in order:
            held = jnp.concatenate([held, exchange(held, "dp", bit)])
            offsets = offsets + [offset ^ (1 << bit) for offset in offsets]
        sorted_at = sorted(range(len(offsets)), key=lambda at: offsets[at])
        halves.append(jnp.stack([held[at] for at in sorted_at]))
    chip = jnp.concatenate(halves, axis=1)
    return chip, exchange(chip, "dp", 0)


def scatter_blocks(blocks):
    count, here = lax.axis_size("dp"), lax.axis_index("dp")
    bits = count.bit_length() - 1
    rows, width = blocks.shape[1:]

    def halve(held, bit, axis):
        mine = (here >> bit) & 1
        sent = exchange(pick(held, 1 - mine, axis).astype(LOW), "dp", bit)
        return pick(held, mine, axis).astype(WIDE) + sent.astype(WIDE)

    held = halve(blocks.reshape(count // 2, 2, rows, width), 0, 1)
    held = held.reshape((2,) * (bits - 1) + (rows, width))
    halves = []
    for block, order in (
        (held[..., : rows // 2, :], range(1, bits)),
        (held[..., rows // 2 :, :], range(bits - 1, 0, -1)),
    ):
        left = list(range(bits - 1, 0, -1))
        for bit in order:
            block = halve(block, bit, left.index(bit))
            left.remove(bit)
        halves.append(block)
    return jnp.concatenate(halves)


def sum_over_seq(block):
    count, here = lax.axis_size("seq"), lax.axis_index("seq")
    mine = here & 1
    halves = block.reshape((2, -1) + block.shape[1:])
    sent = exchange(pick(halves, 1 - mine).astype(LOW), "seq", 0)
    held = pick(halves, mine).astype(WIDE) + sent.astype(WIDE)
    for bit in range(1, count.bit_length() - 1):
        held = held + exchange(held.astype(LOW), "seq", bit).astype(WIDE)
    held = held.astype(LOW)
    other = exchange(held, "seq", 0)
    first, second = jnp.where(mine == 0, held, other), jnp.where(mine == 0, other, held)
    return jnp.concatenate([first, second]).astype(WIDE)


def gather(shard):
    return lax.all_gather(shard, "dp", axis=0, tiled=True)


def scatter(whole):
    return lax.psum_scatter(whole.astype(LOW), "dp", scatter_dimension=0, tiled=True)


def shards(
    tokens, first_values, cotangent, ln1_gain, ln1_bias, w_query, w_key, w_value, w_out,
    ln2_gain, ln2_bias, w_fc, w_proj,
):
    owners = lax.axis_size("dp")
    groups = lax.axis_size("seq")
    rows, width = tokens.shape
    local = HEADS // groups
    part, fresh_part = w_query.shape[1], w_value.shape[1]
    fresh_width = fresh_part * owners

    weight_rows = -(-(2 * part + fresh_part) // 16) * 16
    pack_rows = -(-(weight_rows + 16) // 32) * 32
    aligned = fresh_part % 16 == 0 and pack_rows == weight_rows + 16
    here = lax.axis_index("dp")

    vectors = jnp.concatenate([ln1_gain, ln1_bias, ln2_gain, ln2_bias])[None]
    first_pack = jnp.concatenate([w_query.T, w_key.T, w_value.T], axis=0)
    first_pack = jnp.pad(first_pack, ((0, weight_rows - first_pack.shape[0]), (0, 0)))
    vectors = jnp.pad(
        vectors, ((0, pack_rows - weight_rows - 1), (0, width - vectors.shape[1]))
    )
    near, far = gather_blocks(jnp.concatenate([first_pack, vectors], axis=0))
    out_t = gather(w_out.T)
    fc_t = gather(w_fc.T)
    proj_t = gather(w_proj.T)

    def rejoin(first, count, zero=0):
        blocks = []
        for owner in range(owners):
            offset = owner ^ (here + zero)
            block = jnp.where(offset & 1, pick(far, offset >> 1), pick(near, offset >> 1))
            blocks.append(block[first : first + count])
        return jnp.concatenate(blocks)

    def by_head(features):
        return features.reshape(-1, groups, HEAD, rows)

    early = {}
    first_t = first_values.T
    for slot in range(-(-fresh_width // (groups * HEAD)), local):
        first = (slot * groups * HEAD - fresh_width) // HEAD
        early[slot], _ = swap(first_t.reshape(-1, HEAD, rows)[first : first + groups])

    vectors = rejoin(weight_rows, 1)[:, : 4 * part].reshape(owners, 4, part)
    vectors = vectors.transpose(1, 0, 2).reshape(4, width).astype(WIDE)
    gain_one, bias_one, gain_two, bias_two = (vectors[at : at + 1] for at in range(4))
    if aligned:
        offsets = jnp.arange(owners, dtype=jnp.int32) ^ here
        queries, keys, fresh, low_one = project(
            tokens, gain_one, bias_one, near, far,
            jnp.stack([offsets >> 1, offsets & 1]), part, fresh_part,
        )
    else:
        normed_one, _ = normalize(tokens.astype(WIDE), 1)
        low_one = (normed_one * gain_one + bias_one).astype(LOW)
        queries = dot(rejoin(0, part), low_one, 1, 1).astype(LOW)
        queries = queries * jnp.asarray(HEAD ** (-0.5), LOW)
        keys = dot(rejoin(part, part), low_one, 1, 1).astype(LOW)
        fresh = dot(rejoin(2 * part, fresh_part), low_one, 1, 1).astype(LOW)
    values = jnp.concatenate([fresh, first_t], axis=0)
    queries, keys, values = by_head(queries), by_head(keys), by_head(values)

    packed, attended, log_totals, returned = {}, {}, {}, {}
    behind = None
    for slot in reversed(range(local)):
        late = [queries[slot], keys[slot]]
        if slot not in early:
            late.append(values[slot])
        arrived, behind = swap(jnp.stack(late, axis=1), behind)
        if slot in early:
            arrived = jnp.concatenate([arrived, early[slot][:, None]], axis=1)
            zero = after(behind[1])
        packed[slot] = arrived
    for slot in reversed(range(local)):
        attended[slot], log_totals[slot] = attend(packed[slot])
        returned[slot], _ = swap(attended[slot], behind if slot else None)
    attn = jnp.stack([returned[slot] for slot in range(local)]).reshape(width, rows)

    query_t, key_t = rejoin(0, part, zero), rejoin(part, part, zero)
    value_t = rejoin(2 * part, fresh_part, zero)
    tokens_t, cot_t = tokens.T, cotangent.T
    (
        output, grad_out, grad_fc, grad_proj, grad_attended, grad_residual,
        grad_gain_two, grad_bias_two,
    ) = middle(attn, tokens_t, cot_t, gain_two.T, bias_two.T, out_t, fc_t, proj_t)
    grad_attended = by_head(grad_attended)
    grad_fc = scatter(grad_fc)
    grad_out = scatter(grad_out)

    incoming = {}
    behind = None
    for slot in range(local):
        incoming[slot], sent = swap(grad_attended[slot], behind)
        behind = sent if behind is None else behind
    grad_proj = scatter_blocks(grad_proj.reshape(owners, part, -1))
    back_q, back_k, back_v = [], [], []
    for slot in range(local):
        grads = attend_backward(packed[slot], incoming[slot], attended[slot], log_totals[slot])
        if slot in early:
            home, sent = swap(grads[:, :2])
            back_v.append(swap(grads[:, 2], sent)[0])
        else:
            home, sent = swap(grads)
            back_v.append(home[:, 2])
        back_q.append(home[:, 0])
        back_k.append(home[:, 1])
    back_q = jnp.stack(back_q).reshape(width, rows)
    back_k = jnp.stack(back_k).reshape(width, rows)
    back_v = jnp.stack(back_v).reshape(width, rows)
    grad_fresh, grad_first = back_v[:fresh_width], back_v[fresh_width:].T
    if aligned:
        last_pack, grad_one = weights_back(
            back_q, back_k, grad_fresh, low_one, query_t, key_t, value_t, tokens_t,
            grad_gain_two, grad_bias_two, owners,
        )
    else:
        grad_one = (
            dot(query_t, back_q, 0, 0)
            + dot(key_t, back_k, 0, 0)
            + dot(value_t, grad_fresh, 0, 0)
        )
        normed_one, _ = normalize(tokens_t.astype(WIDE), 0)
        table = jnp.concatenate(
            [
                jnp.sum(grad_one * normed_one, axis=1, keepdims=True),
                jnp.sum(grad_one, axis=1, keepdims=True),
                grad_gain_two,
                grad_bias_two,
            ],
            axis=1,
        ).T
        last_rows = 2 * part + fresh_part
        last_pack = jnp.concatenate(
            [
                dot(back_q, low_one, 1, 0).reshape(owners, part, width),
                dot(back_k, low_one, 1, 0).reshape(owners, part, width),
                dot(grad_fresh, low_one, 1, 0).reshape(owners, fresh_part, width),
                jnp.zeros((owners, weight_rows - last_rows, width), WIDE),
                jnp.broadcast_to(table, (owners, 4, width)),
                jnp.zeros((owners, pack_rows - weight_rows - 4, width), WIDE),
            ],
            axis=1,
        ).astype(LOW)
    grad_tokens = tokens_back(grad_one, tokens_t, grad_residual, gain_one.T)
    last_pack = sum_over_seq(scatter_blocks(last_pack))
    vectors = last_pack[weight_rows : weight_rows + 4].reshape(4, owners, part)
    vectors = pick(vectors, here, 1)
    return (
        output,
        grad_tokens,
        grad_first,
        vectors[0],
        vectors[1],
        last_pack[:part].T,
        last_pack[part : 2 * part].T,
        last_pack[2 * part : 2 * part + fresh_part].T,
        sum_over_seq(grad_out.astype(WIDE)).T,
        vectors[2],
        vectors[3],
        sum_over_seq(grad_fc.astype(WIDE)).T,
        sum_over_seq(grad_proj).T,
    )


def solution(mesh):
    row = P(("dp", "seq"), None)
    vector, matrix = P("dp"), P(None, "dp")
    weights = (vector, vector, matrix, matrix, matrix, matrix, vector, vector, matrix, matrix)
    return jax.shard_map(
        shards,
        mesh=mesh,
        in_specs=(row, row, row) + weights,
        out_specs=(row, row, row) + weights,
        check_vma=False,
    )
```

```python
import functools
import math

import jax
import jax.numpy as jnp
from jax import lax
from jax.experimental import pallas as pl
from jax.experimental.pallas import tpu as pltpu
from jax.sharding import PartitionSpec as P

HEADS = 12
HEAD = 64
EPSILON = 1e-05
LOW = jnp.bfloat16
WIDE = jnp.float32


def dot(left, right, left_dim, right_dim):
    return lax.dot_general(
        left, right, (((left_dim,), (right_dim,)), ((), ())), preferred_element_type=WIDE
    )


def causal(scores):
    key_pos = lax.broadcasted_iota(jnp.int32, scores.shape, 0)
    query_pos = lax.broadcasted_iota(jnp.int32, scores.shape, 1)
    return jnp.where(key_pos <= query_pos, scores, -1e30)


def turned(block):
    return jnp.transpose(block.astype(WIDE)).astype(LOW)


def sub_width(rows):
    for parts in (2, 3, 4, 6):
        if rows % (parts * 128) == 0:
            return rows // parts
    return rows


def normalize(values, axis):
    centred = values - jnp.mean(values, axis=axis, keepdims=True)
    scale = lax.rsqrt(jnp.mean(centred * centred, axis=axis, keepdims=True) + EPSILON)
    return centred * scale, scale


def norm_back(grad, normed, scale):
    return scale * (
        grad
        - jnp.mean(grad, axis=0, keepdims=True)
        - normed * jnp.mean(grad * normed, axis=0, keepdims=True)
    )


def whole(*dims):
    return pl.BlockSpec(dims, lambda *_: (0,) * len(dims), pipeline_mode=pl.Buffered(1))


def untouched():
    return pl.BlockSpec(memory_space=pl.ANY)


def head_block(rows, at):
    return pl.BlockSpec((1, 1, HEAD, rows), lambda i: (i, at, 0, 0))


def head_whole(parts, rows, at):
    return pl.BlockSpec((parts, 1, HEAD, rows), lambda i: (0, at, 0, 0))


def grant(mebibytes):
    return pltpu.CompilerParams(vmem_limit_bytes=mebibytes << 20)


def forward_kernel(q_ref, k_ref, v_ref, *refs):
    o_ref, log_ref, key_rows = refs[-4], refs[-3], refs[-1]
    step = pl.program_id(0)
    parts, rows = k_ref.shape[0], k_ref.shape[3]
    sub = sub_width(rows)

    @pl.when(step == 0)
    def _():
        for part in range(parts):
            key_rows[part] = turned(k_ref[part, 0])

    for first in range(0, rows, sub):
        cols = pl.ds(first, sub)
        q = q_ref[0, 0, :, cols]
        blocks = []
        if first:
            blocks.append((0, dot(key_rows[step, pl.ds(0, first)], q, 1, 0)))
        blocks.append((first, causal(dot(key_rows[step, cols], q, 1, 0))))
        top = functools.reduce(
            jnp.maximum, [jnp.max(scores, axis=0, keepdims=True) for _, scores in blocks]
        )
        total = jnp.zeros((1, sub), WIDE)
        mixed = jnp.zeros((HEAD, sub), WIDE)
        for offset, scores in blocks:
            raised = jnp.exp(scores - top)
            total = total + jnp.sum(raised, axis=0, keepdims=True)
            mixed = mixed + dot(
                v_ref[step, 0, :, pl.ds(offset, scores.shape[0])], raised.astype(LOW), 1, 0
            )

        def earlier(part, carried):
            top, total, mixed = carried
            scores = dot(key_rows[part], q, 1, 0)
            new_top = jnp.maximum(top, jnp.max(scores, axis=0, keepdims=True))
            shrink = jnp.exp(top - new_top)
            raised = jnp.exp(scores - new_top)
            return (
                new_top,
                shrink * total + jnp.sum(raised, axis=0, keepdims=True),
                shrink * mixed + dot(v_ref[part, 0], raised.astype(LOW), 1, 0),
            )

        top, total, mixed = lax.fori_loop(0, step, earlier, (top, total, mixed))
        o_ref[0, 0, :, cols] = (mixed / total).astype(LOW)
        log_ref[0, :, cols] = top + jnp.log(total)


def pair_cost(parts, rows, matmuls):
    pairs = parts * parts * rows * rows // 2
    return pl.CostEstimate(
        flops=2 * matmuls * pairs * HEAD * 4,
        bytes_accessed=parts * rows * HEAD * 16,
        transcendentals=pairs,
    )


def attend(packed, values, value_at, held, held_at, held_slots, passed):
    parts, _, _, rows = packed.shape
    shape = jax.ShapeDtypeStruct
    carried = [] if held is None else [held]
    first = 3 + len(carried)
    aliases = {first: 2} if held is None else {3: 0, first: 2}
    return pl.pallas_call(
        forward_kernel,
        grid=(parts,),
        in_specs=[
            head_block(rows, 0), head_whole(parts, rows, 1), head_whole(parts, rows, value_at),
        ]
        + [untouched() for _ in carried]
        + [untouched()],
        out_specs=[
            head_block(rows, held_at),
            pl.BlockSpec((1, 1, rows), lambda i: (i, 0, 0)),
            untouched(),
        ],
        out_shape=[
            shape((parts, held_slots, HEAD, rows), LOW),
            shape((parts, 1, rows), WIDE),
            shape(passed.shape, passed.dtype),
        ],
        scratch_shapes=[pltpu.VMEM((parts, rows, HEAD), LOW)],
        input_output_aliases=aliases,
        compiler_params=grant(40),
        cost_estimate=pair_cost(parts, rows, 2),
        name="attend",
    )(packed, packed, values, *carried, passed)


def backward_kernel(
    q_ref, k_ref, v_ref, do_ref, o_ref, log_ref, behind_ref, out_ref,
    key_rows, value_rows, query_rows, grad_rows, inner_ref, key_sum, value_sum,
):
    step = pl.program_id(0)
    parts, rows = k_ref.shape[0], k_ref.shape[3]
    sub = sub_width(rows)

    @pl.when(step == 0)
    def _():
        for part in range(parts):
            key_rows[part] = turned(k_ref[part, 0])
            value_rows[part] = turned(v_ref[part, 0])
        key_sum[...] = jnp.zeros_like(key_sum)
        value_sum[...] = jnp.zeros_like(value_sum)

    query_rows[...] = turned(q_ref[0, 0])
    grads = do_ref[0, 0].astype(WIDE)
    grad_rows[...] = jnp.transpose(grads).astype(LOW)
    inner_ref[...] = jnp.sum(grads * o_ref[0, 0].astype(WIDE), axis=0, keepdims=True)
    for first in range(0, rows, sub):
        cols = pl.ds(first, sub)
        q, do = q_ref[0, 0, :, cols], do_ref[0, 0, :, cols]
        log_total, inner = log_ref[0, :, cols], inner_ref[:, cols]
        q_rows, do_rows = query_rows[cols], grad_rows[cols]

        def pair(part, offset, size, masked):
            span = pl.ds(offset, size)
            scores = dot(key_rows[part, span], q, 1, 0)
            if masked:
                scores = causal(scores)
            probs = jnp.exp(scores - log_total)
            grad_probs = dot(value_rows[part, span], do, 1, 0)
            grad_scores = (probs * (grad_probs - inner)).astype(LOW)
            value_sum[part, span] += dot(probs.astype(LOW), do_rows, 1, 0)
            key_sum[part, span] += dot(grad_scores, q_rows, 1, 0)
            return dot(k_ref[part, 0, :, span], grad_scores, 1, 0)

        grad_q = pair(step, first, sub, True)
        if first:
            grad_q = grad_q + pair(step, 0, first, False)
        grad_q = lax.fori_loop(
            0, step, lambda part, carried: carried + pair(part, 0, rows, False), grad_q
        )
        out_ref[step, 0, :, cols] = (grad_q * HEAD ** (-0.5)).astype(LOW)

    @pl.when(step == parts - 1)
    def _():
        for part in range(parts):
            out_ref[part, 1] = jnp.transpose(key_sum[part]).astype(LOW)
            out_ref[part, 2] = jnp.transpose(value_sum[part]).astype(LOW)


def attend_backward(
    packed, values, value_at, grads, grads_at, attended, attended_at, log_totals, behind
):
    parts, _, _, rows = packed.shape
    return pl.pallas_call(
        backward_kernel,
        grid=(parts,),
        in_specs=[
            head_block(rows, 0), head_whole(parts, rows, 1), head_whole(parts, rows, value_at),
            head_block(rows, grads_at), head_block(rows, attended_at),
            pl.BlockSpec((1, 1, rows), lambda i: (i, 0, 0)),
            untouched(),
        ],
        out_specs=pl.BlockSpec((parts, 3, HEAD, rows), lambda i: (0, 0, 0, 0)),
        out_shape=jax.ShapeDtypeStruct((parts, 3, HEAD, rows), LOW),
        scratch_shapes=[
            pltpu.VMEM((parts, rows, HEAD), LOW),
            pltpu.VMEM((parts, rows, HEAD), LOW),
            pltpu.VMEM((rows, HEAD), LOW),
            pltpu.VMEM((rows, HEAD), LOW),
            pltpu.VMEM((1, rows), WIDE),
            pltpu.VMEM((parts, rows, HEAD), WIDE),
            pltpu.VMEM((parts, rows, HEAD), WIDE),
        ],
        compiler_params=grant(40),
        cost_estimate=pair_cost(parts, rows, 5),
        name="attend_backward",
    )(packed, packed, values, grads, attended, log_totals, behind)


SLOPE = 0.7978845608028654


def project_kernel(
    order_ref, tokens_ref, first_ref, near_a, far_a, near_b, far_b, behind_ref, *refs,
):
    *messages, low_ref, turned_ref, query_ref, key_ref, value_ref, vec_ref = refs
    owners = order_ref.shape[1]
    part, fresh_part = query_ref.shape[0] // owners, value_ref.shape[0] // owners
    half = near_a.shape[1]
    groups = messages[0].shape[0]
    fresh_width = value_ref.shape[0]

    vectors = jnp.zeros((16, near_b.shape[2]), WIDE)
    for at in range(near_b.shape[0]):
        vectors = vectors + near_b[at, half - 16 :].astype(WIDE)
        vectors = vectors + far_b[at, half - 16 :].astype(WIDE)
    inputs = tokens_ref[...].astype(WIDE)
    normed, _ = normalize(inputs, 1)
    low_ref[...] = (normed * vectors[0:1] + vectors[1:2]).astype(LOW)
    turned_ref[...] = jnp.transpose(inputs).astype(LOW)
    blank = jnp.zeros((128 - vectors.shape[0], vectors.shape[1]), WIDE)
    vec_ref[...] = jnp.transpose(jnp.concatenate([vectors, blank], axis=0))
    for owner in range(owners):
        same_core = order_ref[0, owner] == 0
        weights = jnp.concatenate(
            [
                jnp.where(same_core, near_a[order_ref[1, owner]], far_a[order_ref[1, owner]]),
                jnp.where(same_core, near_b[order_ref[2, owner]], far_b[order_ref[2, owner]]),
            ],
            axis=0,
        )
        first = 0
        for ref, count in ((query_ref, part), (key_ref, part), (value_ref, fresh_part)):
            ref[owner * count : (owner + 1) * count] = weights[first : first + count]
            first += count
    low_one = low_ref[...]
    for which, ref in enumerate((query_ref, key_ref, value_ref)):
        products = dot(ref[...], low_one, 1, 1).astype(LOW)
        if which == 0:
            products = products * jnp.asarray(HEAD ** (-0.5), LOW)
        for slot, message in enumerate(messages):
            for group in range(groups):
                feature = (slot * groups + group) * HEAD
                if which < message.shape[1] and feature < products.shape[0]:
                    message[group, which] = products[feature : feature + HEAD]
    for slot, message in enumerate(messages):
        for group in range(groups):
            first = (slot * groups + group) * HEAD - fresh_width
            if message.shape[1] == 3 and first >= 0:
                start = first // 128 * 128
                block = turned(first_ref[:, start : start + 128])
                message[group, 2] = block[first - start : first - start + HEAD]


def project(tokens, first_values, halves, order, behind, widths, part, fresh_part, groups):
    rows, width = tokens.shape
    owners = order.shape[1]
    held = [tokens, first_values, *halves[0], *halves[1]]
    shape = jax.ShapeDtypeStruct
    outs = [shape((groups, count, HEAD, rows), LOW) for count in widths] + [
        shape((rows, width), LOW), shape((width, rows), LOW), shape((width, width), LOW),
        shape((width, width), LOW), shape((fresh_part * owners, width), LOW),
        shape((width, 128), WIDE),
    ]
    return pl.pallas_call(
        project_kernel,
        in_specs=[pl.BlockSpec(memory_space=pltpu.SMEM)]
        + [pl.BlockSpec(memory_space=pltpu.VMEM) for _ in held]
        + [untouched()],
        out_specs=[pl.BlockSpec(memory_space=pltpu.VMEM) for _ in outs],
        out_shape=outs,
        compiler_params=grant(48),
        name="project",
    )(order, *held, behind)


def project_plain(tokens, first_values, halves, order, behind, widths, part, fresh_part, groups):
    rows, width = tokens.shape
    owners = order.shape[1]
    blocks = []
    for owner in range(owners):
        pieces = []
        for at, (near, far) in enumerate(halves):
            index = order[1 + at, owner]
            pieces.append(jnp.where(order[0, owner] == 0, pick(near, index), pick(far, index)))
        blocks.append(jnp.concatenate(pieces, axis=0))
    blocks = jnp.stack(blocks)
    query_t = blocks[:, :part].reshape(-1, width)
    key_t = blocks[:, part : 2 * part].reshape(-1, width)
    value_t = blocks[:, 2 * part : 2 * part + fresh_part].reshape(-1, width)
    vectors = jnp.sum(blocks[:, -16:].astype(WIDE), axis=0)
    normed, _ = normalize(tokens.astype(WIDE), 1)
    low_one = (normed * vectors[0:1] + vectors[1:2]).astype(LOW)
    queries = dot(query_t, low_one, 1, 1).astype(LOW) * jnp.asarray(HEAD ** (-0.5), LOW)
    keys = dot(key_t, low_one, 1, 1).astype(LOW)
    values = jnp.concatenate([dot(value_t, low_one, 1, 1).astype(LOW), first_values.T], axis=0)
    stacked = [array.reshape(-1, groups, HEAD, rows) for array in (queries, keys, values)]
    messages = [
        jnp.stack([array[slot] for array in stacked[:count]], axis=1)
        for slot, count in enumerate(widths)
    ]
    table = jnp.pad(vectors.T, ((0, 0), (0, 128 - vectors.shape[0])))
    return (*messages, low_one, tokens.T, query_t, key_t, value_t, table)


def middle_kernel(
    attn_zero, attn_rest, tokens_ref, cot_ref, vec_ref, out_ref, fc_ref, proj_ref,
    output_ref, pack_ref, grad_zero, grad_rest, grad_res_ref, vec_back,
    attn_ref, cot_t, low_ref, normed_ref, scale_ref, sum_ref, back_ref,
):
    step = pl.program_id(0)
    owners = pack_ref.shape[0]
    block, width = fc_ref.shape
    part = width // owners
    fc_part = pl.num_programs(0) * block // owners
    share = block // fc_part
    groups = attn_zero.shape[0]

    def spots(zero, rest):
        for slot in range(1 + rest.shape[1]):
            for group in range(groups):
                ref = zero.at[group, 0] if slot == 0 else rest.at[group, slot - 1]
                yield (slot * groups + group) * HEAD, ref

    @pl.when(step == 0)
    def _():
        for first, ref in spots(attn_zero, attn_rest):
            attn_ref[first : first + HEAD] = ref[...]
        cot_t[...] = turned(cot_ref[...])
        residual = tokens_ref[...].astype(WIDE) + dot(out_ref[...], attn_ref[...], 1, 0)
        normed, scale = normalize(residual, 0)
        low_ref[...] = (normed * vec_ref[:, 2:3] + vec_ref[:, 3:4]).astype(LOW)
        normed_ref[...] = normed
        scale_ref[...] = scale
        sum_ref[...] = residual
        back_ref[...] = jnp.zeros_like(back_ref)

    low = low_ref[...]
    hidden = dot(fc_ref[...], low, 1, 0)
    bent = jnp.tanh(SLOPE * (hidden + 0.044715 * hidden * hidden * hidden))
    half = 0.5 * (1.0 + bent)
    active = (hidden * half).astype(LOW)
    slope = half + hidden * (0.5 * (1.0 - bent * bent)) * (
        SLOPE * (1.0 + (3 * 0.044715) * hidden * hidden)
    )
    sum_ref[...] += dot(proj_ref[...], active, 1, 0)
    cot = cot_t[...]
    grad_hidden = (dot(proj_ref[...], cot, 0, 0) * slope).astype(LOW)
    grad_proj = dot(cot, active, 1, 1).astype(LOW)
    grad_fc = dot(grad_hidden, low, 1, 1).astype(LOW)
    for owner in range(owners):
        pack_ref[owner, pl.ds(pl.multiple_of(fc_part + step * part, 16), part)] = grad_proj[
            owner * part : (owner + 1) * part
        ]
    for at in range(share):
        pack_ref[step * share + at, pl.ds(0, fc_part)] = grad_fc[at * fc_part : (at + 1) * fc_part]
    back_ref[...] += dot(fc_ref[...], grad_hidden, 0, 0)

    @pl.when(step == pl.num_programs(0) - 1)
    def _():
        output_ref[...] = jnp.transpose(sum_ref[...]).astype(LOW)
        grad, normed = back_ref[...], normed_ref[...]
        lane = lax.broadcasted_iota(jnp.int32, vec_back.shape, 1)
        grad_gain = jnp.sum(grad * normed, axis=1, keepdims=True)
        grad_bias = jnp.sum(grad, axis=1, keepdims=True)
        vec_back[...] = jnp.where(lane == 2, grad_gain, jnp.where(lane == 3, grad_bias, 0.0))
        grad_res = cot_t[...].astype(WIDE) + norm_back(
            grad * vec_ref[:, 2:3], normed, scale_ref[...]
        )
        grad_res_ref[...] = grad_res
        mixed = grad_res.astype(LOW)
        grad_attn = dot(out_ref[...], mixed, 0, 0).astype(LOW)
        for first, ref in spots(grad_zero, grad_rest):
            ref[...] = grad_attn[first : first + HEAD]
        grad_out = dot(mixed, attn_ref[...], 1, 1).astype(LOW)
        for owner in range(owners):
            pack_ref[owner, pl.ds(2 * fc_part, part)] = grad_out[owner * part : (owner + 1) * part]


def middle(attn_zero, attn_rest, tokens_t, cotangent, vectors, out_t, fc_t, proj_t, owners):
    width, rows = tokens_t.shape
    hidden = fc_t.shape[0]
    block = width
    shape = jax.ShapeDtypeStruct
    down = pl.BlockSpec((block, width), lambda j: (j, 0))
    along = pl.BlockSpec((width, block), lambda j: (0, j))
    held = (width, rows)
    pack = (owners, (2 * hidden + width) // owners, width)
    return pl.pallas_call(
        middle_kernel,
        grid=(hidden // block,),
        in_specs=[
            whole(*attn_zero.shape), whole(*attn_rest.shape), whole(*held), whole(rows, width),
            whole(width, 128), whole(width, width), down, along,
        ],
        out_specs=[
            whole(rows, width), whole(*pack), whole(*attn_zero.shape), whole(*attn_rest.shape),
            whole(*held), whole(width, 128),
        ],
        out_shape=[
            shape((rows, width), LOW), shape(pack, LOW), shape(attn_zero.shape, LOW),
            shape(attn_rest.shape, LOW), shape(held, WIDE), shape((width, 128), WIDE),
        ],
        scratch_shapes=[
            pltpu.VMEM(held, LOW), pltpu.VMEM(held, LOW), pltpu.VMEM(held, LOW),
            pltpu.VMEM(held, WIDE), pltpu.VMEM((1, rows), WIDE), pltpu.VMEM(held, WIDE),
            pltpu.VMEM(held, WIDE),
        ],
        compiler_params=grant(60),
        name="middle",
    )(attn_zero, attn_rest, tokens_t, cotangent, vectors, out_t, fc_t, proj_t)


def joined(zero, rest):
    both = jnp.concatenate([zero, rest], axis=1).swapaxes(0, 1)
    return both.reshape(-1, both.shape[-1])


def middle_plain(attn_zero, attn_rest, tokens_t, cotangent, vectors, out_t, fc_t, proj_t, owners):
    width = tokens_t.shape[0]
    attn = joined(attn_zero, attn_rest)
    gain, bias = vectors[:, 2:3], vectors[:, 3:4]
    cot_t = cotangent.T
    residual = tokens_t.astype(WIDE) + dot(out_t, attn, 1, 0)
    normed, scale = normalize(residual, 0)
    low = (normed * gain + bias).astype(LOW)
    hidden = dot(fc_t, low, 1, 0)
    active, pull = jax.vjp(functools.partial(jax.nn.gelu, approximate=True), hidden)
    low_active = active.astype(LOW)
    output = (residual + dot(proj_t, low_active, 1, 0)).astype(LOW).T
    (grad_hidden,) = pull(dot(proj_t, cot_t, 0, 0))
    grad_hidden = grad_hidden.astype(LOW)
    grad_proj = dot(cot_t, low_active, 1, 1).astype(LOW)
    grad_fc = dot(grad_hidden, low, 1, 1).astype(LOW)
    grad = dot(fc_t, grad_hidden, 0, 0)
    grad_gain = jnp.sum(grad * normed, axis=1, keepdims=True)
    grad_bias = jnp.sum(grad, axis=1, keepdims=True)
    grad_res = cot_t.astype(WIDE) + norm_back(grad * gain, normed, scale)
    mixed = grad_res.astype(LOW)
    part = width // owners
    grad_proj = grad_proj.reshape(owners, part, -1, width).transpose(0, 2, 1, 3)
    pack = jnp.concatenate(
        [
            grad_fc.reshape(owners, -1, width),
            grad_proj.reshape(owners, -1, width),
            dot(mixed, attn, 1, 1).astype(LOW).reshape(owners, part, width),
        ],
        axis=1,
    )
    grad_attn = dot(out_t, mixed, 0, 0).astype(LOW)
    grad_attn = grad_attn.reshape(-1, attn_zero.shape[0], HEAD, attn.shape[1]).swapaxes(0, 1)
    table = jnp.concatenate([jnp.zeros((width, 2), WIDE), grad_gain, grad_bias], axis=1)
    table = jnp.pad(table, ((0, 0), (0, 124)))
    return output, pack, grad_attn[:, :1], grad_attn[:, 1:], grad_res, table


def weights_kernel(*refs):
    *homes, low_ref, query_ref, key_ref, value_ref, tokens_ref, vec_ref = refs[:-5]
    pack_ref, grad_ref, q_ref, k_ref, v_ref = refs[-5:]
    owners = pack_ref.shape[0]
    groups = homes[0].shape[0]
    for slot, home in enumerate(homes):
        for group in range(groups):
            first = (slot * groups + group) * HEAD
            for which, back in enumerate((q_ref, k_ref, v_ref)):
                if first < back.shape[0]:
                    back[first : first + HEAD] = home[group, which]
    low = low_ref[...]
    first = 0
    for back in (q_ref, k_ref, v_ref):
        grads = dot(back[...], low, 1, 0).astype(LOW)
        rows = grads.shape[0] // owners
        for owner in range(owners):
            pack_ref[owner, first : first + rows] = grads[owner * rows : (owner + 1) * rows]
        first += rows
    grad = (
        dot(query_ref[...], q_ref[...], 0, 0)
        + dot(key_ref[...], k_ref[...], 0, 0)
        + dot(value_ref[...], v_ref[...], 0, 0)
    )
    grad_ref[...] = grad
    normed, _ = normalize(tokens_ref[...].astype(WIDE), 0)
    lane = lax.broadcasted_iota(jnp.int32, vec_ref.shape, 1)
    grad_gain = jnp.sum(grad * normed, axis=1, keepdims=True)
    grad_bias = jnp.sum(grad, axis=1, keepdims=True)
    table = jnp.where(lane == 0, grad_gain, jnp.where(lane == 1, grad_bias, vec_ref[...]))
    table = jnp.transpose(table)[:16].astype(LOW)
    for owner in range(owners):
        pack_ref[owner, first : first + 16] = table


def weights_back(homes, low_one, query_t, key_t, value_t, tokens_t, vec_back, owners):
    width, rows = tokens_t.shape
    fresh_width = value_t.shape[0]
    pack_rows = (2 * width + fresh_width) // owners + 16
    held = [*homes, low_one, query_t, key_t, value_t, tokens_t, vec_back]
    return pl.pallas_call(
        weights_kernel,
        out_shape=[
            jax.ShapeDtypeStruct((owners, pack_rows, width), LOW),
            jax.ShapeDtypeStruct((width, rows), WIDE),
        ],
        scratch_shapes=[
            pltpu.VMEM((width, rows), LOW), pltpu.VMEM((width, rows), LOW),
            pltpu.VMEM((fresh_width, rows), LOW),
        ],
        compiler_params=grant(56),
        name="weights_back",
    )(*held)


def weights_plain(homes, low_one, query_t, key_t, value_t, tokens_t, vec_back, owners):
    width, rows = tokens_t.shape
    back_q, back_k = (
        jnp.stack([home[:, which] for home in homes]).reshape(width, rows) for which in range(2)
    )
    back_v = jnp.stack([home[:, 2] for home in homes])
    back_v = back_v.reshape(-1, rows)[: value_t.shape[0]]
    grad = dot(query_t, back_q, 0, 0) + dot(key_t, back_k, 0, 0) + dot(value_t, back_v, 0, 0)
    normed, _ = normalize(tokens_t.astype(WIDE), 0)
    table = jnp.concatenate(
        [
            jnp.sum(grad * normed, axis=1, keepdims=True), jnp.sum(grad, axis=1, keepdims=True),
            vec_back[:, 2:16],
        ],
        axis=1,
    ).T
    pieces = [
        dot(back, low_one, 1, 0).reshape(owners, -1, width) for back in (back_q, back_k, back_v)
    ]
    count = sum(piece.shape[1] for piece in pieces)
    padded = -(-count // 16) * 16
    padded = -(-(padded + 16) // 32) * 32 - 16
    pieces.append(jnp.zeros((owners, padded - count, width), WIDE))
    pieces.append(jnp.broadcast_to(table, (owners,) + table.shape))
    return jnp.concatenate(pieces, axis=1).astype(LOW), grad


def tokens_kernel(grad_ref, tokens_ref, res_ref, gain_ref, out_ref):
    normed, scale = normalize(tokens_ref[...].astype(WIDE), 0)
    grad = res_ref[...] + norm_back(grad_ref[...] * gain_ref[:, 0:1], normed, scale)
    out_ref[...] = jnp.transpose(grad).astype(LOW)


def tokens_back(grad_one, tokens_t, grad_residual, vectors):
    width, rows = grad_one.shape
    return pl.pallas_call(
        tokens_kernel,
        out_shape=jax.ShapeDtypeStruct((rows, width), LOW),
        compiler_params=grant(40),
        name="tokens_back",
    )(grad_one, tokens_t, grad_residual, vectors)


def gate_kernel(*refs):
    pass


def gate(array, behind):
    return pl.pallas_call(
        gate_kernel,
        in_specs=[untouched(), untouched()],
        out_specs=untouched(),
        out_shape=jax.ShapeDtypeStruct(array.shape, array.dtype),
        input_output_aliases={0: 0},
        name="gate",
    )(array, behind)


def pick(stacked, index, axis=0):
    return lax.dynamic_index_in_dim(stacked, index, axis, keepdims=False)


def exchange(block, axis, bit):
    count = lax.axis_size(axis)
    return lax.ppermute(block, axis, [(i, i ^ (1 << bit)) for i in range(count)])


def swap(message):
    return lax.all_to_all(message, "seq", split_axis=0, concat_axis=0, tiled=True)


def gather_halves(shard, behind):
    bits = lax.axis_size("dp").bit_length() - 1
    half = shard.shape[0] // 2
    halves = []
    for block, order in (
        (shard[:half], range(1, bits)),
        (shard[half:], range(bits - 1, 0, -1)),
    ):
        held = block[None]
        for bit in order:
            held = jnp.concatenate([held, exchange(held, "dp", bit)])
        halves.append(held)
    halves[1] = gate(halves[1], behind)
    return [(held, exchange(held, "dp", 0)) for held in halves]


def gathered_order():
    count, here = lax.axis_size("dp"), lax.axis_index("dp")
    bits = count.bit_length() - 1
    offset = jnp.arange(count, dtype=jnp.int32) ^ here
    places = [0, 0]
    for at in range(bits - 1):
        bit = (offset >> (at + 1)) & 1
        places[0] = places[0] + (bit << at)
        places[1] = places[1] + (bit << (bits - 2 - at))
    return jnp.stack([offset & 1, *places])


def scatter_blocks(blocks):
    count, here = lax.axis_size("dp"), lax.axis_index("dp")
    bits = count.bit_length() - 1
    rows, width = blocks.shape[1:]

    def halve(held, bit, axis):
        mine = (here >> bit) & 1
        sent = exchange(pick(held, 1 - mine, axis).astype(LOW), "dp", bit)
        return pick(held, mine, axis).astype(WIDE) + sent.astype(WIDE)

    held = halve(blocks.reshape(count // 2, 2, rows, width), 0, 1)
    held = held.reshape((2,) * (bits - 1) + (rows, width))
    halves = []
    for block, order in (
        (held[..., : rows // 2, :], range(1, bits)),
        (held[..., rows // 2 :, :], range(bits - 1, 0, -1)),
    ):
        left = list(range(bits - 1, 0, -1))
        for bit in order:
            block = halve(block, bit, left.index(bit))
            left.remove(bit)
        halves.append(block)
    return jnp.concatenate(halves)


def sum_over_seq(block):
    count, here = lax.axis_size("seq"), lax.axis_index("seq")
    mine = here & 1
    halves = block.reshape((2, -1) + block.shape[1:])
    sent = exchange(pick(halves, 1 - mine).astype(LOW), "seq", 0)
    held = pick(halves, mine).astype(WIDE) + sent.astype(WIDE)
    for bit in range(1, count.bit_length() - 1):
        held = held + exchange(held.astype(LOW), "seq", bit).astype(WIDE)
    held = held.astype(LOW)
    other = exchange(held, "seq", 0)
    first, second = jnp.where(mine == 0, held, other), jnp.where(mine == 0, other, held)
    return jnp.concatenate([first, second]).astype(WIDE)


def gather(shard):
    return lax.all_gather(shard, "dp", axis=0, tiled=True)


def shards(
    tokens, first_values, cotangent, ln1_gain, ln1_bias, w_query, w_key, w_value, w_out,
    ln2_gain, ln2_bias, w_fc, w_proj,
):
    owners = lax.axis_size("dp")
    groups = lax.axis_size("seq")
    rows, width = tokens.shape
    local = HEADS // groups
    part, fresh_part = w_query.shape[1], w_value.shape[1]
    fresh_width = fresh_part * owners

    weight_rows = -(-(2 * part + fresh_part) // 16) * 16
    pack_rows = -(-(weight_rows + 16) // 32) * 32
    aligned = fresh_part % 16 == 0 and pack_rows == weight_rows + 16
    here = lax.axis_index("dp")

    last = local - 1
    first = (last * groups * HEAD - fresh_width) // HEAD
    early = first_values[:, first * HEAD :].T.reshape(groups, 1, HEAD, rows)
    early = swap(early)
    vectors = jnp.stack([ln1_gain, ln1_bias, ln2_gain, ln2_bias])
    vectors = lax.dynamic_update_slice(jnp.zeros((16, width), LOW), vectors, (0, here * part))
    first_pack = jnp.concatenate([w_query.T, w_key.T, w_value.T], axis=0)
    first_pack = jnp.pad(first_pack, ((0, pack_rows - 16 - first_pack.shape[0]), (0, 0)))
    halves = gather_halves(jnp.concatenate([first_pack, vectors], axis=0), early)
    out_t = gather(w_out.T)
    fc_t = gather(w_fc.T)
    proj_t = gather(w_proj.T)

    widths = [3] * last + [2]
    *messages, low_one, tokens_t, query_t, key_t, value_t, vectors = (
        project if aligned else project_plain
    )(
        tokens, first_values, halves, gathered_order(), early, widths, part, fresh_part, groups
    )

    arrived, log_totals, held = {}, {}, None
    for slot in reversed(range(local)):
        arrived[slot] = swap(messages[slot])
        if slot < last:
            done = slot + 1
            values, at = (early, 0) if done == last else (arrived[done], 2)
            wait = max(slot - 1, 0)
            passed = messages[wait] if slot else log_totals[last]
            held, log_totals[done], passed = attend(
                arrived[done], values, at, held, done - 1, last, passed
            )
            if slot:
                messages[wait] = passed
            else:
                log_totals[last] = passed
    rest = held
    zero, log_totals[0], _ = attend(arrived[0], arrived[0], 2, None, 0, 1, log_totals[1])

    output, grad_pack, grad_zero, grad_rest, grad_residual, vec_back = (
        middle if aligned else middle_plain
    )(swap(zero), swap(rest), tokens_t, cotangent, vectors, out_t, fc_t, proj_t, owners)
    grad_pack = lax.psum_scatter(
        grad_pack.reshape(-1, width), "dp", scatter_dimension=0, tiled=True
    )
    grad_pack = lax.psum(grad_pack, "seq")

    grad_zero = swap(grad_zero)
    grad_rest = swap(grad_rest)
    homes = []
    for slot in range(local):
        values, at = (early, 0) if slot == last else (arrived[slot], 2)
        grads, grads_at = (grad_rest, slot - 1) if slot else (grad_zero, 0)
        attended, attended_at = (rest, slot - 1) if slot else (zero, 0)
        behind = homes[slot - 2] if slot > 1 else log_totals[slot]
        grads = attend_backward(
            arrived[slot], values, at, grads, grads_at, attended, attended_at, log_totals[slot],
            behind,
        )
        homes.append(swap(grads))
    last_pack, grad_one = (weights_back if aligned else weights_plain)(
        homes, low_one, query_t, key_t, value_t, tokens_t, vec_back, owners
    )
    last_pack = sum_over_seq(gate(scatter_blocks(last_pack), grad_pack))
    grad_pack = grad_pack.astype(WIDE)
    grad_tokens = tokens_back(grad_one, tokens_t, grad_residual, vectors)
    grad_first = jnp.concatenate([home[:, 2] for home in homes]).reshape(-1, rows)
    grad_first = grad_first[fresh_width:].T

    vectors = last_pack[pack_rows - 16 : pack_rows - 12].reshape(4, owners, part)
    vectors = pick(vectors, here, 1)
    fc_part = w_fc.shape[1]
    grad_proj = grad_pack[fc_part : 2 * fc_part].reshape(-1, part, width).transpose(0, 2, 1)
    return (
        output,
        grad_tokens,
        grad_first,
        vectors[0],
        vectors[1],
        last_pack[:part].T,
        last_pack[part : 2 * part].T,
        last_pack[2 * part : 2 * part + fresh_part].T,
        grad_pack[2 * fc_part :].T,
        vectors[2],
        vectors[3],
        grad_pack[:fc_part].T,
        grad_proj.reshape(-1, part),
    )


def solution(mesh):
    row = P(("dp", "seq"), None)
    vector, matrix = P("dp"), P(None, "dp")
    weights = (vector, vector, matrix, matrix, matrix, matrix, vector, vector, matrix, matrix)
    return jax.shard_map(
        shards,
        mesh=mesh,
        in_specs=(row, row, row) + weights,
        out_specs=(row, row, row) + weights,
        check_vma=False,
    )
```

```python
import functools
import math

import jax
import jax.numpy as jnp
from jax import lax
from jax.experimental import pallas as pl
from jax.experimental.pallas import tpu as pltpu
from jax.sharding import PartitionSpec as P

HEADS = 12
HEAD = 64
EPSILON = 1e-05
LOW = jnp.bfloat16
WIDE = jnp.float32


def dot(left, right, left_dim, right_dim):
    return lax.dot_general(
        left, right, (((left_dim,), (right_dim,)), ((), ())), preferred_element_type=WIDE
    )


def causal(scores):
    key_pos = lax.broadcasted_iota(jnp.int32, scores.shape, 0)
    query_pos = lax.broadcasted_iota(jnp.int32, scores.shape, 1)
    return jnp.where(key_pos <= query_pos, scores, -1e30)


def turned(block):
    return jnp.transpose(block.astype(WIDE)).astype(LOW)


def sub_width(rows):
    for parts in (2, 3, 4, 6):
        if rows % (parts * 128) == 0:
            return rows // parts
    return rows


def normalize(values, axis):
    centred = values - jnp.mean(values, axis=axis, keepdims=True)
    scale = lax.rsqrt(jnp.mean(centred * centred, axis=axis, keepdims=True) + EPSILON)
    return centred * scale, scale


def norm_back(grad, normed, scale):
    return scale * (
        grad
        - jnp.mean(grad, axis=0, keepdims=True)
        - normed * jnp.mean(grad * normed, axis=0, keepdims=True)
    )


def whole(*dims):
    return pl.BlockSpec(dims, lambda *_: (0,) * len(dims), pipeline_mode=pl.Buffered(1))


def untouched():
    return pl.BlockSpec(memory_space=pl.ANY)


def head_block(rows, at):
    return pl.BlockSpec((1, 1, HEAD, rows), lambda i: (i, at, 0, 0))


def head_whole(parts, rows, at):
    return pl.BlockSpec((parts, 1, HEAD, rows), lambda i: (0, at, 0, 0))


def grant(mebibytes):
    return pltpu.CompilerParams(vmem_limit_bytes=mebibytes << 20)


def forward_kernel(q_ref, k_ref, v_ref, *refs):
    o_ref, log_ref, key_rows = refs[-4], refs[-3], refs[-1]
    step = pl.program_id(0)
    parts, rows = k_ref.shape[0], k_ref.shape[3]
    sub = sub_width(rows)

    @pl.when(step == 0)
    def _():
        for part in range(parts):
            key_rows[part] = turned(k_ref[part, 0])

    for first in range(0, rows, sub):
        cols = pl.ds(first, sub)
        q = q_ref[0, 0, :, cols]
        blocks = []
        if first:
            blocks.append((0, dot(key_rows[step, pl.ds(0, first)], q, 1, 0)))
        blocks.append((first, causal(dot(key_rows[step, cols], q, 1, 0))))
        top = functools.reduce(
            jnp.maximum, [jnp.max(scores, axis=0, keepdims=True) for _, scores in blocks]
        )
        total = jnp.zeros((1, sub), WIDE)
        mixed = jnp.zeros((HEAD, sub), WIDE)
        for offset, scores in blocks:
            raised = jnp.exp(scores - top)
            total = total + jnp.sum(raised, axis=0, keepdims=True)
            mixed = mixed + dot(
                v_ref[step, 0, :, pl.ds(offset, scores.shape[0])], raised.astype(LOW), 1, 0
            )

        def earlier(part, carried):
            top, total, mixed = carried
            scores = dot(key_rows[part], q, 1, 0)
            new_top = jnp.maximum(top, jnp.max(scores, axis=0, keepdims=True))
            shrink = jnp.exp(top - new_top)
            raised = jnp.exp(scores - new_top)
            return (
                new_top,
                shrink * total + jnp.sum(raised, axis=0, keepdims=True),
                shrink * mixed + dot(v_ref[part, 0], raised.astype(LOW), 1, 0),
            )

        top, total, mixed = lax.fori_loop(0, step, earlier, (top, total, mixed))
        o_ref[0, 0, :, cols] = (mixed / total).astype(LOW)
        log_ref[0, :, cols] = top + jnp.log(total)


def work(units, width):
    return pl.CostEstimate(
        flops=units * 2 * width**3, bytes_accessed=units * 2 * width**2, transcendentals=0
    )


def pair_cost(parts, rows, matmuls):
    pairs = parts * parts * rows * rows // 2
    return pl.CostEstimate(
        flops=2 * matmuls * pairs * HEAD * 4,
        bytes_accessed=parts * rows * HEAD * 16,
        transcendentals=pairs,
    )


def attend(packed, values, value_at, held, held_at, held_slots, passed):
    parts, _, _, rows = packed.shape
    shape = jax.ShapeDtypeStruct
    carried = [] if held is None else [held]
    first = 3 + len(carried)
    aliases = {first: 2} if held is None else {3: 0, first: 2}
    return pl.pallas_call(
        forward_kernel,
        grid=(parts,),
        in_specs=[
            head_block(rows, 0), head_whole(parts, rows, 1), head_whole(parts, rows, value_at),
        ]
        + [untouched() for _ in carried]
        + [untouched()],
        out_specs=[
            head_block(rows, held_at),
            pl.BlockSpec((1, 1, rows), lambda i: (i, 0, 0)),
            untouched(),
        ],
        out_shape=[
            shape((parts, held_slots, HEAD, rows), LOW),
            shape((parts, 1, rows), WIDE),
            shape(passed.shape, passed.dtype),
        ],
        scratch_shapes=[pltpu.VMEM((parts, rows, HEAD), LOW)],
        input_output_aliases=aliases,
        compiler_params=grant(40),
        cost_estimate=pair_cost(parts, rows, 2),
        name="attend",
    )(packed, packed, values, *carried, passed)


def backward_kernel(
    q_ref, k_ref, v_ref, do_ref, o_ref, log_ref, behind_ref, out_ref,
    key_rows, value_rows, query_rows, grad_rows, inner_ref, key_sum, value_sum,
):
    step = pl.program_id(0)
    parts, rows = k_ref.shape[0], k_ref.shape[3]
    sub = sub_width(rows)

    @pl.when(step == 0)
    def _():
        for part in range(parts):
            key_rows[part] = turned(k_ref[part, 0])
            value_rows[part] = turned(v_ref[part, 0])
        key_sum[...] = jnp.zeros_like(key_sum)
        value_sum[...] = jnp.zeros_like(value_sum)

    query_rows[...] = turned(q_ref[0, 0])
    grads = do_ref[0, 0].astype(WIDE)
    grad_rows[...] = jnp.transpose(grads).astype(LOW)
    inner_ref[...] = jnp.sum(grads * o_ref[0, 0].astype(WIDE), axis=0, keepdims=True)
    for first in range(0, rows, sub):
        cols = pl.ds(first, sub)
        q, do = q_ref[0, 0, :, cols], do_ref[0, 0, :, cols]
        log_total, inner = log_ref[0, :, cols], inner_ref[:, cols]
        q_rows, do_rows = query_rows[cols], grad_rows[cols]

        def pair(part, offset, size, masked):
            span = pl.ds(offset, size)
            scores = dot(key_rows[part, span], q, 1, 0)
            if masked:
                scores = causal(scores)
            probs = jnp.exp(scores - log_total)
            grad_probs = dot(value_rows[part, span], do, 1, 0)
            grad_scores = (probs * (grad_probs - inner)).astype(LOW)
            value_sum[part, span] += dot(probs.astype(LOW), do_rows, 1, 0)
            key_sum[part, span] += dot(grad_scores, q_rows, 1, 0)
            return dot(k_ref[part, 0, :, span], grad_scores, 1, 0)

        grad_q = pair(step, first, sub, True)
        if first:
            grad_q = grad_q + pair(step, 0, first, False)
        grad_q = lax.fori_loop(
            0, step, lambda part, carried: carried + pair(part, 0, rows, False), grad_q
        )
        out_ref[step, 0, :, cols] = (grad_q * HEAD ** (-0.5)).astype(LOW)

    @pl.when(step == parts - 1)
    def _():
        for part in range(parts):
            out_ref[part, 1] = jnp.transpose(key_sum[part]).astype(LOW)
            out_ref[part, 2] = jnp.transpose(value_sum[part]).astype(LOW)


def attend_backward(
    packed, values, value_at, grads, grads_at, attended, attended_at, log_totals, behind
):
    parts, _, _, rows = packed.shape
    return pl.pallas_call(
        backward_kernel,
        grid=(parts,),
        in_specs=[
            head_block(rows, 0), head_whole(parts, rows, 1), head_whole(parts, rows, value_at),
            head_block(rows, grads_at), head_block(rows, attended_at),
            pl.BlockSpec((1, 1, rows), lambda i: (i, 0, 0)),
            untouched(),
        ],
        out_specs=pl.BlockSpec((parts, 3, HEAD, rows), lambda i: (0, 0, 0, 0)),
        out_shape=jax.ShapeDtypeStruct((parts, 3, HEAD, rows), LOW),
        scratch_shapes=[
            pltpu.VMEM((parts, rows, HEAD), LOW),
            pltpu.VMEM((parts, rows, HEAD), LOW),
            pltpu.VMEM((rows, HEAD), LOW),
            pltpu.VMEM((rows, HEAD), LOW),
            pltpu.VMEM((1, rows), WIDE),
            pltpu.VMEM((parts, rows, HEAD), WIDE),
            pltpu.VMEM((parts, rows, HEAD), WIDE),
        ],
        compiler_params=grant(40),
        cost_estimate=pair_cost(parts, rows, 5),
        name="attend_backward",
    )(packed, packed, values, grads, attended, log_totals, behind)


SLOPE = 0.7978845608028654


def project_kernel(
    order_ref, tokens_ref, first_ref, near_a, far_a, near_b, far_b, behind_ref, *refs,
):
    *messages, low_ref, turned_ref, query_ref, key_ref, value_ref, vec_ref = refs
    owners = order_ref.shape[1]
    part, fresh_part = query_ref.shape[0] // owners, value_ref.shape[0] // owners
    half = near_a.shape[1]
    groups = messages[0].shape[0]
    fresh_width = value_ref.shape[0]

    vectors = jnp.zeros((16, near_b.shape[2]), WIDE)
    for at in range(near_b.shape[0]):
        vectors = vectors + near_b[at, half - 16 :].astype(WIDE)
        vectors = vectors + far_b[at, half - 16 :].astype(WIDE)
    inputs = tokens_ref[...].astype(WIDE)
    normed, _ = normalize(inputs, 1)
    low_ref[...] = (normed * vectors[0:1] + vectors[1:2]).astype(LOW)
    turned_ref[...] = jnp.transpose(inputs).astype(LOW)
    blank = jnp.zeros((128 - vectors.shape[0], vectors.shape[1]), WIDE)
    vec_ref[...] = jnp.transpose(jnp.concatenate([vectors, blank], axis=0))
    for owner in range(owners):
        same_core = order_ref[0, owner] == 0
        weights = jnp.concatenate(
            [
                jnp.where(same_core, near_a[order_ref[1, owner]], far_a[order_ref[1, owner]]),
                jnp.where(same_core, near_b[order_ref[2, owner]], far_b[order_ref[2, owner]]),
            ],
            axis=0,
        )
        first = 0
        for ref, count in ((query_ref, part), (key_ref, part), (value_ref, fresh_part)):
            ref[owner * count : (owner + 1) * count] = weights[first : first + count]
            first += count
    low_one = low_ref[...]
    for which, ref in enumerate((query_ref, key_ref, value_ref)):
        products = dot(ref[...], low_one, 1, 1).astype(LOW)
        if which == 0:
            products = products * jnp.asarray(HEAD ** (-0.5), LOW)
        for slot, message in enumerate(messages):
            for group in range(groups):
                feature = (slot * groups + group) * HEAD
                if which < message.shape[1] and feature < products.shape[0]:
                    message[group, which] = products[feature : feature + HEAD]
    for slot, message in enumerate(messages):
        for group in range(groups):
            first = (slot * groups + group) * HEAD - fresh_width
            if message.shape[1] == 3 and first >= 0:
                start = first // 128 * 128
                block = turned(first_ref[:, start : start + 128])
                message[group, 2] = block[first - start : first - start + HEAD]


def project(tokens, first_values, halves, order, behind, widths, part, fresh_part, groups):
    rows, width = tokens.shape
    owners = order.shape[1]
    held = [tokens, first_values, *halves[0], *halves[1]]
    shape = jax.ShapeDtypeStruct
    outs = [shape((groups, count, HEAD, rows), LOW) for count in widths] + [
        shape((rows, width), LOW), shape((width, rows), LOW), shape((width, width), LOW),
        shape((width, width), LOW), shape((fresh_part * owners, width), LOW),
        shape((width, 128), WIDE),
    ]
    return pl.pallas_call(
        project_kernel,
        in_specs=[pl.BlockSpec(memory_space=pltpu.SMEM)]
        + [pl.BlockSpec(memory_space=pltpu.VMEM) for _ in held]
        + [untouched()],
        out_specs=[pl.BlockSpec(memory_space=pltpu.VMEM) for _ in outs],
        out_shape=outs,
        compiler_params=grant(48),
        cost_estimate=work(8, width),
        name="project",
    )(order, *held, behind)


def project_plain(tokens, first_values, halves, order, behind, widths, part, fresh_part, groups):
    rows, width = tokens.shape
    owners = order.shape[1]
    blocks = []
    for owner in range(owners):
        pieces = []
        for at, (near, far) in enumerate(halves):
            index = order[1 + at, owner]
            pieces.append(jnp.where(order[0, owner] == 0, pick(near, index), pick(far, index)))
        blocks.append(jnp.concatenate(pieces, axis=0))
    blocks = jnp.stack(blocks)
    query_t = blocks[:, :part].reshape(-1, width)
    key_t = blocks[:, part : 2 * part].reshape(-1, width)
    value_t = blocks[:, 2 * part : 2 * part + fresh_part].reshape(-1, width)
    vectors = jnp.sum(blocks[:, -16:].astype(WIDE), axis=0)
    normed, _ = normalize(tokens.astype(WIDE), 1)
    low_one = (normed * vectors[0:1] + vectors[1:2]).astype(LOW)
    queries = dot(query_t, low_one, 1, 1).astype(LOW) * jnp.asarray(HEAD ** (-0.5), LOW)
    keys = dot(key_t, low_one, 1, 1).astype(LOW)
    values = jnp.concatenate([dot(value_t, low_one, 1, 1).astype(LOW), first_values.T], axis=0)
    stacked = [array.reshape(-1, groups, HEAD, rows) for array in (queries, keys, values)]
    messages = [
        jnp.stack([array[slot] for array in stacked[:count]], axis=1)
        for slot, count in enumerate(widths)
    ]
    table = jnp.pad(vectors.T, ((0, 0), (0, 128 - vectors.shape[0])))
    return (*messages, low_one, tokens.T, query_t, key_t, value_t, table)


def middle_kernel(
    attn_zero, attn_rest, tokens_ref, cot_ref, vec_ref, out_ref, fc_ref, proj_ref,
    output_ref, pack_ref, grad_zero, grad_rest, grad_res_ref, vec_back,
    attn_ref, cot_t, low_ref, normed_ref, scale_ref, sum_ref, back_ref,
):
    step = pl.program_id(0)
    owners = pack_ref.shape[0]
    block, width = fc_ref.shape
    part = width // owners
    fc_part = pl.num_programs(0) * block // owners
    share = block // fc_part
    groups = attn_zero.shape[0]

    def spots(zero, rest):
        for slot in range(1 + rest.shape[1]):
            for group in range(groups):
                ref = zero.at[group, 0] if slot == 0 else rest.at[group, slot - 1]
                yield (slot * groups + group) * HEAD, ref

    @pl.when(step == 0)
    def _():
        for first, ref in spots(attn_zero, attn_rest):
            attn_ref[first : first + HEAD] = ref[...]
        cot_t[...] = turned(cot_ref[...])
        residual = tokens_ref[...].astype(WIDE) + dot(out_ref[...], attn_ref[...], 1, 0)
        normed, scale = normalize(residual, 0)
        low_ref[...] = (normed * vec_ref[:, 2:3] + vec_ref[:, 3:4]).astype(LOW)
        normed_ref[...] = normed
        scale_ref[...] = scale
        sum_ref[...] = residual
        back_ref[...] = jnp.zeros_like(back_ref)

    low = low_ref[...]
    hidden = dot(fc_ref[...], low, 1, 0)
    bent = jnp.tanh(SLOPE * (hidden + 0.044715 * hidden * hidden * hidden))
    half = 0.5 * (1.0 + bent)
    active = (hidden * half).astype(LOW)
    slope = half + hidden * (0.5 * (1.0 - bent * bent)) * (
        SLOPE * (1.0 + (3 * 0.044715) * hidden * hidden)
    )
    sum_ref[...] += dot(proj_ref[...], active, 1, 0)
    cot = cot_t[...]
    grad_hidden = (dot(proj_ref[...], cot, 0, 0) * slope).astype(LOW)
    grad_proj = dot(cot, active, 1, 1).astype(LOW)
    grad_fc = dot(grad_hidden, low, 1, 1).astype(LOW)
    for owner in range(owners):
        pack_ref[owner, pl.ds(pl.multiple_of(fc_part + step * part, 16), part)] = grad_proj[
            owner * part : (owner + 1) * part
        ]
    for at in range(share):
        pack_ref[step * share + at, pl.ds(0, fc_part)] = grad_fc[at * fc_part : (at + 1) * fc_part]
    back_ref[...] += dot(fc_ref[...], grad_hidden, 0, 0)

    @pl.when(step == pl.num_programs(0) - 1)
    def _():
        output_ref[...] = jnp.transpose(sum_ref[...]).astype(LOW)
        grad, normed = back_ref[...], normed_ref[...]
        lane = lax.broadcasted_iota(jnp.int32, vec_back.shape, 1)
        grad_gain = jnp.sum(grad * normed, axis=1, keepdims=True)
        grad_bias = jnp.sum(grad, axis=1, keepdims=True)
        vec_back[...] = jnp.where(lane == 2, grad_gain, jnp.where(lane == 3, grad_bias, 0.0))
        grad_res = cot_t[...].astype(WIDE) + norm_back(
            grad * vec_ref[:, 2:3], normed, scale_ref[...]
        )
        grad_res_ref[...] = grad_res
        mixed = grad_res.astype(LOW)
        grad_attn = dot(out_ref[...], mixed, 0, 0).astype(LOW)
        for first, ref in spots(grad_zero, grad_rest):
            ref[...] = grad_attn[first : first + HEAD]
        grad_out = dot(mixed, attn_ref[...], 1, 1).astype(LOW)
        for owner in range(owners):
            pack_ref[owner, pl.ds(2 * fc_part, part)] = grad_out[owner * part : (owner + 1) * part]


def middle(attn_zero, attn_rest, tokens_t, cotangent, vectors, out_t, fc_t, proj_t, owners):
    width, rows = tokens_t.shape
    hidden = fc_t.shape[0]
    block = width
    shape = jax.ShapeDtypeStruct
    down = pl.BlockSpec((block, width), lambda j: (j, 0))
    along = pl.BlockSpec((width, block), lambda j: (0, j))
    held = (width, rows)
    pack = (owners, (2 * hidden + width) // owners, width)
    return pl.pallas_call(
        middle_kernel,
        grid=(hidden // block,),
        in_specs=[
            whole(*attn_zero.shape), whole(*attn_rest.shape), whole(*held), whole(rows, width),
            whole(width, 128), whole(width, width), down, along,
        ],
        out_specs=[
            whole(rows, width), whole(*pack), whole(*attn_zero.shape), whole(*attn_rest.shape),
            whole(*held), whole(width, 128),
        ],
        out_shape=[
            shape((rows, width), LOW), shape(pack, LOW), shape(attn_zero.shape, LOW),
            shape(attn_rest.shape, LOW), shape(held, WIDE), shape((width, 128), WIDE),
        ],
        scratch_shapes=[
            pltpu.VMEM(held, LOW), pltpu.VMEM(held, LOW), pltpu.VMEM(held, LOW),
            pltpu.VMEM(held, WIDE), pltpu.VMEM((1, rows), WIDE), pltpu.VMEM(held, WIDE),
            pltpu.VMEM(held, WIDE),
        ],
        compiler_params=grant(60),
        cost_estimate=work(40, width),
        name="middle",
    )(attn_zero, attn_rest, tokens_t, cotangent, vectors, out_t, fc_t, proj_t)


def joined(zero, rest):
    both = jnp.concatenate([zero, rest], axis=1).swapaxes(0, 1)
    return both.reshape(-1, both.shape[-1])


def middle_plain(attn_zero, attn_rest, tokens_t, cotangent, vectors, out_t, fc_t, proj_t, owners):
    width = tokens_t.shape[0]
    attn = joined(attn_zero, attn_rest)
    gain, bias = vectors[:, 2:3], vectors[:, 3:4]
    cot_t = cotangent.T
    residual = tokens_t.astype(WIDE) + dot(out_t, attn, 1, 0)
    normed, scale = normalize(residual, 0)
    low = (normed * gain + bias).astype(LOW)
    hidden = dot(fc_t, low, 1, 0)
    active, pull = jax.vjp(functools.partial(jax.nn.gelu, approximate=True), hidden)
    low_active = active.astype(LOW)
    output = (residual + dot(proj_t, low_active, 1, 0)).astype(LOW).T
    (grad_hidden,) = pull(dot(proj_t, cot_t, 0, 0))
    grad_hidden = grad_hidden.astype(LOW)
    grad_proj = dot(cot_t, low_active, 1, 1).astype(LOW)
    grad_fc = dot(grad_hidden, low, 1, 1).astype(LOW)
    grad = dot(fc_t, grad_hidden, 0, 0)
    grad_gain = jnp.sum(grad * normed, axis=1, keepdims=True)
    grad_bias = jnp.sum(grad, axis=1, keepdims=True)
    grad_res = cot_t.astype(WIDE) + norm_back(grad * gain, normed, scale)
    mixed = grad_res.astype(LOW)
    part = width // owners
    grad_proj = grad_proj.reshape(owners, part, -1, width).transpose(0, 2, 1, 3)
    pack = jnp.concatenate(
        [
            grad_fc.reshape(owners, -1, width),
            grad_proj.reshape(owners, -1, width),
            dot(mixed, attn, 1, 1).astype(LOW).reshape(owners, part, width),
        ],
        axis=1,
    )
    grad_attn = dot(out_t, mixed, 0, 0).astype(LOW)
    grad_attn = grad_attn.reshape(-1, attn_zero.shape[0], HEAD, attn.shape[1]).swapaxes(0, 1)
    table = jnp.concatenate([jnp.zeros((width, 2), WIDE), grad_gain, grad_bias], axis=1)
    table = jnp.pad(table, ((0, 0), (0, 124)))
    return output, pack, grad_attn[:, :1], grad_attn[:, 1:], grad_res, table


def weights_kernel(*refs):
    core_ref = refs[0]
    *homes, low_ref, query_ref, key_ref, value_ref, tokens_ref, vec_ref, _ = refs[1:-5]
    pack_ref, grad_ref, q_ref, k_ref, v_ref = refs[-5:]
    owners = 2 * pack_ref.shape[1]

    def store(owner, first, block):
        other = (core_ref[0] + owner) & 1
        pack_ref[other, owner // 2, first : first + block.shape[0]] = block

    groups = homes[0].shape[0]
    for slot, home in enumerate(homes):
        for group in range(groups):
            first = (slot * groups + group) * HEAD
            for which, back in enumerate((q_ref, k_ref, v_ref)):
                if first < back.shape[0]:
                    back[first : first + HEAD] = home[group, which]
    low = low_ref[...]
    first = 0
    for back in (q_ref, k_ref, v_ref):
        grads = dot(back[...], low, 1, 0).astype(LOW)
        rows = grads.shape[0] // owners
        for owner in range(owners):
            store(owner, first, grads[owner * rows : (owner + 1) * rows])
        first += rows
    grad = (
        dot(query_ref[...], q_ref[...], 0, 0)
        + dot(key_ref[...], k_ref[...], 0, 0)
        + dot(value_ref[...], v_ref[...], 0, 0)
    )
    grad_ref[...] = grad
    normed, _ = normalize(tokens_ref[...].astype(WIDE), 0)
    lane = lax.broadcasted_iota(jnp.int32, vec_ref.shape, 1)
    grad_gain = jnp.sum(grad * normed, axis=1, keepdims=True)
    grad_bias = jnp.sum(grad, axis=1, keepdims=True)
    table = jnp.where(lane == 0, grad_gain, jnp.where(lane == 1, grad_bias, vec_ref[...]))
    table = jnp.transpose(table)[:16].astype(LOW)
    for owner in range(owners):
        store(owner, first, table)


def weights_back(homes, low_one, query_t, key_t, value_t, tokens_t, vec_back, behind, owners):
    width, rows = tokens_t.shape
    fresh_width = value_t.shape[0]
    pack_rows = (2 * width + fresh_width) // owners + 16
    held = [*homes, low_one, query_t, key_t, value_t, tokens_t, vec_back]
    return pl.pallas_call(
        weights_kernel,
        out_shape=[
            jax.ShapeDtypeStruct((2, owners // 2, pack_rows, width), LOW),
            jax.ShapeDtypeStruct((width, rows), WIDE),
        ],
        scratch_shapes=[
            pltpu.VMEM((width, rows), LOW), pltpu.VMEM((width, rows), LOW),
            pltpu.VMEM((fresh_width, rows), LOW),
        ],
        in_specs=[pl.BlockSpec(memory_space=pltpu.SMEM)]
        + [pl.BlockSpec(memory_space=pltpu.VMEM) for _ in held]
        + [untouched()],
        compiler_params=grant(56),
        cost_estimate=work(12, width),
        name="weights_back",
    )((lax.axis_index("dp") & 1).reshape(1), *held, behind)


def weights_plain(homes, low_one, query_t, key_t, value_t, tokens_t, vec_back, behind, owners):
    width, rows = tokens_t.shape
    back_q, back_k = (
        jnp.stack([home[:, which] for home in homes]).reshape(width, rows) for which in range(2)
    )
    back_v = jnp.stack([home[:, 2] for home in homes])
    back_v = back_v.reshape(-1, rows)[: value_t.shape[0]]
    grad = dot(query_t, back_q, 0, 0) + dot(key_t, back_k, 0, 0) + dot(value_t, back_v, 0, 0)
    normed, _ = normalize(tokens_t.astype(WIDE), 0)
    table = jnp.concatenate(
        [
            jnp.sum(grad * normed, axis=1, keepdims=True), jnp.sum(grad, axis=1, keepdims=True),
            vec_back[:, 2:16],
        ],
        axis=1,
    ).T
    pieces = [
        dot(back, low_one, 1, 0).reshape(owners, -1, width) for back in (back_q, back_k, back_v)
    ]
    count = sum(piece.shape[1] for piece in pieces)
    padded = -(-count // 16) * 16
    padded = -(-(padded + 16) // 32) * 32 - 16
    pieces.append(jnp.zeros((owners, padded - count, width), WIDE))
    pieces.append(jnp.broadcast_to(table, (owners,) + table.shape))
    pack = jnp.concatenate(pieces, axis=1).astype(LOW)
    pack = pack.reshape((-1, 2) + pack.shape[1:])
    mine = lax.axis_index("dp") & 1
    return jnp.stack([pick(pack, mine, 1), pick(pack, 1 - mine, 1)]), grad


def tokens_kernel(grad_ref, tokens_ref, res_ref, gain_ref, out_ref):
    normed, scale = normalize(tokens_ref[...].astype(WIDE), 0)
    grad = res_ref[...] + norm_back(grad_ref[...] * gain_ref[:, 0:1], normed, scale)
    out_ref[...] = jnp.transpose(grad).astype(LOW)


def tokens_back(grad_one, tokens_t, grad_residual, vectors):
    width, rows = grad_one.shape
    return pl.pallas_call(
        tokens_kernel,
        out_shape=jax.ShapeDtypeStruct((rows, width), LOW),
        compiler_params=grant(40),
        cost_estimate=work(4, width),
        name="tokens_back",
    )(grad_one, tokens_t, grad_residual, vectors)


def gate_kernel(*refs):
    pass


def gate(array, behind):
    return pl.pallas_call(
        gate_kernel,
        in_specs=[untouched(), untouched()],
        out_specs=untouched(),
        out_shape=jax.ShapeDtypeStruct(array.shape, array.dtype),
        input_output_aliases={0: 0},
        name="gate",
    )(array, behind)


def pick(stacked, index, axis=0):
    return lax.dynamic_index_in_dim(stacked, index, axis, keepdims=False)


def exchange(block, axis, bit):
    count = lax.axis_size(axis)
    return lax.ppermute(block, axis, [(i, i ^ (1 << bit)) for i in range(count)])


def swap(message):
    return lax.all_to_all(message, "seq", split_axis=0, concat_axis=0, tiled=True)


def gather_halves(shard, behind):
    bits = lax.axis_size("dp").bit_length() - 1
    half = shard.shape[0] // 2
    halves = []
    for block, order in (
        (shard[:half], range(1, bits)),
        (shard[half:], range(bits - 1, 0, -1)),
    ):
        held = block[None]
        for bit in order:
            held = jnp.concatenate([held, exchange(held, "dp", bit)])
        halves.append(held)
    halves[1] = gate(halves[1], behind)
    return [(held, exchange(held, "dp", 0)) for held in halves]


def gathered_order():
    count, here = lax.axis_size("dp"), lax.axis_index("dp")
    bits = count.bit_length() - 1
    offset = jnp.arange(count, dtype=jnp.int32) ^ here
    places = [0, 0]
    for at in range(bits - 1):
        bit = (offset >> (at + 1)) & 1
        places[0] = places[0] + (bit << at)
        places[1] = places[1] + (bit << (bits - 2 - at))
    return jnp.stack([offset & 1, *places])


def scatter_blocks(keep, send, others):
    count, here = lax.axis_size("dp"), lax.axis_index("dp")
    bits = count.bit_length() - 1
    rows, width = keep.shape[1:]

    def halve(held, bit, axis, other):
        mine = (here >> bit) & 1
        sent = pick(held, 1 - mine, axis).astype(LOW)
        sent = exchange(sent if other is None else gate(sent, other), "dp", bit)
        return pick(held, mine, axis).astype(WIDE) + sent.astype(WIDE)

    held = keep.astype(WIDE) + exchange(gate(send, next(others)), "dp", 0).astype(WIDE)
    held = held.reshape((2,) * (bits - 1) + (rows, width))
    halves = [held[..., : rows // 2, :], held[..., rows // 2 :, :]]
    orders = [list(range(1, bits)), list(range(bits - 1, 0, -1))]
    left = [list(range(bits - 1, 0, -1)) for _ in orders]
    for at in range(bits - 1):
        other = next(others, None)
        for which, order in enumerate(orders):
            axis = left[which].index(order[at])
            halves[which] = halve(halves[which], order[at], axis, other)
            left[which].remove(order[at])
    return jnp.concatenate(halves)


def seq_halves(block):
    mine = lax.axis_index("seq") & 1
    halves = block.reshape((2, -1) + block.shape[1:])
    sent = exchange(pick(halves, 1 - mine).astype(LOW), "seq", 0)
    return (pick(halves, mine).astype(WIDE) + sent.astype(WIDE)).astype(LOW)


def seq_pairs(held):
    total = held.astype(WIDE)
    for bit in range(1, lax.axis_size("seq").bit_length() - 1):
        total = total + exchange(total.astype(LOW), "seq", bit).astype(WIDE)
    return total.astype(LOW)


def seq_whole(held):
    mine = lax.axis_index("seq") & 1
    other = exchange(held, "seq", 0)
    first, second = jnp.where(mine == 0, held, other), jnp.where(mine == 0, other, held)
    return jnp.concatenate([first, second]).astype(WIDE)


def gather(shard):
    return lax.all_gather(shard, "dp", axis=0, tiled=True)


def shards(
    tokens, first_values, cotangent, ln1_gain, ln1_bias, w_query, w_key, w_value, w_out,
    ln2_gain, ln2_bias, w_fc, w_proj,
):
    owners = lax.axis_size("dp")
    groups = lax.axis_size("seq")
    rows, width = tokens.shape
    local = HEADS // groups
    part, fresh_part = w_query.shape[1], w_value.shape[1]
    fresh_width = fresh_part * owners

    weight_rows = -(-(2 * part + fresh_part) // 16) * 16
    pack_rows = -(-(weight_rows + 16) // 32) * 32
    aligned = fresh_part % 16 == 0 and pack_rows == weight_rows + 16
    here = lax.axis_index("dp")

    last = local - 1
    first = (last * groups * HEAD - fresh_width) // HEAD
    early = first_values[:, first * HEAD :].T.reshape(groups, 1, HEAD, rows)
    early = swap(early)
    vectors = jnp.stack([ln1_gain, ln1_bias, ln2_gain, ln2_bias])
    vectors = lax.dynamic_update_slice(jnp.zeros((16, width), LOW), vectors, (0, here * part))
    first_pack = jnp.concatenate([w_query.T, w_key.T, w_value.T], axis=0)
    first_pack = jnp.pad(first_pack, ((0, pack_rows - 16 - first_pack.shape[0]), (0, 0)))
    halves = gather_halves(jnp.concatenate([first_pack, vectors], axis=0), early)
    out_t, fc_t, proj_t = (
        gather(shard.T) for shard in (w_out, w_fc, w_proj)
    )

    widths = [3] * last + [2]
    *messages, low_one, tokens_t, query_t, key_t, value_t, vectors = (
        project if aligned else project_plain
    )(
        tokens, first_values, halves, gathered_order(), early, widths, part, fresh_part, groups
    )

    arrived, log_totals, held = {}, {}, None
    for slot in reversed(range(local)):
        arrived[slot] = swap(messages[slot])
        if slot < last:
            done = slot + 1
            values, at = (early, 0) if done == last else (arrived[done], 2)
            wait = max(slot - 1, 0)
            passed = messages[wait] if slot else log_totals[last]
            held, log_totals[done], passed = attend(
                arrived[done], values, at, held, done - 1, last, passed
            )
            if slot:
                messages[wait] = passed
            else:
                log_totals[last] = passed
    rest = held
    zero, log_totals[0], _ = attend(arrived[0], arrived[0], 2, None, 0, 1, log_totals[1])

    output, grad_pack, grad_zero, grad_rest, grad_residual, vec_back = (
        middle if aligned else middle_plain
    )(swap(zero), swap(rest), tokens_t, cotangent, vectors, out_t, fc_t, proj_t, owners)
    grad_pack = lax.psum_scatter(
        grad_pack.reshape(-1, width), "dp", scatter_dimension=0, tiled=True
    )
    grad_pack = seq_halves(grad_pack)

    grad_zero = swap(grad_zero)
    grad_rest = swap(grad_rest)
    homes = []
    for slot in range(local):
        values, at = (early, 0) if slot == last else (arrived[slot], 2)
        grads, grads_at = (grad_rest, slot - 1) if slot else (grad_zero, 0)
        attended, attended_at = (rest, slot - 1) if slot else (zero, 0)
        behind = homes[slot - 2] if slot > 1 else log_totals[slot]
        grads = attend_backward(
            arrived[slot], values, at, grads, grads_at, attended, attended_at, log_totals[slot],
            behind,
        )
        homes.append(swap(grads))
    last_pack, grad_one = (weights_back if aligned else weights_plain)(
        homes, low_one, query_t, key_t, value_t, tokens_t, vec_back, grad_pack, owners
    )
    third = -(-grad_pack.shape[0] // 48) * 16
    grad_pack = [
        seq_pairs(grad_pack[first : first + third])
        for first in range(0, grad_pack.shape[0], third)
    ]
    last_pack = seq_halves(scatter_blocks(*last_pack, iter(grad_pack)))
    last_pack = seq_whole(seq_pairs(last_pack))
    grad_pack = seq_whole(jnp.concatenate(grad_pack))
    grad_tokens = tokens_back(grad_one, tokens_t, grad_residual, vectors)
    grad_first = jnp.concatenate([home[:, 2] for home in homes]).reshape(-1, rows)
    grad_first = grad_first[fresh_width:].T

    vectors = last_pack[pack_rows - 16 : pack_rows - 12].reshape(4, owners, part)
    vectors = pick(vectors, here, 1)
    fc_part = w_fc.shape[1]
    grad_proj = grad_pack[fc_part : 2 * fc_part].reshape(-1, part, width).transpose(0, 2, 1)
    return (
        output,
        grad_tokens,
        grad_first,
        vectors[0],
        vectors[1],
        last_pack[:part].T,
        last_pack[part : 2 * part].T,
        last_pack[2 * part : 2 * part + fresh_part].T,
        grad_pack[2 * fc_part :].T,
        vectors[2],
        vectors[3],
        grad_pack[:fc_part].T,
        grad_proj.reshape(-1, part),
    )


def solution(mesh):
    row = P(("dp", "seq"), None)
    vector, matrix = P("dp"), P(None, "dp")
    weights = (vector, vector, matrix, matrix, matrix, matrix, vector, vector, matrix, matrix)
    return jax.shard_map(
        shards,
        mesh=mesh,
        in_specs=(row, row, row) + weights,
        out_specs=(row, row, row) + weights,
        check_vma=False,
    )
```

```python
import functools
import math

import jax
import jax.numpy as jnp
from jax import lax
from jax.experimental import pallas as pl
from jax.experimental.pallas import tpu as pltpu
from jax.sharding import PartitionSpec as P

HEADS = 12
HEAD = 64
EPSILON = 1e-05
LOW = jnp.bfloat16
WIDE = jnp.float32


def dot(left, right, left_dim, right_dim):
    return lax.dot_general(
        left, right, (((left_dim,), (right_dim,)), ((), ())), preferred_element_type=WIDE
    )


def causal(scores):
    key_pos = lax.broadcasted_iota(jnp.int32, scores.shape, 0)
    query_pos = lax.broadcasted_iota(jnp.int32, scores.shape, 1)
    return jnp.where(key_pos <= query_pos, scores, -1e30)


def turned(block):
    return jnp.transpose(block.astype(WIDE)).astype(LOW)


def sub_width(rows):
    for parts in (2, 3, 4, 6):
        if rows % (parts * 128) == 0:
            return rows // parts
    return rows


def normalize(values, axis):
    centred = values - jnp.mean(values, axis=axis, keepdims=True)
    scale = lax.rsqrt(jnp.mean(centred * centred, axis=axis, keepdims=True) + EPSILON)
    return centred * scale, scale


def norm_back(grad, normed, scale):
    return scale * (
        grad
        - jnp.mean(grad, axis=0, keepdims=True)
        - normed * jnp.mean(grad * normed, axis=0, keepdims=True)
    )


def whole(*dims):
    return pl.BlockSpec(dims, lambda *_: (0,) * len(dims), pipeline_mode=pl.Buffered(1))


def untouched():
    return pl.BlockSpec(memory_space=pl.ANY)


def head_block(rows, at):
    return pl.BlockSpec((1, 1, HEAD, rows), lambda i: (i, at, 0, 0))


def head_whole(parts, rows, at):
    return pl.BlockSpec((parts, 1, HEAD, rows), lambda i: (0, at, 0, 0))


def grant(mebibytes):
    return pltpu.CompilerParams(vmem_limit_bytes=mebibytes << 20)


def forward_kernel(q_ref, k_ref, v_ref, *refs):
    o_ref, log_ref, key_rows = refs[-3:]
    step = pl.program_id(0)
    parts, rows = k_ref.shape[0], k_ref.shape[3]
    sub = sub_width(rows)

    @pl.when(step == 0)
    def _():
        for part in range(parts):
            key_rows[part] = turned(k_ref[part, 0])

    for first in range(0, rows, sub):
        cols = pl.ds(first, sub)
        q = q_ref[0, 0, :, cols]
        blocks = []
        if first:
            blocks.append((0, dot(key_rows[step, pl.ds(0, first)], q, 1, 0)))
        blocks.append((first, causal(dot(key_rows[step, cols], q, 1, 0))))
        top = functools.reduce(
            jnp.maximum, [jnp.max(scores, axis=0, keepdims=True) for _, scores in blocks]
        )
        total = jnp.zeros((1, sub), WIDE)
        mixed = jnp.zeros((HEAD, sub), WIDE)
        for offset, scores in blocks:
            raised = jnp.exp(scores - top)
            total = total + jnp.sum(raised, axis=0, keepdims=True)
            mixed = mixed + dot(
                v_ref[step, 0, :, pl.ds(offset, scores.shape[0])], raised.astype(LOW), 1, 0
            )

        def earlier(part, carried):
            top, total, mixed = carried
            scores = dot(key_rows[part], q, 1, 0)
            new_top = jnp.maximum(top, jnp.max(scores, axis=0, keepdims=True))
            shrink = jnp.exp(top - new_top)
            raised = jnp.exp(scores - new_top)
            return (
                new_top,
                shrink * total + jnp.sum(raised, axis=0, keepdims=True),
                shrink * mixed + dot(v_ref[part, 0], raised.astype(LOW), 1, 0),
            )

        top, total, mixed = lax.fori_loop(0, step, earlier, (top, total, mixed))
        o_ref[0, 0, :, cols] = (mixed / total).astype(LOW)
        log_ref[0, :, cols] = top + jnp.log(total)


def work(units, width):
    return pl.CostEstimate(
        flops=units * 2 * width**3, bytes_accessed=units * 2 * width**2, transcendentals=0
    )


def pair_cost(parts, rows, matmuls):
    pairs = parts * parts * rows * rows // 2
    return pl.CostEstimate(
        flops=2 * matmuls * pairs * HEAD * 4,
        bytes_accessed=parts * rows * HEAD * 16,
        transcendentals=pairs,
    )


def attend(packed, query_at, values, value_at, held, held_at, held_slots):
    parts, _, _, rows = packed.shape
    shape = jax.ShapeDtypeStruct
    carried = [] if held is None else [held]
    return pl.pallas_call(
        forward_kernel,
        grid=(parts,),
        in_specs=[
            head_block(rows, query_at), head_whole(parts, rows, query_at + 1),
            head_whole(parts, rows, value_at),
        ]
        + [untouched() for _ in carried],
        out_specs=[
            head_block(rows, held_at), pl.BlockSpec((1, 1, rows), lambda i: (i, 0, 0)),
        ],
        out_shape=[
            shape((parts, held_slots, HEAD, rows), LOW), shape((parts, 1, rows), WIDE),
        ],
        scratch_shapes=[pltpu.VMEM((parts, rows, HEAD), LOW)],
        input_output_aliases={3: 0} if carried else {},
        compiler_params=grant(40),
        cost_estimate=pair_cost(parts, rows, 2),
        name="attend",
    )(packed, packed, values, *carried)


def backward_kernel(
    q_ref, k_ref, v_ref, do_ref, o_ref, log_ref, behind_ref, out_ref,
    key_rows, value_rows, query_rows, grad_rows, inner_ref, key_sum, value_sum,
):
    step = pl.program_id(0)
    parts, rows = k_ref.shape[0], k_ref.shape[3]
    sub = sub_width(rows)

    @pl.when(step == 0)
    def _():
        for part in range(parts):
            key_rows[part] = turned(k_ref[part, 0])
            value_rows[part] = turned(v_ref[part, 0])
        key_sum[...] = jnp.zeros_like(key_sum)
        value_sum[...] = jnp.zeros_like(value_sum)

    query_rows[...] = turned(q_ref[0, 0])
    grads = do_ref[0, 0].astype(WIDE)
    grad_rows[...] = jnp.transpose(grads).astype(LOW)
    inner_ref[...] = jnp.sum(grads * o_ref[0, 0].astype(WIDE), axis=0, keepdims=True)
    for first in range(0, rows, sub):
        cols = pl.ds(first, sub)
        q, do = q_ref[0, 0, :, cols], do_ref[0, 0, :, cols]
        log_total, inner = log_ref[0, :, cols], inner_ref[:, cols]
        q_rows, do_rows = query_rows[cols], grad_rows[cols]

        def pair(part, offset, size, masked):
            span = pl.ds(offset, size)
            scores = dot(key_rows[part, span], q, 1, 0)
            if masked:
                scores = causal(scores)
            probs = jnp.exp(scores - log_total)
            grad_probs = dot(value_rows[part, span], do, 1, 0)
            grad_scores = (probs * (grad_probs - inner)).astype(LOW)
            value_sum[part, span] += dot(probs.astype(LOW), do_rows, 1, 0)
            key_sum[part, span] += dot(grad_scores, q_rows, 1, 0)
            return dot(k_ref[part, 0, :, span], grad_scores, 1, 0)

        grad_q = pair(step, first, sub, True)
        if first:
            grad_q = grad_q + pair(step, 0, first, False)
        grad_q = lax.fori_loop(
            0, step, lambda part, carried: carried + pair(part, 0, rows, False), grad_q
        )
        out_ref[step, 0, :, cols] = (grad_q * HEAD ** (-0.5)).astype(LOW)

    @pl.when(step == parts - 1)
    def _():
        for part in range(parts):
            out_ref[part, 1] = jnp.transpose(key_sum[part]).astype(LOW)
            out_ref[part, 2] = jnp.transpose(value_sum[part]).astype(LOW)


def attend_backward(
    packed, query_at, values, value_at, grads, grads_at, attended, attended_at, log_totals, behind
):
    parts, _, _, rows = packed.shape
    return pl.pallas_call(
        backward_kernel,
        grid=(parts,),
        in_specs=[
            head_block(rows, query_at), head_whole(parts, rows, query_at + 1),
            head_whole(parts, rows, value_at), head_block(rows, grads_at), head_block(rows, attended_at),
            pl.BlockSpec((1, 1, rows), lambda i: (i, 0, 0)),
            untouched(),
        ],
        out_specs=pl.BlockSpec((parts, 3, HEAD, rows), lambda i: (0, 0, 0, 0)),
        out_shape=jax.ShapeDtypeStruct((parts, 3, HEAD, rows), LOW),
        scratch_shapes=[
            pltpu.VMEM((parts, rows, HEAD), LOW),
            pltpu.VMEM((parts, rows, HEAD), LOW),
            pltpu.VMEM((rows, HEAD), LOW),
            pltpu.VMEM((rows, HEAD), LOW),
            pltpu.VMEM((1, rows), WIDE),
            pltpu.VMEM((parts, rows, HEAD), WIDE),
            pltpu.VMEM((parts, rows, HEAD), WIDE),
        ],
        compiler_params=grant(40),
        cost_estimate=pair_cost(parts, rows, 5),
        name="attend_backward",
    )(packed, packed, values, grads, attended, log_totals, behind)


SLOPE = 0.7978845608028654


def project_kernel(
    layout, order_ref, tokens_ref, first_ref, near_a, far_a, near_b, far_b, behind_ref, *refs,
):
    *sent, low_ref, turned_ref, query_ref, key_ref, value_ref, vec_ref = refs
    owners = order_ref.shape[1]
    messages = [
        [sent[which].at[:, first + at] for at in range(count)] for which, first, count in layout
    ]
    part, fresh_part = query_ref.shape[0] // owners, value_ref.shape[0] // owners
    half = near_a.shape[1]
    groups = sent[0].shape[0]
    fresh_width = value_ref.shape[0]

    vectors = jnp.zeros((16, near_b.shape[2]), WIDE)
    for at in range(near_b.shape[0]):
        vectors = vectors + near_b[at, half - 16 :].astype(WIDE)
        vectors = vectors + far_b[at, half - 16 :].astype(WIDE)
    inputs = tokens_ref[...].astype(WIDE)
    normed, _ = normalize(inputs, 1)
    low_ref[...] = (normed * vectors[0:1] + vectors[1:2]).astype(LOW)
    turned_ref[...] = jnp.transpose(inputs).astype(LOW)
    blank = jnp.zeros((128 - vectors.shape[0], vectors.shape[1]), WIDE)
    vec_ref[...] = jnp.transpose(jnp.concatenate([vectors, blank], axis=0))
    for owner in range(owners):
        same_core = order_ref[0, owner] == 0
        weights = jnp.concatenate(
            [
                jnp.where(same_core, near_a[order_ref[1, owner]], far_a[order_ref[1, owner]]),
                jnp.where(same_core, near_b[order_ref[2, owner]], far_b[order_ref[2, owner]]),
            ],
            axis=0,
        )
        first = 0
        for ref, count in ((query_ref, part), (key_ref, part), (value_ref, fresh_part)):
            ref[owner * count : (owner + 1) * count] = weights[first : first + count]
            first += count
    low_one = low_ref[...]
    for which, ref in enumerate((query_ref, key_ref, value_ref)):
        products = dot(ref[...], low_one, 1, 1).astype(LOW)
        if which == 0:
            products = products * jnp.asarray(HEAD ** (-0.5), LOW)
        for slot, message in enumerate(messages):
            for group in range(groups):
                feature = (slot * groups + group) * HEAD
                if which < len(message) and feature < products.shape[0]:
                    message[which][group] = products[feature : feature + HEAD]
    for slot, message in enumerate(messages):
        for group in range(groups):
            first = (slot * groups + group) * HEAD - fresh_width
            if len(message) == 3 and first >= 0:
                start = first // 128 * 128
                block = turned(first_ref[:, start : start + 128])
                message[2][group] = block[first - start : first - start + HEAD]


def channels(layout):
    return [
        sum(count for which, _, count in layout if which == message)
        for message in range(1 + max(which for which, _, _ in layout))
    ]


def project(tokens, first_values, halves, order, behind, layout, part, fresh_part, groups):
    rows, width = tokens.shape
    owners = order.shape[1]
    held = [tokens, first_values, *halves[0], *halves[1]]
    shape = jax.ShapeDtypeStruct
    outs = [shape((groups, count, HEAD, rows), LOW) for count in channels(layout)] + [
        shape((rows, width), LOW), shape((width, rows), LOW), shape((width, width), LOW),
        shape((width, width), LOW), shape((fresh_part * owners, width), LOW),
        shape((width, 128), WIDE),
    ]
    return pl.pallas_call(
        functools.partial(project_kernel, layout),
        in_specs=[pl.BlockSpec(memory_space=pltpu.SMEM)]
        + [pl.BlockSpec(memory_space=pltpu.VMEM) for _ in held]
        + [untouched()],
        out_specs=[pl.BlockSpec(memory_space=pltpu.VMEM) for _ in outs],
        out_shape=outs,
        compiler_params=grant(48),
        cost_estimate=work(8, width),
        name="project",
    )(order, *held, behind)


def project_plain(tokens, first_values, halves, order, behind, layout, part, fresh_part, groups):
    rows, width = tokens.shape
    owners = order.shape[1]
    blocks = []
    for owner in range(owners):
        pieces = []
        for at, (near, far) in enumerate(halves):
            index = order[1 + at, owner]
            pieces.append(jnp.where(order[0, owner] == 0, pick(near, index), pick(far, index)))
        blocks.append(jnp.concatenate(pieces, axis=0))
    blocks = jnp.stack(blocks)
    query_t = blocks[:, :part].reshape(-1, width)
    key_t = blocks[:, part : 2 * part].reshape(-1, width)
    value_t = blocks[:, 2 * part : 2 * part + fresh_part].reshape(-1, width)
    vectors = jnp.sum(blocks[:, -16:].astype(WIDE), axis=0)
    normed, _ = normalize(tokens.astype(WIDE), 1)
    low_one = (normed * vectors[0:1] + vectors[1:2]).astype(LOW)
    queries = dot(query_t, low_one, 1, 1).astype(LOW) * jnp.asarray(HEAD ** (-0.5), LOW)
    keys = dot(key_t, low_one, 1, 1).astype(LOW)
    values = jnp.concatenate([dot(value_t, low_one, 1, 1).astype(LOW), first_values.T], axis=0)
    stacked = [array.reshape(-1, groups, HEAD, rows) for array in (queries, keys, values)]
    messages = [
        jnp.zeros((groups, count, HEAD, rows), LOW) for count in channels(layout)
    ]
    for slot, (which, first, count) in enumerate(layout):
        for at in range(count):
            messages[which] = messages[which].at[:, first + at].set(stacked[at][slot])
    table = jnp.pad(vectors.T, ((0, 0), (0, 128 - vectors.shape[0])))
    return (*messages, low_one, tokens.T, query_t, key_t, value_t, table)


def middle_kernel(
    attn_zero, attn_rest, tokens_ref, cot_ref, vec_ref, out_ref, fc_ref, proj_ref,
    output_ref, pack_ref, grad_zero, grad_rest, grad_res_ref, vec_back,
    attn_ref, cot_t, low_ref, normed_ref, scale_ref, sum_ref, back_ref,
):
    step = pl.program_id(0)
    owners = pack_ref.shape[0]
    block, width = fc_ref.shape
    part = width // owners
    fc_part = pl.num_programs(0) * block // owners
    share = block // fc_part
    groups = attn_zero.shape[0]

    def spots(zero, rest):
        for slot in range(1 + rest.shape[1]):
            for group in range(groups):
                ref = zero.at[group, 0] if slot == 0 else rest.at[group, slot - 1]
                yield (slot * groups + group) * HEAD, ref

    @pl.when(step == 0)
    def _():
        for first, ref in spots(attn_zero, attn_rest):
            attn_ref[first : first + HEAD] = ref[...]
        cot_t[...] = turned(cot_ref[...])
        residual = tokens_ref[...].astype(WIDE) + dot(out_ref[...], attn_ref[...], 1, 0)
        normed, scale = normalize(residual, 0)
        low_ref[...] = (normed * vec_ref[:, 2:3] + vec_ref[:, 3:4]).astype(LOW)
        normed_ref[...] = normed
        scale_ref[...] = scale
        sum_ref[...] = residual
        back_ref[...] = jnp.zeros_like(back_ref)

    low = low_ref[...]
    hidden = dot(fc_ref[...], low, 1, 0)
    bent = jnp.tanh(SLOPE * (hidden + 0.044715 * hidden * hidden * hidden))
    half = 0.5 * (1.0 + bent)
    active = (hidden * half).astype(LOW)
    slope = half + hidden * (0.5 * (1.0 - bent * bent)) * (
        SLOPE * (1.0 + (3 * 0.044715) * hidden * hidden)
    )
    sum_ref[...] += dot(proj_ref[...], active, 1, 0)
    cot = cot_t[...]
    grad_hidden = (dot(proj_ref[...], cot, 0, 0) * slope).astype(LOW)
    grad_proj = dot(cot, active, 1, 1).astype(LOW)
    grad_fc = dot(grad_hidden, low, 1, 1).astype(LOW)
    for owner in range(owners):
        pack_ref[owner, pl.ds(pl.multiple_of(fc_part + step * part, 16), part)] = grad_proj[
            owner * part : (owner + 1) * part
        ]
    for at in range(share):
        pack_ref[step * share + at, pl.ds(0, fc_part)] = grad_fc[at * fc_part : (at + 1) * fc_part]
    back_ref[...] += dot(fc_ref[...], grad_hidden, 0, 0)

    @pl.when(step == pl.num_programs(0) - 1)
    def _():
        output_ref[...] = jnp.transpose(sum_ref[...]).astype(LOW)
        grad, normed = back_ref[...], normed_ref[...]
        lane = lax.broadcasted_iota(jnp.int32, vec_back.shape, 1)
        grad_gain = jnp.sum(grad * normed, axis=1, keepdims=True)
        grad_bias = jnp.sum(grad, axis=1, keepdims=True)
        vec_back[...] = jnp.where(lane == 2, grad_gain, jnp.where(lane == 3, grad_bias, 0.0))
        grad_res = cot_t[...].astype(WIDE) + norm_back(
            grad * vec_ref[:, 2:3], normed, scale_ref[...]
        )
        grad_res_ref[...] = grad_res
        mixed = grad_res.astype(LOW)
        grad_attn = dot(out_ref[...], mixed, 0, 0).astype(LOW)
        for first, ref in spots(grad_zero, grad_rest):
            ref[...] = grad_attn[first : first + HEAD]
        grad_out = dot(mixed, attn_ref[...], 1, 1).astype(LOW)
        for owner in range(owners):
            pack_ref[owner, pl.ds(2 * fc_part, part)] = grad_out[owner * part : (owner + 1) * part]


def middle(attn_zero, attn_rest, tokens_t, cotangent, vectors, out_t, fc_t, proj_t, owners):
    width, rows = tokens_t.shape
    hidden = fc_t.shape[0]
    block = width
    shape = jax.ShapeDtypeStruct
    down = pl.BlockSpec((block, width), lambda j: (j, 0))
    along = pl.BlockSpec((width, block), lambda j: (0, j))
    held = (width, rows)
    pack = (owners, (2 * hidden + width) // owners, width)
    return pl.pallas_call(
        middle_kernel,
        grid=(hidden // block,),
        in_specs=[
            whole(*attn_zero.shape), whole(*attn_rest.shape), whole(*held), whole(rows, width),
            whole(width, 128), whole(width, width), down, along,
        ],
        out_specs=[
            whole(rows, width), whole(*pack), whole(*attn_zero.shape), whole(*attn_rest.shape),
            whole(*held), whole(width, 128),
        ],
        out_shape=[
            shape((rows, width), LOW), shape(pack, LOW), shape(attn_zero.shape, LOW),
            shape(attn_rest.shape, LOW), shape(held, WIDE), shape((width, 128), WIDE),
        ],
        scratch_shapes=[
            pltpu.VMEM(held, LOW), pltpu.VMEM(held, LOW), pltpu.VMEM(held, LOW),
            pltpu.VMEM(held, WIDE), pltpu.VMEM((1, rows), WIDE), pltpu.VMEM(held, WIDE),
            pltpu.VMEM(held, WIDE),
        ],
        compiler_params=grant(60),
        cost_estimate=work(40, width),
        name="middle",
    )(attn_zero, attn_rest, tokens_t, cotangent, vectors, out_t, fc_t, proj_t)


def joined(zero, rest):
    both = jnp.concatenate([zero, rest], axis=1).swapaxes(0, 1)
    return both.reshape(-1, both.shape[-1])


def middle_plain(attn_zero, attn_rest, tokens_t, cotangent, vectors, out_t, fc_t, proj_t, owners):
    width = tokens_t.shape[0]
    attn = joined(attn_zero, attn_rest)
    gain, bias = vectors[:, 2:3], vectors[:, 3:4]
    cot_t = cotangent.T
    residual = tokens_t.astype(WIDE) + dot(out_t, attn, 1, 0)
    normed, scale = normalize(residual, 0)
    low = (normed * gain + bias).astype(LOW)
    hidden = dot(fc_t, low, 1, 0)
    active, pull = jax.vjp(functools.partial(jax.nn.gelu, approximate=True), hidden)
    low_active = active.astype(LOW)
    output = (residual + dot(proj_t, low_active, 1, 0)).astype(LOW).T
    (grad_hidden,) = pull(dot(proj_t, cot_t, 0, 0))
    grad_hidden = grad_hidden.astype(LOW)
    grad_proj = dot(cot_t, low_active, 1, 1).astype(LOW)
    grad_fc = dot(grad_hidden, low, 1, 1).astype(LOW)
    grad = dot(fc_t, grad_hidden, 0, 0)
    grad_gain = jnp.sum(grad * normed, axis=1, keepdims=True)
    grad_bias = jnp.sum(grad, axis=1, keepdims=True)
    grad_res = cot_t.astype(WIDE) + norm_back(grad * gain, normed, scale)
    mixed = grad_res.astype(LOW)
    part = width // owners
    grad_proj = grad_proj.reshape(owners, part, -1, width).transpose(0, 2, 1, 3)
    pack = jnp.concatenate(
        [
            grad_fc.reshape(owners, -1, width),
            grad_proj.reshape(owners, -1, width),
            dot(mixed, attn, 1, 1).astype(LOW).reshape(owners, part, width),
        ],
        axis=1,
    )
    grad_attn = dot(out_t, mixed, 0, 0).astype(LOW)
    grad_attn = grad_attn.reshape(-1, attn_zero.shape[0], HEAD, attn.shape[1]).swapaxes(0, 1)
    table = jnp.concatenate([jnp.zeros((width, 2), WIDE), grad_gain, grad_bias], axis=1)
    table = jnp.pad(table, ((0, 0), (0, 124)))
    return output, pack, grad_attn[:, :1], grad_attn[:, 1:], grad_res, table


def weights_kernel(*refs):
    core_ref = refs[0]
    *homes, low_ref, query_ref, key_ref, value_ref, tokens_ref, vec_ref, _ = refs[1:-8]
    keep_ref, send_ref, grad_ref, q_ref, k_ref, v_ref, pack_ref, sems = refs[-8:]
    owners = 2 * pack_ref.shape[1]

    def store(owner, first, block):
        pack_ref[owner % 2, owner // 2, first : first + block.shape[0]] = block

    groups = homes[0].shape[0]
    for slot, home in enumerate(homes):
        for group in range(groups):
            first = (slot * groups + group) * HEAD
            for which, back in enumerate((q_ref, k_ref, v_ref)):
                if first < back.shape[0]:
                    back[first : first + HEAD] = home[group, which]
    low = low_ref[...]
    first = 0
    for back in (q_ref, k_ref, v_ref):
        grads = dot(back[...], low, 1, 0).astype(LOW)
        rows = grads.shape[0] // owners
        for owner in range(owners):
            store(owner, first, grads[owner * rows : (owner + 1) * rows])
        first += rows
    grad = (
        dot(query_ref[...], q_ref[...], 0, 0)
        + dot(key_ref[...], k_ref[...], 0, 0)
        + dot(value_ref[...], v_ref[...], 0, 0)
    )
    grad_ref[...] = grad
    normed, _ = normalize(tokens_ref[...].astype(WIDE), 0)
    lane = lax.broadcasted_iota(jnp.int32, vec_ref.shape, 1)
    grad_gain = jnp.sum(grad * normed, axis=1, keepdims=True)
    grad_bias = jnp.sum(grad, axis=1, keepdims=True)
    table = jnp.where(lane == 0, grad_gain, jnp.where(lane == 1, grad_bias, vec_ref[...]))
    table = jnp.transpose(table)[:16].astype(LOW)
    for owner in range(owners):
        store(owner, first, table)
    copies = [
        pltpu.make_async_copy(pack_ref.at[core], ref, sems.at[at])
        for at, (core, ref) in enumerate(((core_ref[0], keep_ref), (1 - core_ref[0], send_ref)))
    ]
    for copy in copies:
        copy.start()
    for copy in copies:
        copy.wait()


def weights_back(homes, low_one, query_t, key_t, value_t, tokens_t, vec_back, behind, owners):
    width, rows = tokens_t.shape
    fresh_width = value_t.shape[0]
    pack_rows = (2 * width + fresh_width) // owners + 16
    held = [*homes, low_one, query_t, key_t, value_t, tokens_t, vec_back]
    return pl.pallas_call(
        weights_kernel,
        out_shape=[
            jax.ShapeDtypeStruct((owners // 2, pack_rows, width), LOW),
            jax.ShapeDtypeStruct((owners // 2, pack_rows, width), LOW),
            jax.ShapeDtypeStruct((width, rows), WIDE),
        ],
        out_specs=[untouched(), untouched(), pl.BlockSpec(memory_space=pltpu.VMEM)],
        scratch_shapes=[
            pltpu.VMEM((width, rows), LOW), pltpu.VMEM((width, rows), LOW),
            pltpu.VMEM((fresh_width, rows), LOW),
            pltpu.VMEM((2, owners // 2, pack_rows, width), LOW),
            pltpu.SemaphoreType.DMA((2,)),
        ],
        in_specs=[pl.BlockSpec(memory_space=pltpu.SMEM)]
        + [pl.BlockSpec(memory_space=pltpu.VMEM) for _ in held]
        + [untouched()],
        compiler_params=grant(56),
        cost_estimate=work(12, width),
        name="weights_back",
    )((lax.axis_index("dp") & 1).reshape(1), *held, behind)


def weights_plain(homes, low_one, query_t, key_t, value_t, tokens_t, vec_back, behind, owners):
    width, rows = tokens_t.shape
    back_q, back_k = (
        jnp.stack([home[:, which] for home in homes]).reshape(width, rows) for which in range(2)
    )
    back_v = jnp.stack([home[:, 2] for home in homes])
    back_v = back_v.reshape(-1, rows)[: value_t.shape[0]]
    grad = dot(query_t, back_q, 0, 0) + dot(key_t, back_k, 0, 0) + dot(value_t, back_v, 0, 0)
    normed, _ = normalize(tokens_t.astype(WIDE), 0)
    table = jnp.concatenate(
        [
            jnp.sum(grad * normed, axis=1, keepdims=True), jnp.sum(grad, axis=1, keepdims=True),
            vec_back[:, 2:16],
        ],
        axis=1,
    ).T
    pieces = [
        dot(back, low_one, 1, 0).reshape(owners, -1, width) for back in (back_q, back_k, back_v)
    ]
    count = sum(piece.shape[1] for piece in pieces)
    padded = -(-count // 16) * 16
    padded = -(-(padded + 16) // 32) * 32 - 16
    pieces.append(jnp.zeros((owners, padded - count, width), WIDE))
    pieces.append(jnp.broadcast_to(table, (owners,) + table.shape))
    pack = jnp.concatenate(pieces, axis=1).astype(LOW)
    pack = pack.reshape((-1, 2) + pack.shape[1:])
    mine = lax.axis_index("dp") & 1
    return pick(pack, mine, 1), pick(pack, 1 - mine, 1), grad


def tokens_kernel(grad_ref, tokens_ref, res_ref, gain_ref, out_ref):
    normed, scale = normalize(tokens_ref[...].astype(WIDE), 0)
    grad = res_ref[...] + norm_back(grad_ref[...] * gain_ref[:, 0:1], normed, scale)
    out_ref[...] = jnp.transpose(grad).astype(LOW)


def tokens_back(grad_one, tokens_t, grad_residual, vectors):
    width, rows = grad_one.shape
    return pl.pallas_call(
        tokens_kernel,
        out_shape=jax.ShapeDtypeStruct((rows, width), LOW),
        compiler_params=grant(40),
        cost_estimate=work(4, width),
        name="tokens_back",
    )(grad_one, tokens_t, grad_residual, vectors)


def gate_kernel(*refs):
    pass


def gate(array, *behind):
    return pl.pallas_call(
        gate_kernel,
        in_specs=[untouched()] * (1 + len(behind)),
        out_specs=untouched(),
        out_shape=jax.ShapeDtypeStruct(array.shape, array.dtype),
        input_output_aliases={0: 0},
        name="gate",
    )(array, *behind)


def pick(stacked, index, axis=0):
    return lax.dynamic_index_in_dim(stacked, index, axis, keepdims=False)


def exchange(block, axis, bit):
    count = lax.axis_size(axis)
    return lax.ppermute(block, axis, [(i, i ^ (1 << bit)) for i in range(count)])


def swap(message):
    return lax.all_to_all(message, "seq", split_axis=0, concat_axis=0, tiled=True)


def gather_halves(shard, behind):
    bits = lax.axis_size("dp").bit_length() - 1
    half = shard.shape[0] // 2
    halves = []
    for block, order in (
        (shard[:half], range(1, bits)),
        (shard[half:], range(bits - 1, 0, -1)),
    ):
        held = block[None]
        for bit in order:
            held = jnp.concatenate([held, exchange(held, "dp", bit)])
        halves.append(held)
    halves[1] = gate(halves[1], behind)
    return [(held, exchange(held, "dp", 0)) for held in halves]


def gathered_order():
    count, here = lax.axis_size("dp"), lax.axis_index("dp")
    bits = count.bit_length() - 1
    offset = jnp.arange(count, dtype=jnp.int32) ^ here
    places = [0, 0]
    for at in range(bits - 1):
        bit = (offset >> (at + 1)) & 1
        places[0] = places[0] + (bit << at)
        places[1] = places[1] + (bit << (bits - 2 - at))
    return jnp.stack([offset & 1, *places])


def scatter_blocks(keep, send, others):
    count, here = lax.axis_size("dp"), lax.axis_index("dp")
    bits = count.bit_length() - 1
    rows, width = keep.shape[1:]

    def halve(held, bit, axis, other):
        mine = (here >> bit) & 1
        sent = pick(held, 1 - mine, axis).astype(LOW)
        sent = exchange(sent if other is None else gate(sent, other), "dp", bit)
        return pick(held, mine, axis).astype(WIDE) + sent.astype(WIDE)

    held = keep.astype(WIDE) + exchange(send, "dp", 0).astype(WIDE)
    held = held.reshape((2,) * (bits - 1) + (rows, width))
    halves = [held[..., : rows // 2, :], held[..., rows // 2 :, :]]
    orders = [list(range(1, bits)), list(range(bits - 1, 0, -1))]
    left = [list(range(bits - 1, 0, -1)) for _ in orders]
    for at in range(bits - 1):
        other = next(others, None)
        for which, order in enumerate(orders):
            axis = left[which].index(order[at])
            halves[which] = halve(halves[which], order[at], axis, other)
            left[which].remove(order[at])
    return jnp.concatenate(halves)


def first_step_kernel(place_ref, keep_ref, got_ref, a_send, a_keep, b_send, b_keep):
    x, y = place_ref[0], place_ref[1]
    half = keep_ref.shape[1] // 2

    def total(at, first):
        rows = pl.ds(first, half)
        return keep_ref[at, rows].astype(WIDE) + got_ref[at, rows].astype(WIDE)

    for other in range(2):
        a_send[other] = total(2 * other + 1 - x, 0).astype(LOW)
        a_keep[other] = total(2 * other + x, 0)
        b_send[other] = total(2 * (1 - y) + other, half).astype(LOW)
        b_keep[other] = total(2 * y + other, half)


def second_step_kernel(place_ref, a_keep, a_got, b_keep, b_got, a_send, a_next, b_send, b_next):
    x, y = place_ref[0], place_ref[1]
    a_send[...] = (a_keep[1 - y] + a_got[1 - y].astype(WIDE)).astype(LOW)
    a_next[...] = a_keep[y] + a_got[y].astype(WIDE)
    b_send[...] = (b_keep[1 - x] + b_got[1 - x].astype(WIDE)).astype(LOW)
    b_next[...] = b_keep[x] + b_got[x].astype(WIDE)


def third_step_kernel(place_ref, a_keep, a_got, b_keep, b_got, send, keep):
    a_sum = a_keep[...] + a_got[...].astype(WIDE)
    b_sum = b_keep[...] + b_got[...].astype(WIDE)
    first = place_ref[2] == 0
    send[...] = jnp.where(first, b_sum, a_sum).astype(LOW)
    keep[...] = jnp.where(first, a_sum, b_sum)


def last_step_kernel(place_ref, mine_ref, other_ref, query_ref, key_ref, value_ref, vec_ref):
    first = place_ref[2] == 0
    mine, other = mine_ref[...].astype(WIDE), other_ref[...].astype(WIDE)
    pack = jnp.concatenate(
        [jnp.where(first, mine, other), jnp.where(first, other, mine)], axis=0
    )
    at = 0
    for ref in (query_ref, key_ref, value_ref):
        ref[...] = pack[at : at + ref.shape[0]]
        at += ref.shape[0]
    vec_ref[...] = pack[at:]


def step_call(kernel, place, held, shapes):
    return pl.pallas_call(
        kernel,
        in_specs=[pl.BlockSpec(memory_space=pltpu.SMEM)]
        + [pl.BlockSpec(memory_space=pltpu.VMEM) for _ in held],
        out_specs=[pl.BlockSpec(memory_space=pltpu.VMEM) for _ in shapes],
        out_shape=[jax.ShapeDtypeStruct(dims, kind) for dims, kind in shapes],
        compiler_params=grant(32),
        cost_estimate=work(2, held[0].shape[-1]),
        name=kernel.__name__,
    )(place, *held)


def sum_four(keep, send, others, part, fresh_part):
    here = lax.axis_index("dp")
    place = jnp.stack([(here >> 1) & 1, here >> 2, lax.axis_index("seq") & 1])
    _, rows, width = keep.shape
    half = rows // 2
    pair, single = (2, half, width), (half, width)
    got = exchange(gate(send, others[0]), "dp", 0)
    a_send, a_keep, b_send, b_keep = step_call(
        first_step_kernel, place, [keep, got],
        [(pair, LOW), (pair, WIDE), (pair, LOW), (pair, WIDE)],
    )
    a_got = exchange(a_send, "dp", 1)
    b_got = exchange(b_send, "dp", 2)
    a_send, a_keep, b_send, b_keep = step_call(
        second_step_kernel, place, [a_keep, a_got, b_keep, b_got],
        [(single, LOW), (single, WIDE), (single, LOW), (single, WIDE)],
    )
    a_got = exchange(gate(a_send, others[1]), "dp", 2)
    b_got = exchange(gate(b_send, others[1]), "dp", 1)
    send, keep = step_call(
        third_step_kernel, place, [a_keep, a_got, b_keep, b_got], [(single, LOW), (single, WIDE)]
    )
    mine = (keep + exchange(gate(send, others[2]), "seq", 0).astype(WIDE)).astype(LOW)
    mine = seq_pairs(mine)
    query_t, key_t, value_t, vectors = step_call(
        last_step_kernel, place, [mine, exchange(mine, "seq", 0)],
        [
            ((part, width), WIDE), ((part, width), WIDE), ((fresh_part, width), WIDE),
            ((rows - 2 * part - fresh_part, width), WIDE),
        ],
    )
    return query_t.T, key_t.T, value_t.T, vectors, keep


def sum_any(keep, send, others, part, fresh_part):
    pack = seq_whole(seq_pairs(seq_halves(scatter_blocks(keep, send, iter(others)))))
    return (
        pack[:part].T, pack[part : 2 * part].T, pack[2 * part : 2 * part + fresh_part].T,
        pack[-16:], keep,
    )


def seq_halves(block):
    mine = lax.axis_index("seq") & 1
    halves = block.reshape((2, -1) + block.shape[1:])
    sent = exchange(pick(halves, 1 - mine).astype(LOW), "seq", 0)
    return (pick(halves, mine).astype(WIDE) + sent.astype(WIDE)).astype(LOW)


def seq_pairs(held):
    total = held.astype(WIDE)
    for bit in range(1, lax.axis_size("seq").bit_length() - 1):
        total = total + exchange(total.astype(LOW), "seq", bit).astype(WIDE)
    return total.astype(LOW)


def seq_whole(held, other=None):
    mine = lax.axis_index("seq") & 1
    other = exchange(held, "seq", 0) if other is None else other
    first, second = jnp.where(mine == 0, held, other), jnp.where(mine == 0, other, held)
    return jnp.concatenate([first, second]).astype(WIDE)


def gather(shard):
    return lax.all_gather(shard, "dp", axis=0, tiled=True)


def shards(
    tokens, first_values, cotangent, ln1_gain, ln1_bias, w_query, w_key, w_value, w_out,
    ln2_gain, ln2_bias, w_fc, w_proj,
):
    owners = lax.axis_size("dp")
    groups = lax.axis_size("seq")
    rows, width = tokens.shape
    local = HEADS // groups
    part, fresh_part = w_query.shape[1], w_value.shape[1]
    fresh_width = fresh_part * owners

    weight_rows = -(-(2 * part + fresh_part) // 16) * 16
    pack_rows = -(-(weight_rows + 16) // 32) * 32
    aligned = fresh_part % 16 == 0 and pack_rows == weight_rows + 16
    here = lax.axis_index("dp")

    last = local - 1
    first = (last * groups * HEAD - fresh_width) // HEAD
    early = first_values[:, first * HEAD :].T.reshape(groups, 1, HEAD, rows)
    early = swap(early)
    vectors = jnp.stack([ln1_gain, ln1_bias, ln2_gain, ln2_bias])
    vectors = lax.dynamic_update_slice(jnp.zeros((16, width), LOW), vectors, (0, here * part))
    first_pack = jnp.concatenate([w_query.T, w_key.T, w_value.T], axis=0)
    first_pack = jnp.pad(first_pack, ((0, pack_rows - 16 - first_pack.shape[0]), (0, 0)))
    halves = gather_halves(jnp.concatenate([first_pack, vectors], axis=0), early)
    out_t, fc_t, proj_t = (
        gather(shard.T) for shard in (w_out, w_fc, w_proj)
    )

    layout = [(0, 0, 3)] + [(1, 2 + 3 * (last - 2 - at), 3) for at in range(last - 1)] + [(1, 0, 2)]
    *messages, low_one, tokens_t, query_t, key_t, value_t, vectors = (
        project if aligned else project_plain
    )(
        tokens, first_values, halves, gathered_order(), early, layout, part, fresh_part, groups
    )

    arrived = {1: swap(messages[1])}
    arrived[0] = swap(gate(messages[0], arrived[1]))
    log_totals, held = {}, None
    sources = [
        (which, first, (early, 0) if slot == last else (None, first + 2))
        for slot, (which, first, _) in enumerate(layout)
    ]

    def inputs(slot):
        which, first, (values, at) = sources[slot]
        return arrived[which], first, arrived[which] if values is None else values, at

    for slot in range(last, 0, -1):
        held, log_totals[slot] = attend(*inputs(slot), held, slot - 1, last)
    rest = held
    zero, log_totals[0] = attend(*inputs(0), None, 0, 1)

    output, grad_pack, grad_zero, grad_rest, grad_residual, vec_back = (
        middle if aligned else middle_plain
    )(swap(zero), swap(rest), tokens_t, cotangent, vectors, out_t, fc_t, proj_t, owners)
    grad_pack = lax.psum_scatter(
        grad_pack.reshape(-1, width), "dp", scatter_dimension=0, tiled=True
    )
    grad_pack = seq_halves(grad_pack)

    grad_zero = swap(grad_zero)
    grad_rest = swap(grad_rest)
    homes = []
    for slot in range(local):
        grads, grads_at = (grad_rest, slot - 1) if slot else (grad_zero, 0)
        attended, attended_at = (rest, slot - 1) if slot else (zero, 0)
        behind = homes[slot - 2] if slot > 1 else log_totals[slot]
        grads = attend_backward(
            *inputs(slot), grads, grads_at, attended, attended_at, log_totals[slot],
            behind,
        )
        homes.append(swap(grads))
    keep, send, grad_one = (weights_back if aligned else weights_plain)(
        homes, low_one, query_t, key_t, value_t, tokens_t, vec_back, grad_pack, owners
    )
    cut = grad_pack.shape[0] * 3 // 80 * 16
    pairs = [seq_pairs(grad_pack[:cut]), seq_pairs(grad_pack[cut:])]
    backs = [exchange(block, "seq", 0) for block in pairs]
    others = [*pairs, backs[0]]
    grad_query, grad_key, grad_value, vectors_back, behind = (
        sum_four if aligned and owners == 8 else sum_any
    )(keep, send, others, part, fresh_part)
    grad_pack = seq_whole(jnp.concatenate(pairs), jnp.concatenate(backs))
    grad_first = jnp.concatenate([home[:, 2] for home in homes]).reshape(-1, rows)
    grad_first = grad_first[fresh_width:].T

    grad_tokens = tokens_back(gate(grad_one, behind), tokens_t, grad_residual, vectors)
    vectors = lax.dynamic_slice(vectors_back, (0, here * part), (4, part))
    fc_part = w_fc.shape[1]
    grad_proj = grad_pack[fc_part : 2 * fc_part].reshape(-1, part, width).transpose(0, 2, 1)
    return (
        output,
        grad_tokens,
        grad_first,
        vectors[0],
        vectors[1],
        grad_query,
        grad_key,
        grad_value,
        grad_pack[2 * fc_part :].T,
        vectors[2],
        vectors[3],
        grad_pack[:fc_part].T,
        grad_proj.reshape(-1, part),
    )


def solution(mesh):
    row = P(("dp", "seq"), None)
    vector, matrix = P("dp"), P(None, "dp")
    weights = (vector, vector, matrix, matrix, matrix, matrix, vector, vector, matrix, matrix)
    return jax.shard_map(
        shards,
        mesh=mesh,
        in_specs=(row, row, row) + weights,
        out_specs=(row, row, row) + weights,
        check_vma=False,
    )
```

```python
import functools
import math

import jax
import jax.numpy as jnp
from jax import lax
from jax.experimental import pallas as pl
from jax.experimental.pallas import tpu as pltpu
from jax.sharding import PartitionSpec as P

HEADS = 12
HEAD = 64
EPSILON = 1e-05
LOW = jnp.bfloat16
WIDE = jnp.float32


def dot(left, right, left_dim, right_dim):
    return lax.dot_general(
        left, right, (((left_dim,), (right_dim,)), ((), ())), preferred_element_type=WIDE
    )


def causal(scores):
    key_pos = lax.broadcasted_iota(jnp.int32, scores.shape, 0)
    query_pos = lax.broadcasted_iota(jnp.int32, scores.shape, 1)
    return jnp.where(key_pos <= query_pos, scores, -1e30)


def turned(block):
    return jnp.transpose(block.astype(WIDE)).astype(LOW)


def sub_width(rows):
    for parts in (2, 3, 4, 6):
        if rows % (parts * 128) == 0:
            return rows // parts
    return rows


def normalize(values, axis):
    centred = values - jnp.mean(values, axis=axis, keepdims=True)
    scale = lax.rsqrt(jnp.mean(centred * centred, axis=axis, keepdims=True) + EPSILON)
    return centred * scale, scale


def norm_back(grad, normed, scale):
    return scale * (
        grad
        - jnp.mean(grad, axis=0, keepdims=True)
        - normed * jnp.mean(grad * normed, axis=0, keepdims=True)
    )


def whole(*dims):
    return pl.BlockSpec(dims, lambda *_: (0,) * len(dims), pipeline_mode=pl.Buffered(1))


def untouched():
    return pl.BlockSpec(memory_space=pl.ANY)


def head_block(rows, at):
    return pl.BlockSpec((1, 1, HEAD, rows), lambda i: (i, at, 0, 0))


def head_whole(parts, rows, at):
    return pl.BlockSpec((parts, 1, HEAD, rows), lambda i: (0, at, 0, 0))


def grant(mebibytes):
    return pltpu.CompilerParams(vmem_limit_bytes=mebibytes << 20)


def forward_kernel(q_ref, k_ref, v_ref, *refs):
    o_ref, log_ref, key_rows = refs[-3:]
    step = pl.program_id(0)
    parts, rows = k_ref.shape[0], k_ref.shape[3]
    sub = sub_width(rows)

    @pl.when(step == 0)
    def _():
        for part in range(parts):
            key_rows[part] = turned(k_ref[part, 0])

    for first in range(0, rows, sub):
        cols = pl.ds(first, sub)
        q = q_ref[0, 0, :, cols]
        blocks = []
        if first:
            blocks.append((0, dot(key_rows[step, pl.ds(0, first)], q, 1, 0)))
        blocks.append((first, causal(dot(key_rows[step, cols], q, 1, 0))))
        top = functools.reduce(
            jnp.maximum, [jnp.max(scores, axis=0, keepdims=True) for _, scores in blocks]
        )
        total = jnp.zeros((1, sub), WIDE)
        mixed = jnp.zeros((HEAD, sub), WIDE)
        for offset, scores in blocks:
            raised = jnp.exp(scores - top)
            total = total + jnp.sum(raised, axis=0, keepdims=True)
            mixed = mixed + dot(
                v_ref[step, 0, :, pl.ds(offset, scores.shape[0])], raised.astype(LOW), 1, 0
            )

        def earlier(part, carried):
            top, total, mixed = carried
            scores = dot(key_rows[part], q, 1, 0)
            new_top = jnp.maximum(top, jnp.max(scores, axis=0, keepdims=True))
            shrink = jnp.exp(top - new_top)
            raised = jnp.exp(scores - new_top)
            return (
                new_top,
                shrink * total + jnp.sum(raised, axis=0, keepdims=True),
                shrink * mixed + dot(v_ref[part, 0], raised.astype(LOW), 1, 0),
            )

        top, total, mixed = lax.fori_loop(0, step, earlier, (top, total, mixed))
        o_ref[0, 0, :, cols] = (mixed / total).astype(LOW)
        log_ref[0, :, cols] = top + jnp.log(total)


def work(units, width):
    return pl.CostEstimate(
        flops=units * 2 * width**3, bytes_accessed=units * 2 * width**2, transcendentals=0
    )


def pair_cost(parts, rows, matmuls):
    pairs = parts * parts * rows * rows // 2
    return pl.CostEstimate(
        flops=2 * matmuls * pairs * HEAD * 4,
        bytes_accessed=parts * rows * HEAD * 16,
        transcendentals=pairs,
    )


def attend(packed, query_at, values, value_at, held, held_at, held_slots):
    parts, _, _, rows = packed.shape
    shape = jax.ShapeDtypeStruct
    carried = [] if held is None else [held]
    return pl.pallas_call(
        forward_kernel,
        grid=(parts,),
        in_specs=[
            head_block(rows, query_at), head_whole(parts, rows, query_at + 1),
            head_whole(parts, rows, value_at),
        ]
        + [untouched() for _ in carried],
        out_specs=[
            head_block(rows, held_at), pl.BlockSpec((1, 1, rows), lambda i: (i, 0, 0)),
        ],
        out_shape=[
            shape((parts, held_slots, HEAD, rows), LOW), shape((parts, 1, rows), WIDE),
        ],
        scratch_shapes=[pltpu.VMEM((parts, rows, HEAD), LOW)],
        input_output_aliases={3: 0} if carried else {},
        compiler_params=grant(40),
        cost_estimate=pair_cost(parts, rows, 2),
        name="attend",
    )(packed, packed, values, *carried)


def backward_kernel(
    q_ref, k_ref, v_ref, do_ref, o_ref, log_ref, behind_ref, out_ref,
    key_rows, value_rows, query_rows, grad_rows, inner_ref, key_sum, value_sum,
):
    step = pl.program_id(0)
    parts, rows = k_ref.shape[0], k_ref.shape[3]
    sub = sub_width(rows)

    @pl.when(step == 0)
    def _():
        for part in range(parts):
            key_rows[part] = turned(k_ref[part, 0])
            value_rows[part] = turned(v_ref[part, 0])
        key_sum[...] = jnp.zeros_like(key_sum)
        value_sum[...] = jnp.zeros_like(value_sum)

    query_rows[...] = turned(q_ref[0, 0])
    grads = do_ref[0, 0].astype(WIDE)
    grad_rows[...] = jnp.transpose(grads).astype(LOW)
    inner_ref[...] = jnp.sum(grads * o_ref[0, 0].astype(WIDE), axis=0, keepdims=True)
    for first in range(0, rows, sub):
        cols = pl.ds(first, sub)
        q, do = q_ref[0, 0, :, cols], do_ref[0, 0, :, cols]
        log_total, inner = log_ref[0, :, cols], inner_ref[:, cols]
        q_rows, do_rows = query_rows[cols], grad_rows[cols]

        def pair(part, offset, size, masked):
            span = pl.ds(offset, size)
            scores = dot(key_rows[part, span], q, 1, 0)
            if masked:
                scores = causal(scores)
            probs = jnp.exp(scores - log_total)
            grad_probs = dot(value_rows[part, span], do, 1, 0)
            grad_scores = (probs * (grad_probs - inner)).astype(LOW)
            value_sum[part, span] += dot(probs.astype(LOW), do_rows, 1, 0)
            key_sum[part, span] += dot(grad_scores, q_rows, 1, 0)
            return dot(k_ref[part, 0, :, span], grad_scores, 1, 0)

        grad_q = pair(step, first, sub, True)
        if first:
            grad_q = grad_q + pair(step, 0, first, False)
        grad_q = lax.fori_loop(
            0, step, lambda part, carried: carried + pair(part, 0, rows, False), grad_q
        )
        out_ref[step, 0, :, cols] = (grad_q * HEAD ** (-0.5)).astype(LOW)

    @pl.when(step == parts - 1)
    def _():
        for part in range(parts):
            out_ref[part, 1] = jnp.transpose(key_sum[part]).astype(LOW)
            out_ref[part, 2] = jnp.transpose(value_sum[part]).astype(LOW)


def attend_backward(
    packed, query_at, values, value_at, grads, grads_at, attended, attended_at, log_totals, behind
):
    parts, _, _, rows = packed.shape
    return pl.pallas_call(
        backward_kernel,
        grid=(parts,),
        in_specs=[
            head_block(rows, query_at), head_whole(parts, rows, query_at + 1),
            head_whole(parts, rows, value_at), head_block(rows, grads_at), head_block(rows, attended_at),
            pl.BlockSpec((1, 1, rows), lambda i: (i, 0, 0)),
            untouched(),
        ],
        out_specs=pl.BlockSpec((parts, 3, HEAD, rows), lambda i: (0, 0, 0, 0)),
        out_shape=jax.ShapeDtypeStruct((parts, 3, HEAD, rows), LOW),
        scratch_shapes=[
            pltpu.VMEM((parts, rows, HEAD), LOW),
            pltpu.VMEM((parts, rows, HEAD), LOW),
            pltpu.VMEM((rows, HEAD), LOW),
            pltpu.VMEM((rows, HEAD), LOW),
            pltpu.VMEM((1, rows), WIDE),
            pltpu.VMEM((parts, rows, HEAD), WIDE),
            pltpu.VMEM((parts, rows, HEAD), WIDE),
        ],
        compiler_params=grant(40),
        cost_estimate=pair_cost(parts, rows, 5),
        name="attend_backward",
    )(packed, packed, values, grads, attended, log_totals, behind)


SLOPE = 0.7978845608028654


def project_kernel(
    layout, order_ref, tokens_ref, first_ref, near_a, far_a, near_b, far_b, behind_ref, *refs,
):
    *sent, low_ref, turned_ref, query_ref, key_ref, value_ref, vec_ref = refs
    owners = order_ref.shape[1]
    messages = [
        [sent[which].at[:, first + at] for at in range(count)] for which, first, count in layout
    ]
    part, fresh_part = query_ref.shape[0] // owners, value_ref.shape[0] // owners
    half = near_a.shape[1]
    groups = sent[0].shape[0]
    fresh_width = value_ref.shape[0]

    vectors = jnp.zeros((16, near_b.shape[2]), WIDE)
    for at in range(near_b.shape[0]):
        vectors = vectors + near_b[at, half - 16 :].astype(WIDE)
        vectors = vectors + far_b[at, half - 16 :].astype(WIDE)
    inputs = tokens_ref[...].astype(WIDE)
    normed, _ = normalize(inputs, 1)
    low_ref[...] = (normed * vectors[0:1] + vectors[1:2]).astype(LOW)
    turned_ref[...] = jnp.transpose(inputs).astype(LOW)
    blank = jnp.zeros((128 - vectors.shape[0], vectors.shape[1]), WIDE)
    vec_ref[...] = jnp.transpose(jnp.concatenate([vectors, blank], axis=0))
    for owner in range(owners):
        same_core = order_ref[0, owner] == 0
        weights = jnp.concatenate(
            [
                jnp.where(same_core, near_a[order_ref[1, owner]], far_a[order_ref[1, owner]]),
                jnp.where(same_core, near_b[order_ref[2, owner]], far_b[order_ref[2, owner]]),
            ],
            axis=0,
        )
        first = 0
        for ref, count in ((query_ref, part), (key_ref, part), (value_ref, fresh_part)):
            ref[owner * count : (owner + 1) * count] = weights[first : first + count]
            first += count
    low_one = low_ref[...]
    for which, ref in enumerate((query_ref, key_ref, value_ref)):
        products = dot(ref[...], low_one, 1, 1).astype(LOW)
        if which == 0:
            products = products * jnp.asarray(HEAD ** (-0.5), LOW)
        for slot, message in enumerate(messages):
            for group in range(groups):
                feature = (slot * groups + group) * HEAD
                if which < len(message) and feature < products.shape[0]:
                    message[which][group] = products[feature : feature + HEAD]
    for slot, message in enumerate(messages):
        for group in range(groups):
            first = (slot * groups + group) * HEAD - fresh_width
            if len(message) == 3 and first >= 0:
                start = first // 128 * 128
                block = turned(first_ref[:, start : start + 128])
                message[2][group] = block[first - start : first - start + HEAD]


def channels(layout):
    return [
        sum(count for which, _, count in layout if which == message)
        for message in range(1 + max(which for which, _, _ in layout))
    ]


def project(tokens, first_values, halves, order, behind, layout, part, fresh_part, groups):
    rows, width = tokens.shape
    owners = order.shape[1]
    held = [tokens, first_values, *halves[0], *halves[1]]
    shape = jax.ShapeDtypeStruct
    outs = [shape((groups, count, HEAD, rows), LOW) for count in channels(layout)] + [
        shape((rows, width), LOW), shape((width, rows), LOW), shape((width, width), LOW),
        shape((width, width), LOW), shape((fresh_part * owners, width), LOW),
        shape((width, 128), WIDE),
    ]
    return pl.pallas_call(
        functools.partial(project_kernel, layout),
        in_specs=[pl.BlockSpec(memory_space=pltpu.SMEM)]
        + [pl.BlockSpec(memory_space=pltpu.VMEM) for _ in held]
        + [untouched()],
        out_specs=[pl.BlockSpec(memory_space=pltpu.VMEM) for _ in outs],
        out_shape=outs,
        compiler_params=grant(48),
        cost_estimate=work(8, width),
        name="project",
    )(order, *held, behind)


def project_plain(tokens, first_values, halves, order, behind, layout, part, fresh_part, groups):
    rows, width = tokens.shape
    owners = order.shape[1]
    blocks = []
    for owner in range(owners):
        pieces = []
        for at, (near, far) in enumerate(halves):
            index = order[1 + at, owner]
            pieces.append(jnp.where(order[0, owner] == 0, pick(near, index), pick(far, index)))
        blocks.append(jnp.concatenate(pieces, axis=0))
    blocks = jnp.stack(blocks)
    query_t = blocks[:, :part].reshape(-1, width)
    key_t = blocks[:, part : 2 * part].reshape(-1, width)
    value_t = blocks[:, 2 * part : 2 * part + fresh_part].reshape(-1, width)
    vectors = jnp.sum(blocks[:, -16:].astype(WIDE), axis=0)
    normed, _ = normalize(tokens.astype(WIDE), 1)
    low_one = (normed * vectors[0:1] + vectors[1:2]).astype(LOW)
    queries = dot(query_t, low_one, 1, 1).astype(LOW) * jnp.asarray(HEAD ** (-0.5), LOW)
    keys = dot(key_t, low_one, 1, 1).astype(LOW)
    values = jnp.concatenate([dot(value_t, low_one, 1, 1).astype(LOW), first_values.T], axis=0)
    stacked = [array.reshape(-1, groups, HEAD, rows) for array in (queries, keys, values)]
    messages = [
        jnp.zeros((groups, count, HEAD, rows), LOW) for count in channels(layout)
    ]
    for slot, (which, first, count) in enumerate(layout):
        for at in range(count):
            messages[which] = messages[which].at[:, first + at].set(stacked[at][slot])
    table = jnp.pad(vectors.T, ((0, 0), (0, 128 - vectors.shape[0])))
    return (*messages, low_one, tokens.T, query_t, key_t, value_t, table)


def middle_kernel(place_ref, attn_rest, *refs):
    groups = attn_rest.shape[0]
    attn_zero, refs = refs[:groups], refs[groups:]
    (
        tokens_ref, cot_ref, vec_ref, out_ref, fc_ref, proj_ref,
        output_ref, pack_ref, grad_zero, grad_rest, grad_res_ref, vec_back,
        attn_ref, cot_t, low_ref, normed_ref, scale_ref, sum_ref, back_ref,
    ) = refs
    step = pl.program_id(0)
    owners = pack_ref.shape[0]
    block, width = fc_ref.shape
    part = width // owners
    fc_part = pl.num_programs(0) * block // owners
    share = block // fc_part

    def spots(rest, first):
        for slot in range(rest.shape[1]):
            for group in range(groups):
                yield (first + slot * groups + group) * HEAD, rest.at[group, slot]

    @pl.when(step == 0)
    def _():
        for first, ref in spots(attn_rest, groups):
            attn_ref[first : first + HEAD] = ref[...]
        for turn, ref in enumerate(attn_zero):
            group = lax.rem(place_ref[0] + groups - turn, groups)
            attn_ref[pl.ds(pl.multiple_of(group * HEAD, HEAD), HEAD)] = ref[0]
        cot_t[...] = turned(cot_ref[...])
        residual = tokens_ref[...].astype(WIDE) + dot(out_ref[...], attn_ref[...], 1, 0)
        normed, scale = normalize(residual, 0)
        low_ref[...] = (normed * vec_ref[:, 2:3] + vec_ref[:, 3:4]).astype(LOW)
        normed_ref[...] = normed
        scale_ref[...] = scale
        sum_ref[...] = residual
        back_ref[...] = jnp.zeros_like(back_ref)

    low = low_ref[...]
    hidden = dot(fc_ref[...], low, 1, 0)
    bent = jnp.tanh(SLOPE * (hidden + 0.044715 * hidden * hidden * hidden))
    half = 0.5 * (1.0 + bent)
    active = (hidden * half).astype(LOW)
    slope = half + hidden * (0.5 * (1.0 - bent * bent)) * (
        SLOPE * (1.0 + (3 * 0.044715) * hidden * hidden)
    )
    sum_ref[...] += dot(proj_ref[...], active, 1, 0)
    cot = cot_t[...]
    grad_hidden = (dot(proj_ref[...], cot, 0, 0) * slope).astype(LOW)
    grad_proj = dot(cot, active, 1, 1).astype(LOW)
    grad_fc = dot(grad_hidden, low, 1, 1).astype(LOW)
    for owner in range(owners):
        pack_ref[owner, pl.ds(pl.multiple_of(fc_part + step * part, 16), part)] = grad_proj[
            owner * part : (owner + 1) * part
        ]
    for at in range(share):
        pack_ref[step * share + at, pl.ds(0, fc_part)] = grad_fc[at * fc_part : (at + 1) * fc_part]
    back_ref[...] += dot(fc_ref[...], grad_hidden, 0, 0)

    @pl.when(step == pl.num_programs(0) - 1)
    def _():
        output_ref[...] = jnp.transpose(sum_ref[...]).astype(LOW)
        grad, normed = back_ref[...], normed_ref[...]
        lane = lax.broadcasted_iota(jnp.int32, vec_back.shape, 1)
        grad_gain = jnp.sum(grad * normed, axis=1, keepdims=True)
        grad_bias = jnp.sum(grad, axis=1, keepdims=True)
        vec_back[...] = jnp.where(lane == 2, grad_gain, jnp.where(lane == 3, grad_bias, 0.0))
        grad_res = cot_t[...].astype(WIDE) + norm_back(
            grad * vec_ref[:, 2:3], normed, scale_ref[...]
        )
        grad_res_ref[...] = grad_res
        mixed = grad_res.astype(LOW)
        grad_attn = dot(out_ref[...], mixed, 0, 0).astype(LOW)
        for spot, part_of in ((0, grad_zero), (groups, grad_rest)):
            for first, ref in spots(part_of, spot):
                ref[...] = grad_attn[first : first + HEAD]
        grad_out = dot(mixed, attn_ref[...], 1, 1).astype(LOW)
        for owner in range(owners):
            pack_ref[owner, pl.ds(2 * fc_part, part)] = grad_out[owner * part : (owner + 1) * part]


def middle(attn_zero, attn_rest, tokens_t, cotangent, vectors, out_t, fc_t, proj_t, owners):
    width, rows = tokens_t.shape
    hidden = fc_t.shape[0]
    block = width
    shape = jax.ShapeDtypeStruct
    down = pl.BlockSpec((block, width), lambda j: (j, 0))
    along = pl.BlockSpec((width, block), lambda j: (0, j))
    held = (width, rows)
    pack = (owners, (2 * hidden + width) // owners, width)
    zero = (len(attn_zero), *attn_zero[0].shape)
    return pl.pallas_call(
        middle_kernel,
        grid=(hidden // block,),
        in_specs=[
            pl.BlockSpec(memory_space=pltpu.SMEM), whole(*attn_rest.shape),
            *(whole(*block.shape) for block in attn_zero), whole(*held), whole(rows, width),
            whole(width, 128), whole(width, width), down, along,
        ],
        out_specs=[
            whole(rows, width), whole(*pack), whole(*zero), whole(*attn_rest.shape),
            whole(*held), whole(width, 128),
        ],
        out_shape=[
            shape((rows, width), LOW), shape(pack, LOW), shape(zero, LOW),
            shape(attn_rest.shape, LOW), shape(held, WIDE), shape((width, 128), WIDE),
        ],
        scratch_shapes=[
            pltpu.VMEM(held, LOW), pltpu.VMEM(held, LOW), pltpu.VMEM(held, LOW),
            pltpu.VMEM(held, WIDE), pltpu.VMEM((1, rows), WIDE), pltpu.VMEM(held, WIDE),
            pltpu.VMEM(held, WIDE),
        ],
        compiler_params=grant(60),
        cost_estimate=work(40, width),
        name="middle",
    )(
        lax.axis_index("seq").reshape(1), attn_rest, *attn_zero, tokens_t, cotangent, vectors,
        out_t, fc_t, proj_t,
    )


def joined(zero, rest):
    both = jnp.concatenate([zero, rest], axis=1).swapaxes(0, 1)
    return both.reshape(-1, both.shape[-1])


def middle_plain(attn_zero, attn_rest, tokens_t, cotangent, vectors, out_t, fc_t, proj_t, owners):
    width = tokens_t.shape[0]
    attn = joined(by_source(attn_zero), attn_rest)
    gain, bias = vectors[:, 2:3], vectors[:, 3:4]
    cot_t = cotangent.T
    residual = tokens_t.astype(WIDE) + dot(out_t, attn, 1, 0)
    normed, scale = normalize(residual, 0)
    low = (normed * gain + bias).astype(LOW)
    hidden = dot(fc_t, low, 1, 0)
    active, pull = jax.vjp(functools.partial(jax.nn.gelu, approximate=True), hidden)
    low_active = active.astype(LOW)
    output = (residual + dot(proj_t, low_active, 1, 0)).astype(LOW).T
    (grad_hidden,) = pull(dot(proj_t, cot_t, 0, 0))
    grad_hidden = grad_hidden.astype(LOW)
    grad_proj = dot(cot_t, low_active, 1, 1).astype(LOW)
    grad_fc = dot(grad_hidden, low, 1, 1).astype(LOW)
    grad = dot(fc_t, grad_hidden, 0, 0)
    grad_gain = jnp.sum(grad * normed, axis=1, keepdims=True)
    grad_bias = jnp.sum(grad, axis=1, keepdims=True)
    grad_res = cot_t.astype(WIDE) + norm_back(grad * gain, normed, scale)
    mixed = grad_res.astype(LOW)
    part = width // owners
    grad_proj = grad_proj.reshape(owners, part, -1, width).transpose(0, 2, 1, 3)
    pack = jnp.concatenate(
        [
            grad_fc.reshape(owners, -1, width),
            grad_proj.reshape(owners, -1, width),
            dot(mixed, attn, 1, 1).astype(LOW).reshape(owners, part, width),
        ],
        axis=1,
    )
    grad_attn = dot(out_t, mixed, 0, 0).astype(LOW)
    grad_attn = grad_attn.reshape(-1, len(attn_zero), HEAD, attn.shape[1]).swapaxes(0, 1)
    table = jnp.concatenate([jnp.zeros((width, 2), WIDE), grad_gain, grad_bias], axis=1)
    table = jnp.pad(table, ((0, 0), (0, 124)))
    return output, pack, grad_attn[:, :1], grad_attn[:, 1:], grad_res, table


def weights_kernel(counts, *refs):
    core_ref = refs[0]
    *homes, low_ref, query_ref, key_ref, value_ref, tokens_ref, vec_ref, _ = refs[1:-9]
    keep_ref, send_ref, grad_ref, first_ref, q_ref, k_ref, v_ref, pack_ref, sems = refs[-9:]
    owners = 2 * pack_ref.shape[1]

    def store(owner, first, block):
        pack_ref[owner % 2, owner // 2, first : first + block.shape[0]] = block

    fresh_width = value_ref.shape[0]
    homes = iter(homes)
    for slot, count in enumerate(counts):
        groups = count
        if count == 1:
            home = next(homes)
            groups = home.shape[0]
        for turn in range(groups):
            block = home.at[turn] if count == 1 else next(homes)
            group = turn if count == 1 else lax.rem(core_ref[1] + groups - turn, groups)
            rows = pl.ds(pl.multiple_of((slot * groups + group) * HEAD, HEAD), HEAD)
            for which, back in enumerate((q_ref, k_ref, v_ref)):
                back[rows] = block[which]
    first_ref[...] = turned(v_ref[fresh_width:])
    back_v = v_ref[:fresh_width]
    low = low_ref[...]
    first = 0
    for back in (q_ref[...], k_ref[...], back_v):
        grads = dot(back, low, 1, 0).astype(LOW)
        rows = grads.shape[0] // owners
        for owner in range(owners):
            store(owner, first, grads[owner * rows : (owner + 1) * rows])
        first += rows
    grad = (
        dot(query_ref[...], q_ref[...], 0, 0)
        + dot(key_ref[...], k_ref[...], 0, 0)
        + dot(value_ref[...], back_v, 0, 0)
    )
    grad_ref[...] = grad
    normed, _ = normalize(tokens_ref[...].astype(WIDE), 0)
    lane = lax.broadcasted_iota(jnp.int32, vec_ref.shape, 1)
    grad_gain = jnp.sum(grad * normed, axis=1, keepdims=True)
    grad_bias = jnp.sum(grad, axis=1, keepdims=True)
    table = jnp.where(lane == 0, grad_gain, jnp.where(lane == 1, grad_bias, vec_ref[...]))
    table = jnp.transpose(table)[:16].astype(LOW)
    for owner in range(owners):
        store(owner, first, table)
    copies = [
        pltpu.make_async_copy(pack_ref.at[core], ref, sems.at[at])
        for at, (core, ref) in enumerate(((core_ref[0], keep_ref), (1 - core_ref[0], send_ref)))
    ]
    for copy in copies:
        copy.start()
    for copy in copies:
        copy.wait()


def weights_back(homes, low_one, query_t, key_t, value_t, tokens_t, vec_back, behind, owners):
    width, rows = tokens_t.shape
    fresh_width = value_t.shape[0]
    pack_rows = (2 * width + fresh_width) // owners + 16
    counts = [len(home) for home in homes]
    held = [*sum(homes, []), low_one, query_t, key_t, value_t, tokens_t, vec_back]
    return pl.pallas_call(
        functools.partial(weights_kernel, counts),
        out_shape=[
            jax.ShapeDtypeStruct((owners // 2, pack_rows, width), LOW),
            jax.ShapeDtypeStruct((owners // 2, pack_rows, width), LOW),
            jax.ShapeDtypeStruct((width, rows), WIDE),
            jax.ShapeDtypeStruct((rows, width - fresh_width), LOW),
        ],
        out_specs=[untouched(), untouched()] + [pl.BlockSpec(memory_space=pltpu.VMEM)] * 2,
        scratch_shapes=[
            pltpu.VMEM((width, rows), LOW), pltpu.VMEM((width, rows), LOW),
            pltpu.VMEM((width, rows), LOW),
            pltpu.VMEM((2, owners // 2, pack_rows, width), LOW),
            pltpu.SemaphoreType.DMA((2,)),
        ],
        in_specs=[pl.BlockSpec(memory_space=pltpu.SMEM)]
        + [pl.BlockSpec(memory_space=pltpu.VMEM) for _ in held]
        + [untouched()],
        compiler_params=grant(56),
        cost_estimate=work(12, width),
        name="weights_back",
    )(jnp.stack([lax.axis_index("dp") & 1, lax.axis_index("seq")]), *held, behind)


def weights_plain(homes, low_one, query_t, key_t, value_t, tokens_t, vec_back, behind, owners):
    width, rows = tokens_t.shape
    homes = [home[0] if len(home) == 1 else by_source(home) for home in homes]
    back_q, back_k, back_v = (
        jnp.stack([home[:, which] for home in homes]).reshape(width, rows) for which in range(3)
    )
    grad_first = back_v[value_t.shape[0] :].T
    back_v = back_v[: value_t.shape[0]]
    grad = dot(query_t, back_q, 0, 0) + dot(key_t, back_k, 0, 0) + dot(value_t, back_v, 0, 0)
    normed, _ = normalize(tokens_t.astype(WIDE), 0)
    table = jnp.concatenate(
        [
            jnp.sum(grad * normed, axis=1, keepdims=True), jnp.sum(grad, axis=1, keepdims=True),
            vec_back[:, 2:16],
        ],
        axis=1,
    ).T
    pieces = [
        dot(back, low_one, 1, 0).reshape(owners, -1, width) for back in (back_q, back_k, back_v)
    ]
    count = sum(piece.shape[1] for piece in pieces)
    padded = -(-count // 16) * 16
    padded = -(-(padded + 16) // 32) * 32 - 16
    pieces.append(jnp.zeros((owners, padded - count, width), WIDE))
    pieces.append(jnp.broadcast_to(table, (owners,) + table.shape))
    pack = jnp.concatenate(pieces, axis=1).astype(LOW)
    pack = pack.reshape((-1, 2) + pack.shape[1:])
    mine = lax.axis_index("dp") & 1
    return pick(pack, mine, 1), pick(pack, 1 - mine, 1), grad, grad_first


def tokens_kernel(grad_ref, tokens_ref, res_ref, gain_ref, out_ref):
    normed, scale = normalize(tokens_ref[...].astype(WIDE), 0)
    grad = res_ref[...] + norm_back(grad_ref[...] * gain_ref[:, 0:1], normed, scale)
    out_ref[...] = jnp.transpose(grad).astype(LOW)


def tokens_back(grad_one, tokens_t, grad_residual, vectors):
    width, rows = grad_one.shape
    return pl.pallas_call(
        tokens_kernel,
        out_shape=jax.ShapeDtypeStruct((rows, width), LOW),
        compiler_params=grant(40),
        cost_estimate=work(4, width),
        name="tokens_back",
    )(grad_one, tokens_t, grad_residual, vectors)


def gate_kernel(*refs):
    pass


def gate(array, *behind):
    return pl.pallas_call(
        gate_kernel,
        in_specs=[untouched()] * (1 + len(behind)),
        out_specs=untouched(),
        out_shape=jax.ShapeDtypeStruct(array.shape, array.dtype),
        input_output_aliases={0: 0},
        name="gate",
    )(array, *behind)


def pick(stacked, index, axis=0):
    return lax.dynamic_index_in_dim(stacked, index, axis, keepdims=False)


def exchange(block, axis, bit):
    count = lax.axis_size(axis)
    return lax.ppermute(block, axis, [(i, i ^ (1 << bit)) for i in range(count)])


def swap(message):
    return lax.all_to_all(message, "seq", split_axis=0, concat_axis=0, tiled=True)


WHOLE = (0, 1)


def swap_turns(message):
    count, here = lax.axis_size("seq"), lax.axis_index("seq")
    got = [pick(message, here)]
    for turn in range(1, count):
        block = pick(message, (here + turn) % count)
        got.append(lax.ppermute(block, "seq", [(i, (i + turn) % count) for i in range(count)]))
    return got


def by_source(got):
    count, here = len(got), lax.axis_index("seq")
    whole = jnp.stack(got)
    return jnp.stack([pick(whole, (here - source) % count) for source in range(count)])


def gather_halves(shard, behind):
    bits = lax.axis_size("dp").bit_length() - 1
    half = shard.shape[0] // 2
    halves = []
    for block, order in (
        (shard[:half], range(1, bits)),
        (shard[half:], range(bits - 1, 0, -1)),
    ):
        held = block[None]
        for bit in order:
            held = jnp.concatenate([held, exchange(held, "dp", bit)])
        halves.append(held)
    halves[1] = gate(halves[1], behind)
    return [(held, exchange(held, "dp", 0)) for held in halves]


def gathered_order():
    count, here = lax.axis_size("dp"), lax.axis_index("dp")
    bits = count.bit_length() - 1
    offset = jnp.arange(count, dtype=jnp.int32) ^ here
    places = [0, 0]
    for at in range(bits - 1):
        bit = (offset >> (at + 1)) & 1
        places[0] = places[0] + (bit << at)
        places[1] = places[1] + (bit << (bits - 2 - at))
    return jnp.stack([offset & 1, *places])


def scatter_blocks(keep, send, others):
    count, here = lax.axis_size("dp"), lax.axis_index("dp")
    bits = count.bit_length() - 1
    rows, width = keep.shape[1:]

    def halve(held, bit, axis, other):
        mine = (here >> bit) & 1
        sent = pick(held, 1 - mine, axis).astype(LOW)
        sent = exchange(sent if other is None else gate(sent, other), "dp", bit)
        return pick(held, mine, axis).astype(WIDE) + sent.astype(WIDE)

    held = keep.astype(WIDE) + exchange(send, "dp", 0).astype(WIDE)
    held = held.reshape((2,) * (bits - 1) + (rows, width))
    halves = [held[..., : rows // 2, :], held[..., rows // 2 :, :]]
    orders = [list(range(1, bits)), list(range(bits - 1, 0, -1))]
    left = [list(range(bits - 1, 0, -1)) for _ in orders]
    for at in range(bits - 1):
        other = next(others, None)
        for which, order in enumerate(orders):
            axis = left[which].index(order[at])
            halves[which] = halve(halves[which], order[at], axis, other)
            left[which].remove(order[at])
    return jnp.concatenate(halves)


def first_step_kernel(place_ref, keep_ref, got_ref, a_send, a_keep, b_send, b_keep):
    x, y = place_ref[0], place_ref[1]
    half = keep_ref.shape[1] // 2

    def total(at, first):
        rows = pl.ds(first, half)
        return keep_ref[at, rows].astype(WIDE) + got_ref[at, rows].astype(WIDE)

    for other in range(2):
        a_send[other] = total(2 * other + 1 - x, 0).astype(LOW)
        a_keep[other] = total(2 * other + x, 0)
        b_send[other] = total(2 * (1 - y) + other, half).astype(LOW)
        b_keep[other] = total(2 * y + other, half)


def second_step_kernel(place_ref, a_keep, a_got, b_keep, b_got, a_send, a_next, b_send, b_next):
    x, y = place_ref[0], place_ref[1]
    a_send[...] = (a_keep[1 - y] + a_got[1 - y].astype(WIDE)).astype(LOW)
    a_next[...] = a_keep[y] + a_got[y].astype(WIDE)
    b_send[...] = (b_keep[1 - x] + b_got[1 - x].astype(WIDE)).astype(LOW)
    b_next[...] = b_keep[x] + b_got[x].astype(WIDE)


def third_step_kernel(place_ref, a_keep, a_got, b_keep, b_got, send, keep):
    a_sum = a_keep[...] + a_got[...].astype(WIDE)
    b_sum = b_keep[...] + b_got[...].astype(WIDE)
    first = place_ref[2] == 0
    send[...] = jnp.where(first, b_sum, a_sum).astype(LOW)
    keep[...] = jnp.where(first, a_sum, b_sum)


def last_step_kernel(place_ref, mine_ref, other_ref, query_ref, key_ref, value_ref, vec_ref):
    first = place_ref[2] == 0
    mine, other = mine_ref[...].astype(WIDE), other_ref[...].astype(WIDE)
    pack = jnp.concatenate(
        [jnp.where(first, mine, other), jnp.where(first, other, mine)], axis=0
    )
    at = 0
    for ref in (query_ref, key_ref, value_ref):
        ref[...] = pack[at : at + ref.shape[0]]
        at += ref.shape[0]
    vec_ref[...] = pack[at:]


def step_call(kernel, place, held, shapes):
    return pl.pallas_call(
        kernel,
        in_specs=[pl.BlockSpec(memory_space=pltpu.SMEM)]
        + [pl.BlockSpec(memory_space=pltpu.VMEM) for _ in held],
        out_specs=[pl.BlockSpec(memory_space=pltpu.VMEM) for _ in shapes],
        out_shape=[jax.ShapeDtypeStruct(dims, kind) for dims, kind in shapes],
        compiler_params=grant(32),
        cost_estimate=work(2, held[0].shape[-1]),
        name=kernel.__name__,
    )(place, *held)


def sum_four(keep, send, others, part, fresh_part):
    here = lax.axis_index("dp")
    place = jnp.stack([(here >> 1) & 1, here >> 2, lax.axis_index("seq") & 1])
    _, rows, width = keep.shape
    half = rows // 2
    pair, single = (2, half, width), (half, width)
    got = exchange(gate(send, others[0]), "dp", 0)
    a_send, a_keep, b_send, b_keep = step_call(
        first_step_kernel, place, [keep, got],
        [(pair, LOW), (pair, WIDE), (pair, LOW), (pair, WIDE)],
    )
    a_got = exchange(a_send, "dp", 1)
    b_got = exchange(b_send, "dp", 2)
    a_send, a_keep, b_send, b_keep = step_call(
        second_step_kernel, place, [a_keep, a_got, b_keep, b_got],
        [(single, LOW), (single, WIDE), (single, LOW), (single, WIDE)],
    )
    a_got = exchange(gate(a_send, others[1]), "dp", 2)
    b_got = exchange(gate(b_send, others[1]), "dp", 1)
    send, keep = step_call(
        third_step_kernel, place, [a_keep, a_got, b_keep, b_got], [(single, LOW), (single, WIDE)]
    )
    mine = (keep + exchange(gate(send, others[2]), "seq", 0).astype(WIDE)).astype(LOW)
    mine = seq_pairs(mine)
    query_t, key_t, value_t, vectors = step_call(
        last_step_kernel, place, [mine, exchange(mine, "seq", 0)],
        [
            ((part, width), WIDE), ((part, width), WIDE), ((fresh_part, width), WIDE),
            ((rows - 2 * part - fresh_part, width), WIDE),
        ],
    )
    return query_t.T, key_t.T, value_t.T, vectors, keep


def sum_any(keep, send, others, part, fresh_part):
    pack = seq_whole(seq_pairs(seq_halves(scatter_blocks(keep, send, iter(others)))))
    return (
        pack[:part].T, pack[part : 2 * part].T, pack[2 * part : 2 * part + fresh_part].T,
        pack[-16:], keep,
    )


def seq_halves(block):
    mine = lax.axis_index("seq") & 1
    halves = block.reshape((2, -1) + block.shape[1:])
    sent = exchange(pick(halves, 1 - mine).astype(LOW), "seq", 0)
    return (pick(halves, mine).astype(WIDE) + sent.astype(WIDE)).astype(LOW)


def seq_pairs(held):
    total = held.astype(WIDE)
    for bit in range(1, lax.axis_size("seq").bit_length() - 1):
        total = total + exchange(total.astype(LOW), "seq", bit).astype(WIDE)
    return total.astype(LOW)


def seq_whole(held, other=None):
    mine = lax.axis_index("seq") & 1
    other = exchange(held, "seq", 0) if other is None else other
    first, second = jnp.where(mine == 0, held, other), jnp.where(mine == 0, other, held)
    return jnp.concatenate([first, second]).astype(WIDE)


def gather(shard):
    return lax.all_gather(shard, "dp", axis=0, tiled=True)


def shards(
    tokens, first_values, cotangent, ln1_gain, ln1_bias, w_query, w_key, w_value, w_out,
    ln2_gain, ln2_bias, w_fc, w_proj,
):
    owners = lax.axis_size("dp")
    groups = lax.axis_size("seq")
    rows, width = tokens.shape
    local = HEADS // groups
    part, fresh_part = w_query.shape[1], w_value.shape[1]
    fresh_width = fresh_part * owners

    weight_rows = -(-(2 * part + fresh_part) // 16) * 16
    pack_rows = -(-(weight_rows + 16) // 32) * 32
    aligned = fresh_part % 16 == 0 and pack_rows == weight_rows + 16
    here = lax.axis_index("dp")

    last = local - 1
    first = (last * groups * HEAD - fresh_width) // HEAD
    early = first_values[:, first * HEAD :].T.reshape(groups, 1, HEAD, rows)
    early = swap(early)
    vectors = jnp.stack([ln1_gain, ln1_bias, ln2_gain, ln2_bias])
    vectors = lax.dynamic_update_slice(jnp.zeros((16, width), LOW), vectors, (0, here * part))
    first_pack = jnp.concatenate([w_query.T, w_key.T, w_value.T], axis=0)
    first_pack = jnp.pad(first_pack, ((0, pack_rows - 16 - first_pack.shape[0]), (0, 0)))
    halves = gather_halves(jnp.concatenate([first_pack, vectors], axis=0), early)
    out_t, fc_t, proj_t = (
        gather(shard.T) for shard in (w_out, w_fc, w_proj)
    )

    layout = [(0, 0, 3)] + [(1, 2 + 3 * (last - 2 - at), 3) for at in range(last - 1)] + [(1, 0, 2)]
    *messages, low_one, tokens_t, query_t, key_t, value_t, vectors = (
        project if aligned else project_plain
    )(
        tokens, first_values, halves, gathered_order(), early, layout, part, fresh_part, groups
    )

    arrived = {1: swap(messages[1])}
    arrived[0] = swap(gate(messages[0], arrived[1]))
    log_totals, held = {}, None
    sources = [
        (which, first, (early, 0) if slot == last else (None, first + 2))
        for slot, (which, first, _) in enumerate(layout)
    ]

    def inputs(slot):
        which, first, (values, at) = sources[slot]
        return arrived[which], first, arrived[which] if values is None else values, at

    for slot in range(last, 0, -1):
        held, log_totals[slot] = attend(*inputs(slot), held, slot - 1, last)
    rest = held
    zero, log_totals[0] = attend(*inputs(0), None, 0, 1)

    output, grad_pack, grad_zero, grad_rest, grad_residual, vec_back = (
        middle if aligned else middle_plain
    )(swap_turns(zero), swap(rest), tokens_t, cotangent, vectors, out_t, fc_t, proj_t, owners)
    grad_pack = lax.psum_scatter(
        grad_pack.reshape(-1, width), "dp", scatter_dimension=0, tiled=True
    )

    grad_zero = swap(grad_zero)
    grad_rest = swap(grad_rest)
    homes = []
    for slot in range(local):
        incoming, incoming_at = (grad_rest, slot - 1) if slot else (grad_zero, 0)
        attended, attended_at = (rest, slot - 1) if slot else (zero, 0)
        behind = grads if slot else log_totals[slot]
        grads = attend_backward(
            *inputs(slot), incoming, incoming_at, attended, attended_at, log_totals[slot],
            behind,
        )
        homes.append([swap(grads)] if slot in WHOLE else swap_turns(grads))
    grad_pack = seq_halves(gate(grad_pack, grads))
    keep, send, grad_one, grad_first = (weights_back if aligned else weights_plain)(
        homes, low_one, query_t, key_t, value_t, tokens_t, vec_back, grad_pack, owners
    )
    cut = grad_pack.shape[0] * 3 // 80 * 16
    pairs = [seq_pairs(grad_pack[:cut]), seq_pairs(grad_pack[cut:])]
    backs = [exchange(block, "seq", 0) for block in pairs]
    others = [*pairs, backs[0]]
    grad_query, grad_key, grad_value, vectors_back, behind = (
        sum_four if aligned and owners == 8 else sum_any
    )(keep, send, others, part, fresh_part)
    grad_pack = seq_whole(jnp.concatenate(pairs), jnp.concatenate(backs))
    grad_tokens = tokens_back(gate(grad_one, behind), tokens_t, grad_residual, vectors)
    vectors = lax.dynamic_slice(vectors_back, (0, here * part), (4, part))
    fc_part = w_fc.shape[1]
    grad_proj = grad_pack[fc_part : 2 * fc_part].reshape(-1, part, width).transpose(0, 2, 1)
    return (
        output,
        grad_tokens,
        grad_first,
        vectors[0],
        vectors[1],
        grad_query,
        grad_key,
        grad_value,
        grad_pack[2 * fc_part :].T,
        vectors[2],
        vectors[3],
        grad_pack[:fc_part].T,
        grad_proj.reshape(-1, part),
    )


def solution(mesh):
    row = P(("dp", "seq"), None)
    vector, matrix = P("dp"), P(None, "dp")
    weights = (vector, vector, matrix, matrix, matrix, matrix, vector, vector, matrix, matrix)
    return jax.shard_map(
        shards,
        mesh=mesh,
        in_specs=(row, row, row) + weights,
        out_specs=(row, row, row) + weights,
        check_vma=False,
    )
```

```python
import functools
import math

import jax
import jax.numpy as jnp
from jax import lax
from jax.experimental import pallas as pl
from jax.experimental.pallas import tpu as pltpu
from jax.sharding import PartitionSpec as P

HEADS = 12
HEAD = 64
EPSILON = 1e-05
LOW = jnp.bfloat16
WIDE = jnp.float32


def dot(left, right, left_dim, right_dim):
    return lax.dot_general(
        left, right, (((left_dim,), (right_dim,)), ((), ())), preferred_element_type=WIDE
    )


def causal(scores):
    key_pos = lax.broadcasted_iota(jnp.int32, scores.shape, 0)
    query_pos = lax.broadcasted_iota(jnp.int32, scores.shape, 1)
    return jnp.where(key_pos <= query_pos, scores, -1e30)


def turned(block):
    return jnp.transpose(block.astype(WIDE)).astype(LOW)


def sub_width(rows):
    for parts in (2, 3, 4, 6):
        if rows % (parts * 128) == 0:
            return rows // parts
    return rows


def normalize(values, axis):
    centred = values - jnp.mean(values, axis=axis, keepdims=True)
    scale = lax.rsqrt(jnp.mean(centred * centred, axis=axis, keepdims=True) + EPSILON)
    return centred * scale, scale


def norm_back(grad, normed, scale):
    return scale * (
        grad
        - jnp.mean(grad, axis=0, keepdims=True)
        - normed * jnp.mean(grad * normed, axis=0, keepdims=True)
    )


def whole(*dims):
    return pl.BlockSpec(dims, lambda *_: (0,) * len(dims), pipeline_mode=pl.Buffered(1))


def untouched():
    return pl.BlockSpec(memory_space=pl.ANY)


def head_block(rows, at):
    return pl.BlockSpec((1, 1, HEAD, rows), lambda i: (i, at, 0, 0))


def head_whole(parts, rows, at):
    return pl.BlockSpec((parts, 1, HEAD, rows), lambda i: (0, at, 0, 0))


def grant(mebibytes):
    return pltpu.CompilerParams(vmem_limit_bytes=mebibytes << 20)


def forward_kernel(q_ref, k_ref, v_ref, *refs):
    o_ref, log_ref, key_rows = refs[-3:]
    step = pl.program_id(0)
    parts, rows = k_ref.shape[0], k_ref.shape[3]
    sub = rows

    @pl.when(step == 0)
    def _():
        for part in range(parts):
            key_rows[part] = turned(k_ref[part, 0])

    for first in range(0, rows, sub):
        cols = pl.ds(first, sub)
        q = q_ref[0, 0, :, cols]
        blocks = []
        if first:
            blocks.append((0, dot(key_rows[step, pl.ds(0, first)], q, 1, 0)))
        blocks.append((first, causal(dot(key_rows[step, cols], q, 1, 0))))
        top = functools.reduce(
            jnp.maximum, [jnp.max(scores, axis=0, keepdims=True) for _, scores in blocks]
        )
        total = jnp.zeros((1, sub), WIDE)
        mixed = jnp.zeros((HEAD, sub), WIDE)
        for offset, scores in blocks:
            raised = jnp.exp(scores - top)
            total = total + jnp.sum(raised, axis=0, keepdims=True)
            mixed = mixed + dot(
                v_ref[step, 0, :, pl.ds(offset, scores.shape[0])], raised.astype(LOW), 1, 0
            )

        def earlier(part, carried):
            top, total, mixed = carried
            scores = dot(key_rows[part], q, 1, 0)
            new_top = jnp.maximum(top, jnp.max(scores, axis=0, keepdims=True))
            shrink = jnp.exp(top - new_top)
            raised = jnp.exp(scores - new_top)
            return (
                new_top,
                shrink * total + jnp.sum(raised, axis=0, keepdims=True),
                shrink * mixed + dot(v_ref[part, 0], raised.astype(LOW), 1, 0),
            )

        top, total, mixed = lax.fori_loop(0, step, earlier, (top, total, mixed))
        o_ref[0, 0, :, cols] = (mixed / total).astype(LOW)
        log_ref[0, :, cols] = top + jnp.log(total)


def work(units, width):
    return pl.CostEstimate(
        flops=units * 2 * width**3, bytes_accessed=units * 2 * width**2, transcendentals=0
    )


def pair_cost(parts, rows, matmuls):
    pairs = parts * parts * rows * rows // 2
    return pl.CostEstimate(
        flops=2 * matmuls * pairs * HEAD * 4,
        bytes_accessed=parts * rows * HEAD * 16,
        transcendentals=pairs,
    )


def attend(packed, query_at, values, value_at, held, held_at, held_slots):
    parts, _, _, rows = packed.shape
    shape = jax.ShapeDtypeStruct
    carried = [] if held is None else [held]
    return pl.pallas_call(
        forward_kernel,
        grid=(parts,),
        in_specs=[
            head_block(rows, query_at), head_whole(parts, rows, query_at + 1),
            head_whole(parts, rows, value_at),
        ]
        + [untouched() for _ in carried],
        out_specs=[
            head_block(rows, held_at), pl.BlockSpec((1, 1, rows), lambda i: (i, 0, 0)),
        ],
        out_shape=[
            shape((parts, held_slots, HEAD, rows), LOW), shape((parts, 1, rows), WIDE),
        ],
        scratch_shapes=[pltpu.VMEM((parts, rows, HEAD), LOW)],
        input_output_aliases={3: 0} if carried else {},
        compiler_params=grant(40),
        cost_estimate=pair_cost(parts, rows, 2),
        name="attend",
    )(packed, packed, values, *carried)


def backward_kernel(
    q_ref, k_ref, v_ref, do_ref, o_ref, log_ref, behind_ref, out_ref,
    key_rows, value_rows, query_rows, grad_rows, inner_ref, key_sum, value_sum,
):
    step = pl.program_id(0)
    parts, rows = k_ref.shape[0], k_ref.shape[3]
    sub = sub_width(rows)

    @pl.when(step == 0)
    def _():
        for part in range(parts):
            key_rows[part] = turned(k_ref[part, 0])
            value_rows[part] = turned(v_ref[part, 0])
        key_sum[...] = jnp.zeros_like(key_sum)
        value_sum[...] = jnp.zeros_like(value_sum)

    query_rows[...] = turned(q_ref[0, 0])
    grads = do_ref[0, 0].astype(WIDE)
    grad_rows[...] = jnp.transpose(grads).astype(LOW)
    inner_ref[...] = jnp.sum(grads * o_ref[0, 0].astype(WIDE), axis=0, keepdims=True)
    for first in range(0, rows, sub):
        cols = pl.ds(first, sub)
        q, do = q_ref[0, 0, :, cols], do_ref[0, 0, :, cols]
        log_total, inner = log_ref[0, :, cols], inner_ref[:, cols]
        q_rows, do_rows = query_rows[cols], grad_rows[cols]

        def pair(part, offset, size, masked):
            span = pl.ds(offset, size)
            scores = dot(key_rows[part, span], q, 1, 0)
            if masked:
                scores = causal(scores)
            probs = jnp.exp(scores - log_total)
            grad_probs = dot(value_rows[part, span], do, 1, 0)
            grad_scores = (probs * (grad_probs - inner)).astype(LOW)
            value_sum[part, span] += dot(probs.astype(LOW), do_rows, 1, 0)
            key_sum[part, span] += dot(grad_scores, q_rows, 1, 0)
            return dot(k_ref[part, 0, :, span], grad_scores, 1, 0)

        grad_q = pair(step, first, sub, True)
        if first:
            grad_q = grad_q + pair(step, 0, first, False)
        grad_q = lax.fori_loop(
            0, step, lambda part, carried: carried + pair(part, 0, rows, False), grad_q
        )
        out_ref[step, 0, :, cols] = (grad_q * HEAD ** (-0.5)).astype(LOW)

    @pl.when(step == parts - 1)
    def _():
        for part in range(parts):
            out_ref[part, 1] = jnp.transpose(key_sum[part]).astype(LOW)
            out_ref[part, 2] = jnp.transpose(value_sum[part]).astype(LOW)


def attend_backward(
    packed, query_at, values, value_at, grads, grads_at, attended, attended_at, log_totals, behind
):
    parts, _, _, rows = packed.shape
    return pl.pallas_call(
        backward_kernel,
        grid=(parts,),
        in_specs=[
            head_block(rows, query_at), head_whole(parts, rows, query_at + 1),
            head_whole(parts, rows, value_at), head_block(rows, grads_at), head_block(rows, attended_at),
            pl.BlockSpec((1, 1, rows), lambda i: (i, 0, 0)),
            untouched(),
        ],
        out_specs=pl.BlockSpec((parts, 3, HEAD, rows), lambda i: (0, 0, 0, 0)),
        out_shape=jax.ShapeDtypeStruct((parts, 3, HEAD, rows), LOW),
        scratch_shapes=[
            pltpu.VMEM((parts, rows, HEAD), LOW),
            pltpu.VMEM((parts, rows, HEAD), LOW),
            pltpu.VMEM((rows, HEAD), LOW),
            pltpu.VMEM((rows, HEAD), LOW),
            pltpu.VMEM((1, rows), WIDE),
            pltpu.VMEM((parts, rows, HEAD), WIDE),
            pltpu.VMEM((parts, rows, HEAD), WIDE),
        ],
        compiler_params=grant(40),
        cost_estimate=pair_cost(parts, rows, 5),
        name="attend_backward",
    )(packed, packed, values, grads, attended, log_totals, behind)


SLOPE = 0.7978845608028654


def project_kernel(
    layout, order_ref, tokens_ref, first_ref, near_a, far_a, near_b, far_b, behind_ref, *refs,
):
    *sent, low_ref, turned_ref, query_ref, key_ref, value_ref, vec_ref = refs
    owners = order_ref.shape[1]
    messages = [
        [sent[which].at[:, first + at] for at in range(count)] for which, first, count in layout
    ]
    part, fresh_part = query_ref.shape[0] // owners, value_ref.shape[0] // owners
    half = near_a.shape[1]
    groups = sent[0].shape[0]
    fresh_width = value_ref.shape[0]

    vectors = jnp.zeros((16, near_b.shape[2]), WIDE)
    for at in range(near_b.shape[0]):
        vectors = vectors + near_b[at, half - 16 :].astype(WIDE)
        vectors = vectors + far_b[at, half - 16 :].astype(WIDE)
    inputs = tokens_ref[...].astype(WIDE)
    normed, _ = normalize(inputs, 1)
    low_ref[...] = (normed * vectors[0:1] + vectors[1:2]).astype(LOW)
    turned_ref[...] = jnp.transpose(inputs).astype(LOW)
    blank = jnp.zeros((128 - vectors.shape[0], vectors.shape[1]), WIDE)
    vec_ref[...] = jnp.transpose(jnp.concatenate([vectors, blank], axis=0))
    for owner in range(owners):
        same_core = order_ref[0, owner] == 0
        weights = jnp.concatenate(
            [
                jnp.where(same_core, near_a[order_ref[1, owner]], far_a[order_ref[1, owner]]),
                jnp.where(same_core, near_b[order_ref[2, owner]], far_b[order_ref[2, owner]]),
            ],
            axis=0,
        )
        first = 0
        for ref, count in ((query_ref, part), (key_ref, part), (value_ref, fresh_part)):
            ref[owner * count : (owner + 1) * count] = weights[first : first + count]
            first += count
    low_one = low_ref[...]
    for which, ref in enumerate((query_ref, key_ref, value_ref)):
        products = dot(ref[...], low_one, 1, 1).astype(LOW)
        if which == 0:
            products = products * jnp.asarray(HEAD ** (-0.5), LOW)
        for slot, message in enumerate(messages):
            for group in range(groups):
                feature = (slot * groups + group) * HEAD
                if which < len(message) and feature < products.shape[0]:
                    message[which][group] = products[feature : feature + HEAD]
    for slot, message in enumerate(messages):
        for group in range(groups):
            first = (slot * groups + group) * HEAD - fresh_width
            if len(message) == 3 and first >= 0:
                start = first // 128 * 128
                block = turned(first_ref[:, start : start + 128])
                message[2][group] = block[first - start : first - start + HEAD]


def channels(layout):
    return [
        sum(count for which, _, count in layout if which == message)
        for message in range(1 + max(which for which, _, _ in layout))
    ]


def project(tokens, first_values, halves, order, behind, layout, part, fresh_part, groups):
    rows, width = tokens.shape
    owners = order.shape[1]
    held = [tokens, first_values, *halves[0], *halves[1]]
    shape = jax.ShapeDtypeStruct
    outs = [shape((groups, count, HEAD, rows), LOW) for count in channels(layout)] + [
        shape((rows, width), LOW), shape((width, rows), LOW), shape((width, width), LOW),
        shape((width, width), LOW), shape((fresh_part * owners, width), LOW),
        shape((width, 128), WIDE),
    ]
    return pl.pallas_call(
        functools.partial(project_kernel, layout),
        in_specs=[pl.BlockSpec(memory_space=pltpu.SMEM)]
        + [pl.BlockSpec(memory_space=pltpu.VMEM) for _ in held]
        + [untouched()],
        out_specs=[pl.BlockSpec(memory_space=pltpu.VMEM) for _ in outs],
        out_shape=outs,
        compiler_params=grant(48),
        cost_estimate=work(8, width),
        name="project",
    )(order, *held, behind)


def project_plain(tokens, first_values, halves, order, behind, layout, part, fresh_part, groups):
    rows, width = tokens.shape
    owners = order.shape[1]
    blocks = []
    for owner in range(owners):
        pieces = []
        for at, (near, far) in enumerate(halves):
            index = order[1 + at, owner]
            pieces.append(jnp.where(order[0, owner] == 0, pick(near, index), pick(far, index)))
        blocks.append(jnp.concatenate(pieces, axis=0))
    blocks = jnp.stack(blocks)
    query_t = blocks[:, :part].reshape(-1, width)
    key_t = blocks[:, part : 2 * part].reshape(-1, width)
    value_t = blocks[:, 2 * part : 2 * part + fresh_part].reshape(-1, width)
    vectors = jnp.sum(blocks[:, -16:].astype(WIDE), axis=0)
    normed, _ = normalize(tokens.astype(WIDE), 1)
    low_one = (normed * vectors[0:1] + vectors[1:2]).astype(LOW)
    queries = dot(query_t, low_one, 1, 1).astype(LOW) * jnp.asarray(HEAD ** (-0.5), LOW)
    keys = dot(key_t, low_one, 1, 1).astype(LOW)
    values = jnp.concatenate([dot(value_t, low_one, 1, 1).astype(LOW), first_values.T], axis=0)
    stacked = [array.reshape(-1, groups, HEAD, rows) for array in (queries, keys, values)]
    messages = [
        jnp.zeros((groups, count, HEAD, rows), LOW) for count in channels(layout)
    ]
    for slot, (which, first, count) in enumerate(layout):
        for at in range(count):
            messages[which] = messages[which].at[:, first + at].set(stacked[at][slot])
    table = jnp.pad(vectors.T, ((0, 0), (0, 128 - vectors.shape[0])))
    return (*messages, low_one, tokens.T, query_t, key_t, value_t, table)


def middle_kernel(place_ref, attn_rest, *refs):
    groups = attn_rest.shape[0]
    attn_zero, refs = refs[:groups], refs[groups:]
    (
        tokens_ref, cot_ref, vec_ref, out_ref, fc_ref, proj_ref,
        output_ref, pack_ref, grad_zero, grad_rest, grad_res_ref, vec_back,
        attn_ref, cot_t, low_ref, normed_ref, scale_ref, sum_ref, back_ref,
    ) = refs
    step = pl.program_id(0)
    owners = pack_ref.shape[0]
    block, width = fc_ref.shape
    part = width // owners
    fc_part = pl.num_programs(0) * block // owners
    share = block // fc_part

    def spots(rest, first):
        for slot in range(rest.shape[1]):
            for group in range(groups):
                yield (first + slot * groups + group) * HEAD, rest.at[group, slot]

    @pl.when(step == 0)
    def _():
        for first, ref in spots(attn_rest, groups):
            attn_ref[first : first + HEAD] = ref[...]
        for turn, ref in enumerate(attn_zero):
            group = lax.rem(place_ref[0] + groups - turn, groups)
            attn_ref[pl.ds(pl.multiple_of(group * HEAD, HEAD), HEAD)] = ref[0]
        cot_t[...] = turned(cot_ref[...])
        residual = tokens_ref[...].astype(WIDE) + dot(out_ref[...], attn_ref[...], 1, 0)
        normed, scale = normalize(residual, 0)
        low_ref[...] = (normed * vec_ref[:, 2:3] + vec_ref[:, 3:4]).astype(LOW)
        normed_ref[...] = normed
        scale_ref[...] = scale
        sum_ref[...] = residual
        back_ref[...] = jnp.zeros_like(back_ref)

    low = low_ref[...]
    hidden = dot(fc_ref[...], low, 1, 0)
    bent = jnp.tanh(SLOPE * (hidden + 0.044715 * hidden * hidden * hidden))
    half = 0.5 * (1.0 + bent)
    active = (hidden * half).astype(LOW)
    slope = half + hidden * (0.5 * (1.0 - bent * bent)) * (
        SLOPE * (1.0 + (3 * 0.044715) * hidden * hidden)
    )
    sum_ref[...] += dot(proj_ref[...], active, 1, 0)
    cot = cot_t[...]
    grad_hidden = (dot(proj_ref[...], cot, 0, 0) * slope).astype(LOW)
    grad_proj = dot(cot, active, 1, 1).astype(LOW)
    grad_fc = dot(grad_hidden, low, 1, 1).astype(LOW)
    for owner in range(owners):
        pack_ref[owner, pl.ds(pl.multiple_of(fc_part + step * part, 16), part)] = grad_proj[
            owner * part : (owner + 1) * part
        ]
    for at in range(share):
        pack_ref[step * share + at, pl.ds(0, fc_part)] = grad_fc[at * fc_part : (at + 1) * fc_part]
    back_ref[...] += dot(fc_ref[...], grad_hidden, 0, 0)

    @pl.when(step == pl.num_programs(0) - 1)
    def _():
        output_ref[...] = jnp.transpose(sum_ref[...]).astype(LOW)
        grad, normed = back_ref[...], normed_ref[...]
        lane = lax.broadcasted_iota(jnp.int32, vec_back.shape, 1)
        grad_gain = jnp.sum(grad * normed, axis=1, keepdims=True)
        grad_bias = jnp.sum(grad, axis=1, keepdims=True)
        vec_back[...] = jnp.where(lane == 2, grad_gain, jnp.where(lane == 3, grad_bias, 0.0))
        grad_res = cot_t[...].astype(WIDE) + norm_back(
            grad * vec_ref[:, 2:3], normed, scale_ref[...]
        )
        grad_res_ref[...] = grad_res
        mixed = grad_res.astype(LOW)
        grad_attn = dot(out_ref[...], mixed, 0, 0).astype(LOW)
        for spot, part_of in ((0, grad_zero), (groups, grad_rest)):
            for first, ref in spots(part_of, spot):
                ref[...] = grad_attn[first : first + HEAD]
        grad_out = dot(mixed, attn_ref[...], 1, 1).astype(LOW)
        for owner in range(owners):
            pack_ref[owner, pl.ds(2 * fc_part, part)] = grad_out[owner * part : (owner + 1) * part]


def middle(attn_zero, attn_rest, tokens_t, cotangent, vectors, out_t, fc_t, proj_t, owners):
    width, rows = tokens_t.shape
    hidden = fc_t.shape[0]
    block = width
    shape = jax.ShapeDtypeStruct
    down = pl.BlockSpec((block, width), lambda j: (j, 0))
    along = pl.BlockSpec((width, block), lambda j: (0, j))
    held = (width, rows)
    pack = (owners, (2 * hidden + width) // owners, width)
    zero = (len(attn_zero), *attn_zero[0].shape)
    return pl.pallas_call(
        middle_kernel,
        grid=(hidden // block,),
        in_specs=[
            pl.BlockSpec(memory_space=pltpu.SMEM), whole(*attn_rest.shape),
            *(whole(*block.shape) for block in attn_zero), whole(*held), whole(rows, width),
            whole(width, 128), whole(width, width), down, along,
        ],
        out_specs=[
            whole(rows, width), whole(*pack), whole(*zero), whole(*attn_rest.shape),
            whole(*held), whole(width, 128),
        ],
        out_shape=[
            shape((rows, width), LOW), shape(pack, LOW), shape(zero, LOW),
            shape(attn_rest.shape, LOW), shape(held, WIDE), shape((width, 128), WIDE),
        ],
        scratch_shapes=[
            pltpu.VMEM(held, LOW), pltpu.VMEM(held, LOW), pltpu.VMEM(held, LOW),
            pltpu.VMEM(held, WIDE), pltpu.VMEM((1, rows), WIDE), pltpu.VMEM(held, WIDE),
            pltpu.VMEM(held, WIDE),
        ],
        compiler_params=grant(60),
        cost_estimate=work(40, width),
        name="middle",
    )(
        lax.axis_index("seq").reshape(1), attn_rest, *attn_zero, tokens_t, cotangent, vectors,
        out_t, fc_t, proj_t,
    )


def joined(zero, rest):
    both = jnp.concatenate([zero, rest], axis=1).swapaxes(0, 1)
    return both.reshape(-1, both.shape[-1])


def middle_plain(attn_zero, attn_rest, tokens_t, cotangent, vectors, out_t, fc_t, proj_t, owners):
    width = tokens_t.shape[0]
    attn = joined(by_source(attn_zero), attn_rest)
    gain, bias = vectors[:, 2:3], vectors[:, 3:4]
    cot_t = cotangent.T
    residual = tokens_t.astype(WIDE) + dot(out_t, attn, 1, 0)
    normed, scale = normalize(residual, 0)
    low = (normed * gain + bias).astype(LOW)
    hidden = dot(fc_t, low, 1, 0)
    active, pull = jax.vjp(functools.partial(jax.nn.gelu, approximate=True), hidden)
    low_active = active.astype(LOW)
    output = (residual + dot(proj_t, low_active, 1, 0)).astype(LOW).T
    (grad_hidden,) = pull(dot(proj_t, cot_t, 0, 0))
    grad_hidden = grad_hidden.astype(LOW)
    grad_proj = dot(cot_t, low_active, 1, 1).astype(LOW)
    grad_fc = dot(grad_hidden, low, 1, 1).astype(LOW)
    grad = dot(fc_t, grad_hidden, 0, 0)
    grad_gain = jnp.sum(grad * normed, axis=1, keepdims=True)
    grad_bias = jnp.sum(grad, axis=1, keepdims=True)
    grad_res = cot_t.astype(WIDE) + norm_back(grad * gain, normed, scale)
    mixed = grad_res.astype(LOW)
    part = width // owners
    grad_proj = grad_proj.reshape(owners, part, -1, width).transpose(0, 2, 1, 3)
    pack = jnp.concatenate(
        [
            grad_fc.reshape(owners, -1, width),
            grad_proj.reshape(owners, -1, width),
            dot(mixed, attn, 1, 1).astype(LOW).reshape(owners, part, width),
        ],
        axis=1,
    )
    grad_attn = dot(out_t, mixed, 0, 0).astype(LOW)
    grad_attn = grad_attn.reshape(-1, len(attn_zero), HEAD, attn.shape[1]).swapaxes(0, 1)
    table = jnp.concatenate([jnp.zeros((width, 2), WIDE), grad_gain, grad_bias], axis=1)
    table = jnp.pad(table, ((0, 0), (0, 124)))
    return output, pack, grad_attn[:, :1], grad_attn[:, 1:], grad_res, table


def weights_kernel(counts, *refs):
    core_ref = refs[0]
    *homes, low_ref, query_ref, key_ref, value_ref, tokens_ref, vec_ref, _ = refs[1:-9]
    keep_ref, send_ref, grad_ref, first_ref, q_ref, k_ref, v_ref, pack_ref, sems = refs[-9:]
    owners = 2 * pack_ref.shape[1]

    def store(owner, first, block):
        pack_ref[owner % 2, owner // 2, first : first + block.shape[0]] = block

    fresh_width = value_ref.shape[0]
    homes = iter(homes)
    for slot, count in enumerate(counts):
        groups = count
        if count == 1:
            home = next(homes)
            groups = home.shape[0]
        for turn in range(groups):
            block = home.at[turn] if count == 1 else next(homes)
            group = turn if count == 1 else lax.rem(core_ref[1] + groups - turn, groups)
            rows = pl.ds(pl.multiple_of((slot * groups + group) * HEAD, HEAD), HEAD)
            for which, back in enumerate((q_ref, k_ref, v_ref)):
                back[rows] = block[which]
    first_ref[...] = turned(v_ref[fresh_width:])
    back_v = v_ref[:fresh_width]
    low = low_ref[...]
    first = 0
    for back in (q_ref[...], k_ref[...], back_v):
        grads = dot(back, low, 1, 0).astype(LOW)
        rows = grads.shape[0] // owners
        for owner in range(owners):
            store(owner, first, grads[owner * rows : (owner + 1) * rows])
        first += rows
    grad = (
        dot(query_ref[...], q_ref[...], 0, 0)
        + dot(key_ref[...], k_ref[...], 0, 0)
        + dot(value_ref[...], back_v, 0, 0)
    )
    grad_ref[...] = grad
    normed, _ = normalize(tokens_ref[...].astype(WIDE), 0)
    lane = lax.broadcasted_iota(jnp.int32, vec_ref.shape, 1)
    grad_gain = jnp.sum(grad * normed, axis=1, keepdims=True)
    grad_bias = jnp.sum(grad, axis=1, keepdims=True)
    table = jnp.where(lane == 0, grad_gain, jnp.where(lane == 1, grad_bias, vec_ref[...]))
    table = jnp.transpose(table)[:16].astype(LOW)
    for owner in range(owners):
        store(owner, first, table)
    copies = [
        pltpu.make_async_copy(pack_ref.at[core], ref, sems.at[at])
        for at, (core, ref) in enumerate(((core_ref[0], keep_ref), (1 - core_ref[0], send_ref)))
    ]
    for copy in copies:
        copy.start()
    for copy in copies:
        copy.wait()


def weights_back(homes, low_one, query_t, key_t, value_t, tokens_t, vec_back, behind, owners):
    width, rows = tokens_t.shape
    fresh_width = value_t.shape[0]
    pack_rows = (2 * width + fresh_width) // owners + 16
    counts = [len(home) for home in homes]
    held = [*sum(homes, []), low_one, query_t, key_t, value_t, tokens_t, vec_back]
    return pl.pallas_call(
        functools.partial(weights_kernel, counts),
        out_shape=[
            jax.ShapeDtypeStruct((owners // 2, pack_rows, width), LOW),
            jax.ShapeDtypeStruct((owners // 2, pack_rows, width), LOW),
            jax.ShapeDtypeStruct((width, rows), WIDE),
            jax.ShapeDtypeStruct((rows, width - fresh_width), LOW),
        ],
        out_specs=[untouched(), untouched()] + [pl.BlockSpec(memory_space=pltpu.VMEM)] * 2,
        scratch_shapes=[
            pltpu.VMEM((width, rows), LOW), pltpu.VMEM((width, rows), LOW),
            pltpu.VMEM((width, rows), LOW),
            pltpu.VMEM((2, owners // 2, pack_rows, width), LOW),
            pltpu.SemaphoreType.DMA((2,)),
        ],
        in_specs=[pl.BlockSpec(memory_space=pltpu.SMEM)]
        + [pl.BlockSpec(memory_space=pltpu.VMEM) for _ in held]
        + [untouched()],
        compiler_params=grant(56),
        cost_estimate=work(12, width),
        name="weights_back",
    )(jnp.stack([lax.axis_index("dp") & 1, lax.axis_index("seq")]), *held, behind)


def weights_plain(homes, low_one, query_t, key_t, value_t, tokens_t, vec_back, behind, owners):
    width, rows = tokens_t.shape
    homes = [home[0] if len(home) == 1 else by_source(home) for home in homes]
    back_q, back_k, back_v = (
        jnp.stack([home[:, which] for home in homes]).reshape(width, rows) for which in range(3)
    )
    grad_first = back_v[value_t.shape[0] :].T
    back_v = back_v[: value_t.shape[0]]
    grad = dot(query_t, back_q, 0, 0) + dot(key_t, back_k, 0, 0) + dot(value_t, back_v, 0, 0)
    normed, _ = normalize(tokens_t.astype(WIDE), 0)
    table = jnp.concatenate(
        [
            jnp.sum(grad * normed, axis=1, keepdims=True), jnp.sum(grad, axis=1, keepdims=True),
            vec_back[:, 2:16],
        ],
        axis=1,
    ).T
    pieces = [
        dot(back, low_one, 1, 0).reshape(owners, -1, width) for back in (back_q, back_k, back_v)
    ]
    count = sum(piece.shape[1] for piece in pieces)
    padded = -(-count // 16) * 16
    padded = -(-(padded + 16) // 32) * 32 - 16
    pieces.append(jnp.zeros((owners, padded - count, width), WIDE))
    pieces.append(jnp.broadcast_to(table, (owners,) + table.shape))
    pack = jnp.concatenate(pieces, axis=1).astype(LOW)
    pack = pack.reshape((-1, 2) + pack.shape[1:])
    mine = lax.axis_index("dp") & 1
    return pick(pack, mine, 1), pick(pack, 1 - mine, 1), grad, grad_first


def tokens_kernel(grad_ref, tokens_ref, res_ref, gain_ref, out_ref):
    normed, scale = normalize(tokens_ref[...].astype(WIDE), 0)
    grad = res_ref[...] + norm_back(grad_ref[...] * gain_ref[:, 0:1], normed, scale)
    out_ref[...] = jnp.transpose(grad).astype(LOW)


def tokens_back(grad_one, tokens_t, grad_residual, vectors):
    width, rows = grad_one.shape
    return pl.pallas_call(
        tokens_kernel,
        out_shape=jax.ShapeDtypeStruct((rows, width), LOW),
        compiler_params=grant(40),
        cost_estimate=work(4, width),
        name="tokens_back",
    )(grad_one, tokens_t, grad_residual, vectors)


def gate_kernel(*refs):
    pass


def gate(array, *behind):
    return pl.pallas_call(
        gate_kernel,
        in_specs=[untouched()] * (1 + len(behind)),
        out_specs=untouched(),
        out_shape=jax.ShapeDtypeStruct(array.shape, array.dtype),
        input_output_aliases={0: 0},
        name="gate",
    )(array, *behind)


def pick(stacked, index, axis=0):
    return lax.dynamic_index_in_dim(stacked, index, axis, keepdims=False)


def exchange(block, axis, bit):
    count = lax.axis_size(axis)
    return lax.ppermute(block, axis, [(i, i ^ (1 << bit)) for i in range(count)])


def swap(message):
    return lax.all_to_all(message, "seq", split_axis=0, concat_axis=0, tiled=True)


WHOLE = (0, 1)


def swap_turns(message):
    count, here = lax.axis_size("seq"), lax.axis_index("seq")
    got = [pick(message, here)]
    for turn in range(1, count):
        block = pick(message, (here + turn) % count)
        got.append(lax.ppermute(block, "seq", [(i, (i + turn) % count) for i in range(count)]))
    return got


def by_source(got):
    count, here = len(got), lax.axis_index("seq")
    whole = jnp.stack(got)
    return jnp.stack([pick(whole, (here - source) % count) for source in range(count)])


def gather_halves(shard, behind):
    bits = lax.axis_size("dp").bit_length() - 1
    half = shard.shape[0] // 2
    halves = []
    for block, order in (
        (shard[:half], range(1, bits)),
        (shard[half:], range(bits - 1, 0, -1)),
    ):
        held = block[None]
        for bit in order:
            held = jnp.concatenate([held, exchange(held, "dp", bit)])
        halves.append(held)
    halves[1] = gate(halves[1], behind)
    return [(held, exchange(held, "dp", 0)) for held in halves]


def gathered_order():
    count, here = lax.axis_size("dp"), lax.axis_index("dp")
    bits = count.bit_length() - 1
    offset = jnp.arange(count, dtype=jnp.int32) ^ here
    places = [0, 0]
    for at in range(bits - 1):
        bit = (offset >> (at + 1)) & 1
        places[0] = places[0] + (bit << at)
        places[1] = places[1] + (bit << (bits - 2 - at))
    return jnp.stack([offset & 1, *places])


def scatter_blocks(keep, send, others):
    count, here = lax.axis_size("dp"), lax.axis_index("dp")
    bits = count.bit_length() - 1
    rows, width = keep.shape[1:]

    def halve(held, bit, axis, other):
        mine = (here >> bit) & 1
        sent = pick(held, 1 - mine, axis).astype(LOW)
        sent = exchange(sent if other is None else gate(sent, other), "dp", bit)
        return pick(held, mine, axis).astype(WIDE) + sent.astype(WIDE)

    held = keep.astype(WIDE) + exchange(send, "dp", 0).astype(WIDE)
    held = held.reshape((2,) * (bits - 1) + (rows, width))
    halves = [held[..., : rows // 2, :], held[..., rows // 2 :, :]]
    orders = [list(range(1, bits)), list(range(bits - 1, 0, -1))]
    left = [list(range(bits - 1, 0, -1)) for _ in orders]
    for at in range(bits - 1):
        other = next(others, None)
        for which, order in enumerate(orders):
            axis = left[which].index(order[at])
            halves[which] = halve(halves[which], order[at], axis, other)
            left[which].remove(order[at])
    return jnp.concatenate(halves)


def first_step_kernel(place_ref, keep_ref, got_ref, a_send, a_keep, b_send, b_keep):
    x, y = place_ref[0], place_ref[1]
    half = keep_ref.shape[1] // 2

    def total(at, first):
        rows = pl.ds(first, half)
        return keep_ref[at, rows].astype(WIDE) + got_ref[at, rows].astype(WIDE)

    for other in range(2):
        a_send[other] = total(2 * other + 1 - x, 0).astype(LOW)
        a_keep[other] = total(2 * other + x, 0)
        b_send[other] = total(2 * (1 - y) + other, half).astype(LOW)
        b_keep[other] = total(2 * y + other, half)


def second_step_kernel(place_ref, a_keep, a_got, b_keep, b_got, a_send, a_next, b_send, b_next):
    x, y = place_ref[0], place_ref[1]
    a_send[...] = (a_keep[1 - y] + a_got[1 - y].astype(WIDE)).astype(LOW)
    a_next[...] = a_keep[y] + a_got[y].astype(WIDE)
    b_send[...] = (b_keep[1 - x] + b_got[1 - x].astype(WIDE)).astype(LOW)
    b_next[...] = b_keep[x] + b_got[x].astype(WIDE)


def third_step_kernel(place_ref, a_keep, a_got, b_keep, b_got, send, keep):
    a_sum = a_keep[...] + a_got[...].astype(WIDE)
    b_sum = b_keep[...] + b_got[...].astype(WIDE)
    first = place_ref[2] == 0
    send[...] = jnp.where(first, b_sum, a_sum).astype(LOW)
    keep[...] = jnp.where(first, a_sum, b_sum)


def last_step_kernel(place_ref, mine_ref, other_ref, query_ref, key_ref, value_ref, vec_ref):
    first = place_ref[2] == 0
    mine, other = mine_ref[...].astype(WIDE), other_ref[...].astype(WIDE)
    pack = jnp.concatenate(
        [jnp.where(first, mine, other), jnp.where(first, other, mine)], axis=0
    )
    at = 0
    for ref in (query_ref, key_ref, value_ref):
        ref[...] = pack[at : at + ref.shape[0]]
        at += ref.shape[0]
    vec_ref[...] = pack[at:]


def step_call(kernel, place, held, shapes):
    return pl.pallas_call(
        kernel,
        in_specs=[pl.BlockSpec(memory_space=pltpu.SMEM)]
        + [pl.BlockSpec(memory_space=pltpu.VMEM) for _ in held],
        out_specs=[pl.BlockSpec(memory_space=pltpu.VMEM) for _ in shapes],
        out_shape=[jax.ShapeDtypeStruct(dims, kind) for dims, kind in shapes],
        compiler_params=grant(32),
        cost_estimate=work(2, held[0].shape[-1]),
        name=kernel.__name__,
    )(place, *held)


def sum_four(keep, send, others, part, fresh_part):
    here = lax.axis_index("dp")
    place = jnp.stack([(here >> 1) & 1, here >> 2, lax.axis_index("seq") & 1])
    _, rows, width = keep.shape
    half = rows // 2
    pair, single = (2, half, width), (half, width)
    got = exchange(gate(send, others[0]), "dp", 0)
    a_send, a_keep, b_send, b_keep = step_call(
        first_step_kernel, place, [keep, got],
        [(pair, LOW), (pair, WIDE), (pair, LOW), (pair, WIDE)],
    )
    a_got = exchange(a_send, "dp", 1)
    b_got = exchange(b_send, "dp", 2)
    a_send, a_keep, b_send, b_keep = step_call(
        second_step_kernel, place, [a_keep, a_got, b_keep, b_got],
        [(single, LOW), (single, WIDE), (single, LOW), (single, WIDE)],
    )
    a_got = exchange(gate(a_send, others[1]), "dp", 2)
    b_got = exchange(gate(b_send, others[1]), "dp", 1)
    send, keep = step_call(
        third_step_kernel, place, [a_keep, a_got, b_keep, b_got], [(single, LOW), (single, WIDE)]
    )
    mine = (keep + exchange(gate(send, others[2]), "seq", 0).astype(WIDE)).astype(LOW)
    mine = seq_pairs(mine)
    query_t, key_t, value_t, vectors = step_call(
        last_step_kernel, place, [mine, exchange(mine, "seq", 0)],
        [
            ((part, width), WIDE), ((part, width), WIDE), ((fresh_part, width), WIDE),
            ((rows - 2 * part - fresh_part, width), WIDE),
        ],
    )
    return query_t.T, key_t.T, value_t.T, vectors, keep


def sum_any(keep, send, others, part, fresh_part):
    pack = seq_whole(seq_pairs(seq_halves(scatter_blocks(keep, send, iter(others)))))
    return (
        pack[:part].T, pack[part : 2 * part].T, pack[2 * part : 2 * part + fresh_part].T,
        pack[-16:], keep,
    )


def seq_halves(block):
    mine = lax.axis_index("seq") & 1
    halves = block.reshape((2, -1) + block.shape[1:])
    sent = exchange(pick(halves, 1 - mine).astype(LOW), "seq", 0)
    return (pick(halves, mine).astype(WIDE) + sent.astype(WIDE)).astype(LOW)


def seq_pairs(held):
    total = held.astype(WIDE)
    for bit in range(1, lax.axis_size("seq").bit_length() - 1):
        total = total + exchange(total.astype(LOW), "seq", bit).astype(WIDE)
    return total.astype(LOW)


def seq_whole(held, other=None):
    mine = lax.axis_index("seq") & 1
    other = exchange(held, "seq", 0) if other is None else other
    first, second = jnp.where(mine == 0, held, other), jnp.where(mine == 0, other, held)
    return jnp.concatenate([first, second]).astype(WIDE)


def gather(shard):
    return lax.all_gather(shard, "dp", axis=0, tiled=True)


def shards(
    tokens, first_values, cotangent, ln1_gain, ln1_bias, w_query, w_key, w_value, w_out,
    ln2_gain, ln2_bias, w_fc, w_proj,
):
    owners = lax.axis_size("dp")
    groups = lax.axis_size("seq")
    rows, width = tokens.shape
    local = HEADS // groups
    part, fresh_part = w_query.shape[1], w_value.shape[1]
    fresh_width = fresh_part * owners

    weight_rows = -(-(2 * part + fresh_part) // 16) * 16
    pack_rows = -(-(weight_rows + 16) // 32) * 32
    aligned = fresh_part % 16 == 0 and pack_rows == weight_rows + 16
    here = lax.axis_index("dp")

    last = local - 1
    first = (last * groups * HEAD - fresh_width) // HEAD
    early = first_values[:, first * HEAD :].T.reshape(groups, 1, HEAD, rows)
    early = swap(early)
    vectors = jnp.stack([ln1_gain, ln1_bias, ln2_gain, ln2_bias])
    vectors = lax.dynamic_update_slice(jnp.zeros((16, width), LOW), vectors, (0, here * part))
    first_pack = jnp.concatenate([w_query.T, w_key.T, w_value.T], axis=0)
    first_pack = jnp.pad(first_pack, ((0, pack_rows - 16 - first_pack.shape[0]), (0, 0)))
    halves = gather_halves(jnp.concatenate([first_pack, vectors], axis=0), early)
    out_t, fc_t, proj_t = (
        gather(shard.T) for shard in (w_out, w_fc, w_proj)
    )

    layout = [(0, 0, 3)] + [(1, 2 + 3 * (last - 2 - at), 3) for at in range(last - 1)] + [(1, 0, 2)]
    *messages, low_one, tokens_t, query_t, key_t, value_t, vectors = (
        project if aligned else project_plain
    )(
        tokens, first_values, halves, gathered_order(), early, layout, part, fresh_part, groups
    )

    arrived = {1: swap(messages[1])}
    arrived[0] = swap(gate(messages[0], arrived[1]))
    log_totals, held = {}, None
    sources = [
        (which, first, (early, 0) if slot == last else (None, first + 2))
        for slot, (which, first, _) in enumerate(layout)
    ]

    def inputs(slot):
        which, first, (values, at) = sources[slot]
        return arrived[which], first, arrived[which] if values is None else values, at

    for slot in range(last, 0, -1):
        held, log_totals[slot] = attend(*inputs(slot), held, slot - 1, last)
    rest = held
    zero, log_totals[0] = attend(*inputs(0), None, 0, 1)

    output, grad_pack, grad_zero, grad_rest, grad_residual, vec_back = (
        middle if aligned else middle_plain
    )(swap_turns(zero), swap(rest), tokens_t, cotangent, vectors, out_t, fc_t, proj_t, owners)
    grad_pack = lax.psum_scatter(
        grad_pack.reshape(-1, width), "dp", scatter_dimension=0, tiled=True
    )

    grad_zero = swap(grad_zero)
    grad_rest = swap(grad_rest)
    homes = []
    for slot in range(local):
        incoming, incoming_at = (grad_rest, slot - 1) if slot else (grad_zero, 0)
        attended, attended_at = (rest, slot - 1) if slot else (zero, 0)
        behind = grads if slot else log_totals[slot]
        grads = attend_backward(
            *inputs(slot), incoming, incoming_at, attended, attended_at, log_totals[slot],
            behind,
        )
        homes.append([swap(grads)] if slot in WHOLE else swap_turns(grads))
    grad_pack = seq_halves(gate(grad_pack, grads))
    keep, send, grad_one, grad_first = (weights_back if aligned else weights_plain)(
        homes, low_one, query_t, key_t, value_t, tokens_t, vec_back, grad_pack, owners
    )
    cut = grad_pack.shape[0] * 3 // 80 * 16
    pairs = [seq_pairs(grad_pack[:cut]), seq_pairs(grad_pack[cut:])]
    backs = [exchange(block, "seq", 0) for block in pairs]
    others = [*pairs, backs[0]]
    grad_query, grad_key, grad_value, vectors_back, behind = (
        sum_four if aligned and owners == 8 else sum_any
    )(keep, send, others, part, fresh_part)
    grad_pack = seq_whole(jnp.concatenate(pairs), jnp.concatenate(backs))
    grad_tokens = tokens_back(gate(grad_one, behind), tokens_t, grad_residual, vectors)
    vectors = lax.dynamic_slice(vectors_back, (0, here * part), (4, part))
    fc_part = w_fc.shape[1]
    grad_proj = grad_pack[fc_part : 2 * fc_part].reshape(-1, part, width).transpose(0, 2, 1)
    return (
        output,
        grad_tokens,
        grad_first,
        vectors[0],
        vectors[1],
        grad_query,
        grad_key,
        grad_value,
        grad_pack[2 * fc_part :].T,
        vectors[2],
        vectors[3],
        grad_pack[:fc_part].T,
        grad_proj.reshape(-1, part),
    )


def solution(mesh):
    row = P(("dp", "seq"), None)
    vector, matrix = P("dp"), P(None, "dp")
    weights = (vector, vector, matrix, matrix, matrix, matrix, vector, vector, matrix, matrix)
    return jax.shard_map(
        shards,
        mesh=mesh,
        in_specs=(row, row, row) + weights,
        out_specs=(row, row, row) + weights,
        check_vma=False,
    )
```

```python
import functools
import math

import jax
import jax.numpy as jnp
from jax import lax
from jax.experimental import pallas as pl
from jax.experimental.pallas import tpu as pltpu
from jax.sharding import PartitionSpec as P

HEADS = 12
HEAD = 64
EPSILON = 1e-05
LOW = jnp.bfloat16
WIDE = jnp.float32


def dot(left, right, left_dim, right_dim):
    return lax.dot_general(
        left, right, (((left_dim,), (right_dim,)), ((), ())), preferred_element_type=WIDE
    )


def causal(scores):
    key_pos = lax.broadcasted_iota(jnp.int32, scores.shape, 0)
    query_pos = lax.broadcasted_iota(jnp.int32, scores.shape, 1)
    return jnp.where(key_pos <= query_pos, scores, -1e30)


def turned(block):
    return jnp.transpose(block.astype(WIDE)).astype(LOW)


def sub_width(rows):
    for parts in (2, 3, 4, 6):
        if rows % (parts * 128) == 0:
            return rows // parts
    return rows


def normalize(values, axis):
    centred = values - jnp.mean(values, axis=axis, keepdims=True)
    scale = lax.rsqrt(jnp.mean(centred * centred, axis=axis, keepdims=True) + EPSILON)
    return centred * scale, scale


def norm_back(grad, normed, scale):
    return scale * (
        grad
        - jnp.mean(grad, axis=0, keepdims=True)
        - normed * jnp.mean(grad * normed, axis=0, keepdims=True)
    )


def whole(*dims):
    return pl.BlockSpec(dims, lambda *_: (0,) * len(dims), pipeline_mode=pl.Buffered(1))


def untouched():
    return pl.BlockSpec(memory_space=pl.ANY)


def head_block(rows, at):
    return pl.BlockSpec((1, 1, HEAD, rows), lambda i: (i, at, 0, 0))


def head_whole(parts, rows, at):
    return pl.BlockSpec((parts, 1, HEAD, rows), lambda i: (0, at, 0, 0))


def grant(mebibytes):
    return pltpu.CompilerParams(vmem_limit_bytes=mebibytes << 20)


def forward_kernel(q_ref, k_ref, v_ref, *refs):
    o_ref, log_ref, key_rows = refs[-3:]
    step = pl.program_id(0)
    parts, rows = k_ref.shape[0], k_ref.shape[3]
    sub = rows

    @pl.when(step == 0)
    def _():
        for part in range(parts):
            key_rows[part] = turned(k_ref[part, 0])

    for first in range(0, rows, sub):
        cols = pl.ds(first, sub)
        q = q_ref[0, 0, :, cols]
        blocks = []
        if first:
            blocks.append((0, dot(key_rows[step, pl.ds(0, first)], q, 1, 0)))
        blocks.append((first, causal(dot(key_rows[step, cols], q, 1, 0))))
        top = functools.reduce(
            jnp.maximum, [jnp.max(scores, axis=0, keepdims=True) for _, scores in blocks]
        )
        total = jnp.zeros((1, sub), WIDE)
        mixed = jnp.zeros((HEAD, sub), WIDE)
        for offset, scores in blocks:
            raised = jnp.exp(scores - top)
            total = total + jnp.sum(raised, axis=0, keepdims=True)
            mixed = mixed + dot(
                v_ref[step, 0, :, pl.ds(offset, scores.shape[0])], raised.astype(LOW), 1, 0
            )

        def earlier(part, carried):
            top, total, mixed = carried
            scores = dot(key_rows[part], q, 1, 0)
            new_top = jnp.maximum(top, jnp.max(scores, axis=0, keepdims=True))
            shrink = jnp.exp(top - new_top)
            raised = jnp.exp(scores - new_top)
            return (
                new_top,
                shrink * total + jnp.sum(raised, axis=0, keepdims=True),
                shrink * mixed + dot(v_ref[part, 0], raised.astype(LOW), 1, 0),
            )

        top, total, mixed = lax.fori_loop(0, step, earlier, (top, total, mixed))
        o_ref[0, 0, :, cols] = (mixed / total).astype(LOW)
        log_ref[0, :, cols] = top + jnp.log(total)


def work(units, width):
    return pl.CostEstimate(
        flops=units * 2 * width**3, bytes_accessed=units * 2 * width**2, transcendentals=0
    )


def pair_cost(parts, rows, matmuls):
    pairs = parts * parts * rows * rows // 2
    return pl.CostEstimate(
        flops=2 * matmuls * pairs * HEAD * 4,
        bytes_accessed=parts * rows * HEAD * 16,
        transcendentals=pairs,
    )


def attend(packed, query_at, values, value_at, held, held_at, held_slots):
    parts, _, _, rows = packed.shape
    shape = jax.ShapeDtypeStruct
    carried = [] if held is None else [held]
    return pl.pallas_call(
        forward_kernel,
        grid=(parts,),
        in_specs=[
            head_block(rows, query_at), head_whole(parts, rows, query_at + 1),
            head_whole(parts, rows, value_at),
        ]
        + [untouched() for _ in carried],
        out_specs=[
            head_block(rows, held_at), pl.BlockSpec((1, 1, rows), lambda i: (i, 0, 0)),
        ],
        out_shape=[
            shape((parts, held_slots, HEAD, rows), LOW), shape((parts, 1, rows), WIDE),
        ],
        scratch_shapes=[pltpu.VMEM((parts, rows, HEAD), LOW)],
        input_output_aliases={3: 0} if carried else {},
        compiler_params=grant(40),
        cost_estimate=pair_cost(parts, rows, 2),
        name="attend",
    )(packed, packed, values, *carried)


def backward_kernel(
    q_ref, k_ref, v_ref, do_ref, o_ref, log_ref, behind_ref, out_ref,
    key_rows, value_rows, query_rows, grad_rows, inner_ref, key_sum, value_sum,
):
    step = pl.program_id(0)
    parts, rows = k_ref.shape[0], k_ref.shape[3]
    sub = sub_width(rows)

    @pl.when(step == 0)
    def _():
        for part in range(parts):
            key_rows[part] = turned(k_ref[part, 0])
            value_rows[part] = turned(v_ref[part, 0])
        key_sum[...] = jnp.zeros_like(key_sum)
        value_sum[...] = jnp.zeros_like(value_sum)

    query_rows[...] = turned(q_ref[0, 0])
    grads = do_ref[0, 0].astype(WIDE)
    grad_rows[...] = jnp.transpose(grads).astype(LOW)
    inner_ref[...] = jnp.sum(grads * o_ref[0, 0].astype(WIDE), axis=0, keepdims=True)
    for first in range(0, rows, sub):
        cols = pl.ds(first, sub)
        q, do = q_ref[0, 0, :, cols], do_ref[0, 0, :, cols]
        log_total, inner = log_ref[0, :, cols], inner_ref[:, cols]
        q_rows, do_rows = query_rows[cols], grad_rows[cols]

        def pair(part, offset, size, masked):
            span = pl.ds(offset, size)
            scores = dot(key_rows[part, span], q, 1, 0)
            if masked:
                scores = causal(scores)
            probs = jnp.exp(scores - log_total)
            grad_probs = dot(value_rows[part, span], do, 1, 0)
            grad_scores = (probs * (grad_probs - inner)).astype(LOW)
            value_sum[part, span] += dot(probs.astype(LOW), do_rows, 1, 0)
            key_sum[part, span] += dot(grad_scores, q_rows, 1, 0)
            return dot(k_ref[part, 0, :, span], grad_scores, 1, 0)

        grad_q = pair(step, first, sub, True)
        if first:
            grad_q = grad_q + pair(step, 0, first, False)
        grad_q = lax.fori_loop(
            0, step, lambda part, carried: carried + pair(part, 0, rows, False), grad_q
        )
        out_ref[step, 0, :, cols] = (grad_q * HEAD ** (-0.5)).astype(LOW)

    @pl.when(step == parts - 1)
    def _():
        for part in range(parts):
            out_ref[part, 1] = jnp.transpose(key_sum[part]).astype(LOW)
            out_ref[part, 2] = jnp.transpose(value_sum[part]).astype(LOW)


def attend_backward(
    packed, query_at, values, value_at, grads, grads_at, attended, attended_at, log_totals, behind
):
    parts, _, _, rows = packed.shape
    return pl.pallas_call(
        backward_kernel,
        grid=(parts,),
        in_specs=[
            head_block(rows, query_at), head_whole(parts, rows, query_at + 1),
            head_whole(parts, rows, value_at), head_block(rows, grads_at), head_block(rows, attended_at),
            pl.BlockSpec((1, 1, rows), lambda i: (i, 0, 0)),
            untouched(),
        ],
        out_specs=pl.BlockSpec((parts, 3, HEAD, rows), lambda i: (0, 0, 0, 0)),
        out_shape=jax.ShapeDtypeStruct((parts, 3, HEAD, rows), LOW),
        scratch_shapes=[
            pltpu.VMEM((parts, rows, HEAD), LOW),
            pltpu.VMEM((parts, rows, HEAD), LOW),
            pltpu.VMEM((rows, HEAD), LOW),
            pltpu.VMEM((rows, HEAD), LOW),
            pltpu.VMEM((1, rows), WIDE),
            pltpu.VMEM((parts, rows, HEAD), WIDE),
            pltpu.VMEM((parts, rows, HEAD), WIDE),
        ],
        compiler_params=grant(40),
        cost_estimate=pair_cost(parts, rows, 5),
        name="attend_backward",
    )(packed, packed, values, grads, attended, log_totals, behind)


SLOPE = 0.7978845608028654


def project_kernel(
    layout, order_ref, tokens_ref, first_ref, near_a, far_a, near_b, far_b, behind_ref, *refs,
):
    *sent, low_ref, turned_ref, query_ref, key_ref, value_ref, vec_ref = refs
    owners = order_ref.shape[1]
    messages = [
        [sent[which].at[:, first + at] for at in range(count)] for which, first, count in layout
    ]
    part, fresh_part = query_ref.shape[0] // owners, value_ref.shape[0] // owners
    half = near_a.shape[1]
    groups = sent[0].shape[0]
    fresh_width = value_ref.shape[0]

    vectors = jnp.zeros((16, near_b.shape[2]), WIDE)
    for at in range(near_b.shape[0]):
        vectors = vectors + near_b[at, half - 16 :].astype(WIDE)
        vectors = vectors + far_b[at, half - 16 :].astype(WIDE)
    inputs = tokens_ref[...].astype(WIDE)
    normed, _ = normalize(inputs, 1)
    low_ref[...] = (normed * vectors[0:1] + vectors[1:2]).astype(LOW)
    turned_ref[...] = jnp.transpose(inputs).astype(LOW)
    blank = jnp.zeros((128 - vectors.shape[0], vectors.shape[1]), WIDE)
    vec_ref[...] = jnp.transpose(jnp.concatenate([vectors, blank], axis=0))
    for owner in range(owners):
        same_core = order_ref[0, owner] == 0
        weights = jnp.concatenate(
            [
                jnp.where(same_core, near_a[order_ref[1, owner]], far_a[order_ref[1, owner]]),
                jnp.where(same_core, near_b[order_ref[2, owner]], far_b[order_ref[2, owner]]),
            ],
            axis=0,
        )
        first = 0
        for ref, count in ((query_ref, part), (key_ref, part), (value_ref, fresh_part)):
            ref[owner * count : (owner + 1) * count] = weights[first : first + count]
            first += count
    low_one = low_ref[...]
    for which, ref in enumerate((query_ref, key_ref, value_ref)):
        products = dot(ref[...], low_one, 1, 1).astype(LOW)
        if which == 0:
            products = products * jnp.asarray(HEAD ** (-0.5), LOW)
        for slot, message in enumerate(messages):
            for group in range(groups):
                feature = (slot * groups + group) * HEAD
                if which < len(message) and feature < products.shape[0]:
                    message[which][group] = products[feature : feature + HEAD]
    for slot, message in enumerate(messages):
        for group in range(groups):
            first = (slot * groups + group) * HEAD - fresh_width
            if len(message) == 3 and first >= 0:
                start = first // 128 * 128
                block = turned(first_ref[:, start : start + 128])
                message[2][group] = block[first - start : first - start + HEAD]


def channels(layout):
    return [
        sum(count for which, _, count in layout if which == message)
        for message in range(1 + max(which for which, _, _ in layout))
    ]


def project(tokens, first_values, halves, order, behind, layout, part, fresh_part, groups):
    rows, width = tokens.shape
    owners = order.shape[1]
    held = [tokens, first_values, *halves[0], *halves[1]]
    shape = jax.ShapeDtypeStruct
    outs = [shape((groups, count, HEAD, rows), LOW) for count in channels(layout)] + [
        shape((rows, width), LOW), shape((width, rows), LOW), shape((width, width), LOW),
        shape((width, width), LOW), shape((fresh_part * owners, width), LOW),
        shape((width, 128), WIDE),
    ]
    return pl.pallas_call(
        functools.partial(project_kernel, layout),
        in_specs=[pl.BlockSpec(memory_space=pltpu.SMEM)]
        + [pl.BlockSpec(memory_space=pltpu.VMEM) for _ in held]
        + [untouched()],
        out_specs=[pl.BlockSpec(memory_space=pltpu.VMEM) for _ in outs],
        out_shape=outs,
        compiler_params=grant(48),
        cost_estimate=work(8, width),
        name="project",
    )(order, *held, behind)


def project_plain(tokens, first_values, halves, order, behind, layout, part, fresh_part, groups):
    rows, width = tokens.shape
    owners = order.shape[1]
    blocks = []
    for owner in range(owners):
        pieces = []
        for at, (near, far) in enumerate(halves):
            index = order[1 + at, owner]
            pieces.append(jnp.where(order[0, owner] == 0, pick(near, index), pick(far, index)))
        blocks.append(jnp.concatenate(pieces, axis=0))
    blocks = jnp.stack(blocks)
    query_t = blocks[:, :part].reshape(-1, width)
    key_t = blocks[:, part : 2 * part].reshape(-1, width)
    value_t = blocks[:, 2 * part : 2 * part + fresh_part].reshape(-1, width)
    vectors = jnp.sum(blocks[:, -16:].astype(WIDE), axis=0)
    normed, _ = normalize(tokens.astype(WIDE), 1)
    low_one = (normed * vectors[0:1] + vectors[1:2]).astype(LOW)
    queries = dot(query_t, low_one, 1, 1).astype(LOW) * jnp.asarray(HEAD ** (-0.5), LOW)
    keys = dot(key_t, low_one, 1, 1).astype(LOW)
    values = jnp.concatenate([dot(value_t, low_one, 1, 1).astype(LOW), first_values.T], axis=0)
    stacked = [array.reshape(-1, groups, HEAD, rows) for array in (queries, keys, values)]
    messages = [
        jnp.zeros((groups, count, HEAD, rows), LOW) for count in channels(layout)
    ]
    for slot, (which, first, count) in enumerate(layout):
        for at in range(count):
            messages[which] = messages[which].at[:, first + at].set(stacked[at][slot])
    table = jnp.pad(vectors.T, ((0, 0), (0, 128 - vectors.shape[0])))
    return (*messages, low_one, tokens.T, query_t, key_t, value_t, table)


def middle_kernel(place_ref, attn_rest, *refs):
    groups = attn_rest.shape[0]
    attn_zero, refs = refs[:groups], refs[groups:]
    (
        tokens_ref, cot_ref, vec_ref, out_ref, fc_ref, proj_ref,
        output_ref, pack_ref, grad_zero, grad_rest, grad_res_ref, vec_back,
        attn_ref, cot_t, low_ref, normed_ref, scale_ref, sum_ref, back_ref,
    ) = refs
    step = pl.program_id(0)
    owners = pack_ref.shape[0]
    block, width = fc_ref.shape
    part = width // owners
    fc_part = pl.num_programs(0) * block // owners
    share = block // fc_part

    def spots(rest, first):
        for slot in range(rest.shape[1]):
            for group in range(groups):
                yield (first + slot * groups + group) * HEAD, rest.at[group, slot]

    @pl.when(step == 0)
    def _():
        for first, ref in spots(attn_rest, groups):
            attn_ref[first : first + HEAD] = ref[...]
        for turn, ref in enumerate(attn_zero):
            group = lax.rem(place_ref[0] + groups - turn, groups)
            attn_ref[pl.ds(pl.multiple_of(group * HEAD, HEAD), HEAD)] = ref[0]
        cot_t[...] = turned(cot_ref[...])
        residual = tokens_ref[...].astype(WIDE) + dot(out_ref[...], attn_ref[...], 1, 0)
        normed, scale = normalize(residual, 0)
        low_ref[...] = (normed * vec_ref[:, 2:3] + vec_ref[:, 3:4]).astype(LOW)
        normed_ref[...] = normed
        scale_ref[...] = scale
        sum_ref[...] = residual
        back_ref[...] = jnp.zeros_like(back_ref)

    low = low_ref[...]
    hidden = dot(fc_ref[...], low, 1, 0)
    bent = jnp.tanh(SLOPE * (hidden + 0.044715 * hidden * hidden * hidden))
    half = 0.5 * (1.0 + bent)
    active = (hidden * half).astype(LOW)
    slope = half + hidden * (0.5 * (1.0 - bent * bent)) * (
        SLOPE * (1.0 + (3 * 0.044715) * hidden * hidden)
    )
    sum_ref[...] += dot(proj_ref[...], active, 1, 0)
    cot = cot_t[...]
    grad_hidden = (dot(proj_ref[...], cot, 0, 0) * slope).astype(LOW)
    grad_proj = dot(cot, active, 1, 1).astype(LOW)
    grad_fc = dot(grad_hidden, low, 1, 1).astype(LOW)
    for owner in range(owners):
        pack_ref[owner, pl.ds(pl.multiple_of(fc_part + step * part, 16), part)] = grad_proj[
            owner * part : (owner + 1) * part
        ]
    for at in range(share):
        pack_ref[step * share + at, pl.ds(0, fc_part)] = grad_fc[at * fc_part : (at + 1) * fc_part]
    back_ref[...] += dot(fc_ref[...], grad_hidden, 0, 0)

    @pl.when(step == pl.num_programs(0) - 1)
    def _():
        output_ref[...] = jnp.transpose(sum_ref[...]).astype(LOW)
        grad, normed = back_ref[...], normed_ref[...]
        lane = lax.broadcasted_iota(jnp.int32, vec_back.shape, 1)
        grad_gain = jnp.sum(grad * normed, axis=1, keepdims=True)
        grad_bias = jnp.sum(grad, axis=1, keepdims=True)
        vec_back[...] = jnp.where(lane == 2, grad_gain, jnp.where(lane == 3, grad_bias, 0.0))
        grad_res = cot_t[...].astype(WIDE) + norm_back(
            grad * vec_ref[:, 2:3], normed, scale_ref[...]
        )
        grad_res_ref[...] = grad_res
        mixed = grad_res.astype(LOW)
        grad_attn = dot(out_ref[...], mixed, 0, 0).astype(LOW)
        for spot, part_of in ((0, grad_zero), (groups, grad_rest)):
            for first, ref in spots(part_of, spot):
                ref[...] = grad_attn[first : first + HEAD]
        grad_out = dot(mixed, attn_ref[...], 1, 1).astype(LOW)
        for owner in range(owners):
            pack_ref[owner, pl.ds(2 * fc_part, part)] = grad_out[owner * part : (owner + 1) * part]


def middle(attn_zero, attn_rest, tokens_t, cotangent, vectors, out_t, fc_t, proj_t, owners):
    width, rows = tokens_t.shape
    hidden = fc_t.shape[0]
    block = width
    shape = jax.ShapeDtypeStruct
    down = pl.BlockSpec((block, width), lambda j: (j, 0))
    along = pl.BlockSpec((width, block), lambda j: (0, j))
    held = (width, rows)
    pack = (owners, (2 * hidden + width) // owners, width)
    zero = (len(attn_zero), *attn_zero[0].shape)
    return pl.pallas_call(
        middle_kernel,
        grid=(hidden // block,),
        in_specs=[
            pl.BlockSpec(memory_space=pltpu.SMEM), whole(*attn_rest.shape),
            *(whole(*block.shape) for block in attn_zero), whole(*held), whole(rows, width),
            whole(width, 128), whole(width, width), down, along,
        ],
        out_specs=[
            whole(rows, width), whole(*pack), whole(*zero), whole(*attn_rest.shape),
            whole(*held), whole(width, 128),
        ],
        out_shape=[
            shape((rows, width), LOW), shape(pack, LOW), shape(zero, LOW),
            shape(attn_rest.shape, LOW), shape(held, WIDE), shape((width, 128), WIDE),
        ],
        scratch_shapes=[
            pltpu.VMEM(held, LOW), pltpu.VMEM(held, LOW), pltpu.VMEM(held, LOW),
            pltpu.VMEM(held, WIDE), pltpu.VMEM((1, rows), WIDE), pltpu.VMEM(held, WIDE),
            pltpu.VMEM(held, WIDE),
        ],
        compiler_params=grant(60),
        cost_estimate=work(40, width),
        name="middle",
    )(
        lax.axis_index("seq").reshape(1), attn_rest, *attn_zero, tokens_t, cotangent, vectors,
        out_t, fc_t, proj_t,
    )


def joined(zero, rest):
    both = jnp.concatenate([zero, rest], axis=1).swapaxes(0, 1)
    return both.reshape(-1, both.shape[-1])


def middle_plain(attn_zero, attn_rest, tokens_t, cotangent, vectors, out_t, fc_t, proj_t, owners):
    width = tokens_t.shape[0]
    attn = joined(by_source(attn_zero), attn_rest)
    gain, bias = vectors[:, 2:3], vectors[:, 3:4]
    cot_t = cotangent.T
    residual = tokens_t.astype(WIDE) + dot(out_t, attn, 1, 0)
    normed, scale = normalize(residual, 0)
    low = (normed * gain + bias).astype(LOW)
    hidden = dot(fc_t, low, 1, 0)
    active, pull = jax.vjp(functools.partial(jax.nn.gelu, approximate=True), hidden)
    low_active = active.astype(LOW)
    output = (residual + dot(proj_t, low_active, 1, 0)).astype(LOW).T
    (grad_hidden,) = pull(dot(proj_t, cot_t, 0, 0))
    grad_hidden = grad_hidden.astype(LOW)
    grad_proj = dot(cot_t, low_active, 1, 1).astype(LOW)
    grad_fc = dot(grad_hidden, low, 1, 1).astype(LOW)
    grad = dot(fc_t, grad_hidden, 0, 0)
    grad_gain = jnp.sum(grad * normed, axis=1, keepdims=True)
    grad_bias = jnp.sum(grad, axis=1, keepdims=True)
    grad_res = cot_t.astype(WIDE) + norm_back(grad * gain, normed, scale)
    mixed = grad_res.astype(LOW)
    part = width // owners
    grad_proj = grad_proj.reshape(owners, part, -1, width).transpose(0, 2, 1, 3)
    pack = jnp.concatenate(
        [
            grad_fc.reshape(owners, -1, width),
            grad_proj.reshape(owners, -1, width),
            dot(mixed, attn, 1, 1).astype(LOW).reshape(owners, part, width),
        ],
        axis=1,
    )
    grad_attn = dot(out_t, mixed, 0, 0).astype(LOW)
    grad_attn = grad_attn.reshape(-1, len(attn_zero), HEAD, attn.shape[1]).swapaxes(0, 1)
    table = jnp.concatenate([jnp.zeros((width, 2), WIDE), grad_gain, grad_bias], axis=1)
    table = jnp.pad(table, ((0, 0), (0, 124)))
    return output, pack, grad_attn[:, :1], grad_attn[:, 1:], grad_res, table


def store_rows(pack_ref, at, feature, products):
    part = products[1]
    block, first = products[0], feature
    while first < feature + block.shape[0]:
        owner, row = first // part, first % part
        count = min(part - row, feature + block.shape[0] - first)
        pack_ref[owner % 2, owner // 2, at + row : at + row + count] = block[
            first - feature : first - feature + count
        ]
        first += count


def early_weights_kernel(
    *refs
):
    *homes, low_ref, query_ref, key_ref, value_ref, pack_ref, grad_ref, first_ref = refs[:-3]
    backs = refs[-3:]
    owners = 2 * pack_ref.shape[1]
    width = low_ref.shape[1]
    fresh_width = value_ref.shape[0]
    part, fresh_part = width // owners, fresh_width // owners
    for slot, home in enumerate(homes):
        groups = home.shape[0]
        for group in range(groups):
            first = (slot * groups + group) * HEAD
            for which, back in enumerate(backs):
                back[first : first + HEAD] = home[group, which]
    known = backs[0].shape[0]
    low = low_ref[...]
    fresh = backs[2][:fresh_width]
    store_rows(pack_ref, 0, 0, (dot(backs[0][...], low, 1, 0).astype(LOW), part))
    store_rows(pack_ref, part, 0, (dot(backs[1][...], low, 1, 0).astype(LOW), part))
    store_rows(pack_ref, 2 * part, 0, (dot(fresh, low, 1, 0).astype(LOW), fresh_part))
    grad_ref[...] = (
        dot(query_ref[:known], backs[0][...], 0, 0)
        + dot(key_ref[:known], backs[1][...], 0, 0)
        + dot(value_ref[...], fresh, 0, 0)
    )
    first_ref[...] = turned(backs[2][fresh_width:])


def early_weights(homes, low_one, query_t, key_t, value_t, owners, pack_rows):
    rows, width = low_one.shape
    known = len(homes) * homes[0].shape[0] * HEAD
    fresh_width = value_t.shape[0]
    held = [*homes, low_one, query_t, key_t, value_t]
    vmem = pl.BlockSpec(memory_space=pltpu.VMEM)
    shape = jax.ShapeDtypeStruct
    return pl.pallas_call(
        early_weights_kernel,
        in_specs=[vmem] * len(held),
        out_specs=[vmem] * 3,
        out_shape=[
            shape((2, owners // 2, pack_rows, width), LOW),
            shape((width, rows), WIDE),
            shape((rows, known - fresh_width), LOW),
        ],
        scratch_shapes=[pltpu.VMEM((known, rows), LOW) for _ in range(3)],
        compiler_params=grant(56),
        cost_estimate=work(10, width),
        name="early_weights",
    )(*held)


def weights_kernel(
    place_ref, *refs
):
    (
        *pieces, low_ref, query_ref, key_ref, tokens_ref, vec_ref, known_ref, known_grad, _,
        keep_ref, send_ref, grad_ref, first_ref, q_ref, k_ref, v_ref, pack_ref, sems,
    ) = refs
    groups = len(pieces)
    owners = 2 * pack_ref.shape[1]
    width = low_ref.shape[1]
    part = width // owners
    feature = width - groups * HEAD
    for turn, piece in enumerate(pieces):
        group = lax.rem(place_ref[1] + groups - turn, groups)
        rows = pl.ds(pl.multiple_of(group * HEAD, HEAD), HEAD)
        for which, back in enumerate((q_ref, k_ref, v_ref)):
            back[rows] = piece[which]
    low = low_ref[...]
    pack_ref[...] = known_ref[...]
    store_rows(pack_ref, 0, feature, (dot(q_ref[...], low, 1, 0).astype(LOW), part))
    store_rows(pack_ref, part, feature, (dot(k_ref[...], low, 1, 0).astype(LOW), part))
    grad = (
        known_grad[...]
        + dot(query_ref[feature:], q_ref[...], 0, 0)
        + dot(key_ref[feature:], k_ref[...], 0, 0)
    )
    grad_ref[...] = grad
    normed, _ = normalize(tokens_ref[...].astype(WIDE), 0)
    lane = lax.broadcasted_iota(jnp.int32, vec_ref.shape, 1)
    grad_gain = jnp.sum(grad * normed, axis=1, keepdims=True)
    grad_bias = jnp.sum(grad, axis=1, keepdims=True)
    table = jnp.where(lane == 0, grad_gain, jnp.where(lane == 1, grad_bias, vec_ref[...]))
    table = jnp.transpose(table)[:16].astype(LOW)
    last = pack_ref.shape[2] - 16
    for owner in range(owners):
        pack_ref[owner % 2, owner // 2, last:] = table
    copies = [
        pltpu.make_async_copy(pack_ref.at[core], ref, sems.at[at])
        for at, (core, ref) in enumerate(((place_ref[0], keep_ref), (1 - place_ref[0], send_ref)))
    ]
    for copy in copies:
        copy.start()
    first_ref[...] = turned(v_ref[...])
    for copy in copies:
        copy.wait()


def weights_back(homes, low_one, query_t, key_t, value_t, tokens_t, vec_back, behind, owners):
    width, rows = tokens_t.shape
    *known, pieces = homes
    pack_rows = (2 * width + value_t.shape[0]) // owners + 16
    known_pack, known_grad, known_first = early_weights(
        [home[0] for home in known], low_one, query_t, key_t, value_t, owners, pack_rows
    )
    own = len(pieces) * HEAD
    vmem = pl.BlockSpec(memory_space=pltpu.VMEM)
    shape = jax.ShapeDtypeStruct
    keep, send, grad, last_first = pl.pallas_call(
        weights_kernel,
        in_specs=[pl.BlockSpec(memory_space=pltpu.SMEM)]
        + [vmem] * (len(pieces) + 7)
        + [untouched()],
        out_specs=[untouched(), untouched(), vmem, vmem],
        out_shape=[
            shape((owners // 2, pack_rows, width), LOW),
            shape((owners // 2, pack_rows, width), LOW),
            shape((width, rows), WIDE),
            shape((rows, own), LOW),
        ],
        scratch_shapes=[pltpu.VMEM((own, rows), LOW) for _ in range(3)]
        + [
            pltpu.VMEM((2, owners // 2, pack_rows, width), LOW),
            pltpu.SemaphoreType.DMA((2,)),
        ],
        compiler_params=grant(56),
        cost_estimate=work(6, width),
        name="weights_back",
    )(
        jnp.stack([lax.axis_index("dp") & 1, lax.axis_index("seq")]), *pieces, low_one, query_t,
        key_t, tokens_t, vec_back, known_pack, known_grad, behind,
    )
    return keep, send, grad, jnp.concatenate([known_first, last_first], axis=1)


def weights_plain(homes, low_one, query_t, key_t, value_t, tokens_t, vec_back, behind, owners):
    width, rows = tokens_t.shape
    homes = [home[0] if len(home) == 1 else by_source(home) for home in homes]
    back_q, back_k, back_v = (
        jnp.stack([home[:, which] for home in homes]).reshape(width, rows) for which in range(3)
    )
    grad_first = back_v[value_t.shape[0] :].T
    back_v = back_v[: value_t.shape[0]]
    grad = dot(query_t, back_q, 0, 0) + dot(key_t, back_k, 0, 0) + dot(value_t, back_v, 0, 0)
    normed, _ = normalize(tokens_t.astype(WIDE), 0)
    table = jnp.concatenate(
        [
            jnp.sum(grad * normed, axis=1, keepdims=True), jnp.sum(grad, axis=1, keepdims=True),
            vec_back[:, 2:16],
        ],
        axis=1,
    ).T
    pieces = [
        dot(back, low_one, 1, 0).reshape(owners, -1, width) for back in (back_q, back_k, back_v)
    ]
    count = sum(piece.shape[1] for piece in pieces)
    padded = -(-count // 16) * 16
    padded = -(-(padded + 16) // 32) * 32 - 16
    pieces.append(jnp.zeros((owners, padded - count, width), WIDE))
    pieces.append(jnp.broadcast_to(table, (owners,) + table.shape))
    pack = jnp.concatenate(pieces, axis=1).astype(LOW)
    pack = pack.reshape((-1, 2) + pack.shape[1:])
    mine = lax.axis_index("dp") & 1
    return pick(pack, mine, 1), pick(pack, 1 - mine, 1), grad, grad_first


def tokens_kernel(grad_ref, tokens_ref, res_ref, gain_ref, out_ref):
    normed, scale = normalize(tokens_ref[...].astype(WIDE), 0)
    grad = res_ref[...] + norm_back(grad_ref[...] * gain_ref[:, 0:1], normed, scale)
    out_ref[...] = jnp.transpose(grad).astype(LOW)


def tokens_back(grad_one, tokens_t, grad_residual, vectors):
    width, rows = grad_one.shape
    return pl.pallas_call(
        tokens_kernel,
        out_shape=jax.ShapeDtypeStruct((rows, width), LOW),
        compiler_params=grant(40),
        cost_estimate=work(4, width),
        name="tokens_back",
    )(grad_one, tokens_t, grad_residual, vectors)


def gate_kernel(*refs):
    pass


def gate(array, *behind):
    return pl.pallas_call(
        gate_kernel,
        in_specs=[untouched()] * (1 + len(behind)),
        out_specs=untouched(),
        out_shape=jax.ShapeDtypeStruct(array.shape, array.dtype),
        input_output_aliases={0: 0},
        name="gate",
    )(array, *behind)


def pick(stacked, index, axis=0):
    return lax.dynamic_index_in_dim(stacked, index, axis, keepdims=False)


def exchange(block, axis, bit):
    count = lax.axis_size(axis)
    return lax.ppermute(block, axis, [(i, i ^ (1 << bit)) for i in range(count)])


def swap(message):
    return lax.all_to_all(message, "seq", split_axis=0, concat_axis=0, tiled=True)


WHOLE = (0, 1)


def swap_turns(message):
    count, here = lax.axis_size("seq"), lax.axis_index("seq")
    got = [pick(message, here)]
    for turn in range(1, count):
        block = pick(message, (here + turn) % count)
        got.append(lax.ppermute(block, "seq", [(i, (i + turn) % count) for i in range(count)]))
    return got


def by_source(got):
    count, here = len(got), lax.axis_index("seq")
    whole = jnp.stack(got)
    return jnp.stack([pick(whole, (here - source) % count) for source in range(count)])


def gather_halves(shard, behind):
    bits = lax.axis_size("dp").bit_length() - 1
    half = shard.shape[0] // 2
    halves = []
    for block, order in (
        (shard[:half], range(1, bits)),
        (shard[half:], range(bits - 1, 0, -1)),
    ):
        held = block[None]
        for bit in order:
            held = jnp.concatenate([held, exchange(held, "dp", bit)])
        halves.append(held)
    halves[1] = gate(halves[1], behind)
    return [(held, exchange(held, "dp", 0)) for held in halves]


def gathered_order():
    count, here = lax.axis_size("dp"), lax.axis_index("dp")
    bits = count.bit_length() - 1
    offset = jnp.arange(count, dtype=jnp.int32) ^ here
    places = [0, 0]
    for at in range(bits - 1):
        bit = (offset >> (at + 1)) & 1
        places[0] = places[0] + (bit << at)
        places[1] = places[1] + (bit << (bits - 2 - at))
    return jnp.stack([offset & 1, *places])


def scatter_blocks(keep, send, others):
    count, here = lax.axis_size("dp"), lax.axis_index("dp")
    bits = count.bit_length() - 1
    rows, width = keep.shape[1:]

    def halve(held, bit, axis, other):
        mine = (here >> bit) & 1
        sent = pick(held, 1 - mine, axis).astype(LOW)
        sent = exchange(sent if other is None else gate(sent, other), "dp", bit)
        return pick(held, mine, axis).astype(WIDE) + sent.astype(WIDE)

    held = keep.astype(WIDE) + exchange(send, "dp", 0).astype(WIDE)
    held = held.reshape((2,) * (bits - 1) + (rows, width))
    halves = [held[..., : rows // 2, :], held[..., rows // 2 :, :]]
    orders = [list(range(1, bits)), list(range(bits - 1, 0, -1))]
    left = [list(range(bits - 1, 0, -1)) for _ in orders]
    for at in range(bits - 1):
        other = next(others, None)
        for which, order in enumerate(orders):
            axis = left[which].index(order[at])
            halves[which] = halve(halves[which], order[at], axis, other)
            left[which].remove(order[at])
    return jnp.concatenate(halves)


def first_step_kernel(place_ref, keep_ref, got_ref, a_send, a_keep, b_send, b_keep):
    x, y = place_ref[0], place_ref[1]
    half = keep_ref.shape[1] // 2

    def total(at, first):
        rows = pl.ds(first, half)
        return keep_ref[at, rows].astype(WIDE) + got_ref[at, rows].astype(WIDE)

    for other in range(2):
        a_send[other] = total(2 * other + 1 - x, 0).astype(LOW)
        a_keep[other] = total(2 * other + x, 0)
        b_send[other] = total(2 * (1 - y) + other, half).astype(LOW)
        b_keep[other] = total(2 * y + other, half)


def second_step_kernel(place_ref, a_keep, a_got, b_keep, b_got, a_send, a_next, b_send, b_next):
    x, y = place_ref[0], place_ref[1]
    a_send[...] = (a_keep[1 - y] + a_got[1 - y].astype(WIDE)).astype(LOW)
    a_next[...] = a_keep[y] + a_got[y].astype(WIDE)
    b_send[...] = (b_keep[1 - x] + b_got[1 - x].astype(WIDE)).astype(LOW)
    b_next[...] = b_keep[x] + b_got[x].astype(WIDE)


def third_step_kernel(place_ref, a_keep, a_got, b_keep, b_got, send, keep):
    a_sum = a_keep[...] + a_got[...].astype(WIDE)
    b_sum = b_keep[...] + b_got[...].astype(WIDE)
    first = place_ref[2] == 0
    send[...] = jnp.where(first, b_sum, a_sum).astype(LOW)
    keep[...] = jnp.where(first, a_sum, b_sum)


def last_step_kernel(place_ref, mine_ref, other_ref, query_ref, key_ref, value_ref, vec_ref):
    first = place_ref[2] == 0
    mine, other = mine_ref[...].astype(WIDE), other_ref[...].astype(WIDE)
    pack = jnp.concatenate(
        [jnp.where(first, mine, other), jnp.where(first, other, mine)], axis=0
    )
    at = 0
    for ref in (query_ref, key_ref, value_ref):
        ref[...] = pack[at : at + ref.shape[0]]
        at += ref.shape[0]
    vec_ref[...] = pack[at:]


def step_call(kernel, place, held, shapes):
    return pl.pallas_call(
        kernel,
        in_specs=[pl.BlockSpec(memory_space=pltpu.SMEM)]
        + [pl.BlockSpec(memory_space=pltpu.VMEM) for _ in held],
        out_specs=[pl.BlockSpec(memory_space=pltpu.VMEM) for _ in shapes],
        out_shape=[jax.ShapeDtypeStruct(dims, kind) for dims, kind in shapes],
        compiler_params=grant(32),
        cost_estimate=work(2, held[0].shape[-1]),
        name=kernel.__name__,
    )(place, *held)


def sum_four(keep, send, others, part, fresh_part):
    here = lax.axis_index("dp")
    place = jnp.stack([(here >> 1) & 1, here >> 2, lax.axis_index("seq") & 1])
    _, rows, width = keep.shape
    half = rows // 2
    pair, single = (2, half, width), (half, width)
    got = exchange(gate(send, others[0]), "dp", 0)
    a_send, a_keep, b_send, b_keep = step_call(
        first_step_kernel, place, [keep, got],
        [(pair, LOW), (pair, WIDE), (pair, LOW), (pair, WIDE)],
    )
    a_got = exchange(a_send, "dp", 1)
    b_got = exchange(b_send, "dp", 2)
    a_send, a_keep, b_send, b_keep = step_call(
        second_step_kernel, place, [a_keep, a_got, b_keep, b_got],
        [(single, LOW), (single, WIDE), (single, LOW), (single, WIDE)],
    )
    a_got = exchange(gate(a_send, others[1]), "dp", 2)
    b_got = exchange(gate(b_send, others[1]), "dp", 1)
    send, keep = step_call(
        third_step_kernel, place, [a_keep, a_got, b_keep, b_got], [(single, LOW), (single, WIDE)]
    )
    mine = (keep + exchange(gate(send, others[2]), "seq", 0).astype(WIDE)).astype(LOW)
    mine = seq_pairs(mine)
    query_t, key_t, value_t, vectors = step_call(
        last_step_kernel, place, [mine, exchange(mine, "seq", 0)],
        [
            ((part, width), WIDE), ((part, width), WIDE), ((fresh_part, width), WIDE),
            ((rows - 2 * part - fresh_part, width), WIDE),
        ],
    )
    return query_t.T, key_t.T, value_t.T, vectors, keep


def sum_any(keep, send, others, part, fresh_part):
    pack = seq_whole(seq_pairs(seq_halves(scatter_blocks(keep, send, iter(others)))))
    return (
        pack[:part].T, pack[part : 2 * part].T, pack[2 * part : 2 * part + fresh_part].T,
        pack[-16:], keep,
    )


def seq_halves(block):
    mine = lax.axis_index("seq") & 1
    halves = block.reshape((2, -1) + block.shape[1:])
    sent = exchange(pick(halves, 1 - mine).astype(LOW), "seq", 0)
    return (pick(halves, mine).astype(WIDE) + sent.astype(WIDE)).astype(LOW)


def seq_pairs(held):
    total = held.astype(WIDE)
    for bit in range(1, lax.axis_size("seq").bit_length() - 1):
        total = total + exchange(total.astype(LOW), "seq", bit).astype(WIDE)
    return total.astype(LOW)


def seq_whole(held, other=None):
    mine = lax.axis_index("seq") & 1
    other = exchange(held, "seq", 0) if other is None else other
    first, second = jnp.where(mine == 0, held, other), jnp.where(mine == 0, other, held)
    return jnp.concatenate([first, second]).astype(WIDE)


def gather(shard):
    return lax.all_gather(shard, "dp", axis=0, tiled=True)


def shards(
    tokens, first_values, cotangent, ln1_gain, ln1_bias, w_query, w_key, w_value, w_out,
    ln2_gain, ln2_bias, w_fc, w_proj,
):
    owners = lax.axis_size("dp")
    groups = lax.axis_size("seq")
    rows, width = tokens.shape
    local = HEADS // groups
    part, fresh_part = w_query.shape[1], w_value.shape[1]
    fresh_width = fresh_part * owners

    weight_rows = -(-(2 * part + fresh_part) // 16) * 16
    pack_rows = -(-(weight_rows + 16) // 32) * 32
    aligned = fresh_part % 16 == 0 and pack_rows == weight_rows + 16
    here = lax.axis_index("dp")

    last = local - 1
    first = (last * groups * HEAD - fresh_width) // HEAD
    early = first_values[:, first * HEAD :].T.reshape(groups, 1, HEAD, rows)
    early = swap(early)
    vectors = jnp.stack([ln1_gain, ln1_bias, ln2_gain, ln2_bias])
    vectors = lax.dynamic_update_slice(jnp.zeros((16, width), LOW), vectors, (0, here * part))
    first_pack = jnp.concatenate([w_query.T, w_key.T, w_value.T], axis=0)
    first_pack = jnp.pad(first_pack, ((0, pack_rows - 16 - first_pack.shape[0]), (0, 0)))
    halves = gather_halves(jnp.concatenate([first_pack, vectors], axis=0), early)
    out_t, fc_t, proj_t = (
        gather(shard.T) for shard in (w_out, w_fc, w_proj)
    )

    layout = [(0, 0, 3)] + [(1, 2 + 3 * (last - 2 - at), 3) for at in range(last - 1)] + [(1, 0, 2)]
    *messages, low_one, tokens_t, query_t, key_t, value_t, vectors = (
        project if aligned else project_plain
    )(
        tokens, first_values, halves, gathered_order(), early, layout, part, fresh_part, groups
    )

    arrived = {1: swap(messages[1])}
    arrived[0] = swap(gate(messages[0], arrived[1]))
    log_totals, held = {}, None
    sources = [
        (which, first, (early, 0) if slot == last else (None, first + 2))
        for slot, (which, first, _) in enumerate(layout)
    ]

    def inputs(slot):
        which, first, (values, at) = sources[slot]
        return arrived[which], first, arrived[which] if values is None else values, at

    for slot in range(last, 0, -1):
        held, log_totals[slot] = attend(*inputs(slot), held, slot - 1, last)
    rest = held
    zero, log_totals[0] = attend(*inputs(0), None, 0, 1)

    output, grad_pack, grad_zero, grad_rest, grad_residual, vec_back = (
        middle if aligned else middle_plain
    )(swap_turns(zero), swap(rest), tokens_t, cotangent, vectors, out_t, fc_t, proj_t, owners)
    grad_pack = lax.psum_scatter(
        grad_pack.reshape(-1, width), "dp", scatter_dimension=0, tiled=True
    )

    grad_zero = swap(grad_zero)
    grad_rest = swap(grad_rest)
    homes = []
    for slot in range(local):
        incoming, incoming_at = (grad_rest, slot - 1) if slot else (grad_zero, 0)
        attended, attended_at = (rest, slot - 1) if slot else (zero, 0)
        behind = grads if slot else log_totals[slot]
        grads = attend_backward(
            *inputs(slot), incoming, incoming_at, attended, attended_at, log_totals[slot],
            behind,
        )
        homes.append([swap(grads)] if slot in WHOLE else swap_turns(grads))
    grad_pack = seq_halves(gate(grad_pack, grads))
    unit = grad_pack.shape[0] // 3 // 16 * 16
    cuts = [0, unit, unit + unit * 4 // 3 // 16 * 16, grad_pack.shape[0]]
    pairs = [seq_pairs(grad_pack[first:last]) for first, last in zip(cuts, cuts[1:])]
    backs = [exchange(block, "seq", 0) for block in pairs]
    others = [pairs[1], pairs[2], backs[0]]
    keep, send, grad_one, grad_first = (weights_back if aligned else weights_plain)(
        homes, low_one, query_t, key_t, value_t, tokens_t, vec_back, pairs[0], owners
    )
    grad_query, grad_key, grad_value, vectors_back, behind = (
        sum_four if aligned and owners == 8 else sum_any
    )(keep, send, others, part, fresh_part)
    grad_pack = seq_whole(jnp.concatenate(pairs), jnp.concatenate(backs))
    grad_tokens = tokens_back(gate(grad_one, behind), tokens_t, grad_residual, vectors)
    vectors = lax.dynamic_slice(vectors_back, (0, here * part), (4, part))
    fc_part = w_fc.shape[1]
    grad_proj = grad_pack[fc_part : 2 * fc_part].reshape(-1, part, width).transpose(0, 2, 1)
    return (
        output,
        grad_tokens,
        grad_first,
        vectors[0],
        vectors[1],
        grad_query,
        grad_key,
        grad_value,
        grad_pack[2 * fc_part :].T,
        vectors[2],
        vectors[3],
        grad_pack[:fc_part].T,
        grad_proj.reshape(-1, part),
    )


def solution(mesh):
    row = P(("dp", "seq"), None)
    vector, matrix = P("dp"), P(None, "dp")
    weights = (vector, vector, matrix, matrix, matrix, matrix, vector, vector, matrix, matrix)
    return jax.shard_map(
        shards,
        mesh=mesh,
        in_specs=(row, row, row) + weights,
        out_specs=(row, row, row) + weights,
        check_vma=False,
    )
```
